512 devices in a mesh: pre: 64 (over z, x, core), head: 8 (over y).
Axes of the slice: x: 4, y: 8, z: 8, core: 2. Of those that a mesh axis runs over, the one named last changes fastest.
Arguments:
- queries: bfloat16 [2048, 64, 3, 128], P('pre', 'head'), may hold values from -8 to 8
- prefix_keys: bfloat16 [64, 512, 8, 128], P('pre', None, 'head'), may hold values from -8 to 8
- prefix_values: bfloat16 [64, 512, 8, 128], P('pre', None, 'head'), may hold values from -4 to 4
- suffix_keys: bfloat16 [2048, 96, 8, 128], P('pre', None, 'head'), may hold values from -8 to 8
- suffix_values: bfloat16 [2048, 96, 8, 128], P('pre', None, 'head'), may hold values from -4 to 4
- new_keys: bfloat16 [2048, 3, 8, 128], P('pre', None, 'head'), may hold values from -8 to 8
- new_values: bfloat16 [2048, 3, 8, 128], P('pre', None, 'head'), may hold values from -4 to 4
- suffix_lengths: int32 [2048], P('pre'), may hold values from 48 to 96, as said below
- prefix_of_row: int32 [2048], P('pre'), may hold values from 0 to 63, as said below
- owner_of_prefix: int32 [64], replicated, may hold values from 0 to 63, each once
Outputs:
- attended: bfloat16 [2048, 64, 3, 128], P(('pre', 'head'))
The draws below stay inside these ranges and needn't reach their ends.
Inputs may be any that keep to these rules, and one draw needn't show every extreme that they name: `suffix_lengths`: every device's rows include at least one of length 96. `prefix_of_row`: the rows of one device name exactly 16 different prefixes, each by exactly 2 rows; one prefix is named on every device.
All inputs are finite; a program needn't handle non-finite values.
Results may differ from the reference program's by a relative error of at most 0.0027.
Values may be sent and summed in bfloat16 or wider, within the bound.
A program may use at most 64 MiB of HBM per device.

```python
import jax
import jax.numpy as jnp
from jax import lax

HEADS = 64
KVH = 8
HD = 128
STEPS = 3
SUF = 96
ROWS_DEV = 32
PRE_LEN = 512
SAMPLES = 2
ROWS = 2048
PREFIXES = 64


def shared_parts(key):
    key_row, key_step = jax.random.split(key, 2)
    row_direction = jnp.clip(jax.random.normal(key_row, (ROWS, KVH, HD), jnp.float32), -3.5, 3.5)
    step_direction = jnp.clip(jax.random.normal(key_step, (ROWS, KVH, STEPS, HD), jnp.float32), -3.5, 3.5)
    return (row_direction, step_direction)


def base_noise(key, shape):
    return jnp.clip(jax.random.normal(key, shape, jnp.float32), -3.5, 3.5)


def draw_queries(key, part):
    row_direction, step_direction = shared_parts(key)
    key = jax.random.fold_in(key, 11)
    group_size = HEADS // KVH
    noise = base_noise(key, (ROWS, HEADS, STEPS, HD))
    row_heads = jnp.repeat(row_direction, group_size, axis=1)[:, :, None, :]
    step_heads = jnp.repeat(step_direction, group_size, axis=1)
    values = noise + 0.3 * row_heads + 0.75 * step_heads
    return values.astype(jnp.bfloat16)


def draw_prefix_keys(key, part):
    key = jax.random.fold_in(key, 14)
    key_noise = jax.random.fold_in(key, 0)
    shape = (PREFIXES, PRE_LEN, KVH, HD)
    values = jnp.clip(jax.random.normal(key_noise, shape, jnp.float32), -4.0, 4.0)
    return values.astype(jnp.bfloat16)


def draw_suffix_keys(key, part):
    row_direction, step_direction = shared_parts(key)
    key = jax.random.fold_in(key, 12)
    noise = base_noise(key, (ROWS, SUF, KVH, HD))
    values = noise + 0.3 * row_direction[:, None, :, :]
    return values.astype(jnp.bfloat16)


def draw_new_keys(key, part):
    row_direction, step_direction = shared_parts(key)
    key = jax.random.fold_in(key, 13)
    noise = base_noise(key, (ROWS, STEPS, KVH, HD))
    values = 0.66 * noise + 0.75 * jnp.transpose(step_direction, (0, 2, 1, 3))
    return values.astype(jnp.bfloat16)


def draw_suffix_lengths(key, part):
    key = jax.random.fold_in(key, 31)
    key_len, key_full = jax.random.split(key)
    block_count = ROWS // ROWS_DEV
    lengths = jax.random.randint(key_len, (block_count, ROWS_DEV), SUF // 2, SUF + 1)
    full_slot = jax.random.randint(key_full, (block_count,), 0, ROWS_DEV)
    lengths = jnp.where(jnp.arange(ROWS_DEV, dtype=jnp.int32)[None, :] == full_slot[:, None], SUF, lengths)
    return lengths.reshape(ROWS).astype(jnp.int32)


def draw_prefix_of_row(key, part):
    key = jax.random.fold_in(key, 21)
    key_rank, key_hot, key_raw, key_mix = jax.random.split(key, 4)
    block_count = ROWS // ROWS_DEV
    group_count = ROWS_DEV // SAMPLES
    popularity = jax.random.permutation(key_rank, PREFIXES).astype(jnp.int32)
    hot_prefix = jax.random.randint(key_hot, (), 0, PREFIXES)
    raw_score = jax.random.randint(key_raw, (block_count, PREFIXES), 0, 65536)
    prefix_index = jnp.arange(PREFIXES, dtype=jnp.int32)
    pick_score = raw_score * (PREFIXES - popularity)[None, :] * PREFIXES + prefix_index[None, :]
    pick_score = jnp.where(prefix_index[None, :] == hot_prefix, 2 ** 30, pick_score)
    unused, picked = lax.top_k(pick_score, group_count)
    prompt_ids = jnp.repeat(picked, SAMPLES, axis=1)
    mix_score = jax.random.randint(key_mix, (block_count, ROWS_DEV), 0, 2 ** 20) * ROWS_DEV + jnp.arange(ROWS_DEV, dtype=jnp.int32)[None, :]
    shuffle_order = jnp.argsort(mix_score, axis=1, stable=True)
    prompt_ids = jnp.take_along_axis(prompt_ids, shuffle_order, axis=1)
    return prompt_ids.reshape(ROWS).astype(jnp.int32)


def shard_levels(key, extent, cuts, low, top_value):
    loudness = 1.0
    for dim, blocks in cuts:
        draws = jax.random.uniform(jax.random.fold_in(jax.random.fold_in(key, 6), dim), (blocks,), jnp.float32, low / len(cuts), top_value / len(cuts))
        loudness = loudness * jnp.repeat(jnp.exp(draws), extent[dim] // blocks).reshape((-1,) + (1,) * (len(extent) - 1 - dim))
    return loudness


def centred(stream_key, dims, spread, limit, cuts=(), kind=jnp.bfloat16):
    result = jax.random.normal(stream_key, dims, jnp.float32) * spread
    if len(cuts) > 0:
        result = shard_levels(stream_key, dims, cuts, -0.22, 0.18) * result
    return jnp.clip(result, min=-limit, max=limit).astype(kind)


def setup_inputs(seed: int = 0) -> dict:
    arg_keys = jax.random.split(jax.random.key(seed), 11)
    return {
        "queries": draw_queries(jax.random.fold_in(arg_keys[10], 71), 0),
        "prefix_keys": draw_prefix_keys(jax.random.fold_in(arg_keys[10], 71), 0),
        "prefix_values": centred(arg_keys[2], (PREFIXES, PRE_LEN, KVH, HD), 1.0, 4.0, ((0, 64), (2, 8))),
        "suffix_keys": draw_suffix_keys(jax.random.fold_in(arg_keys[10], 71), 0),
        "suffix_values": centred(arg_keys[4], (ROWS, SUF, KVH, HD), 1.0, 4.0, ((0, 64), (2, 8))),
        "new_keys": draw_new_keys(jax.random.fold_in(arg_keys[10], 71), 0),
        "new_values": centred(arg_keys[6], (ROWS, STEPS, KVH, HD), 1.0, 4.0, ((0, 64), (2, 8))),
        "suffix_lengths": draw_suffix_lengths(jax.random.fold_in(arg_keys[10], 71), 0),
        "prefix_of_row": draw_prefix_of_row(jax.random.fold_in(arg_keys[10], 71), 0),
        "owner_of_prefix": jax.random.permutation(arg_keys[9], PREFIXES).astype(jnp.int32),
    }


masked_score = -1e30


def reference(queries, prefix_keys, prefix_values, suffix_keys, suffix_values, new_keys, new_values, suffix_lengths, prefix_of_row, owner_of_prefix):
    group_size = HEADS // KVH
    score_scale = HD ** -0.5
    slots = owner_of_prefix[prefix_of_row].astype(jnp.int32)
    query_step = jnp.arange(group_size * STEPS, dtype=jnp.int32) % STEPS
    suffix_index = jnp.arange(SUF, dtype=jnp.int32)
    new_index = jnp.arange(STEPS, dtype=jnp.int32)

    def one_row(inputs):
        query_row, suf_key, suf_value, fresh_key, fresh_value, length, slot = inputs
        pre_key = lax.dynamic_index_in_dim(prefix_keys, slot, 0, keepdims=False).astype(jnp.float32)
        pre_value = lax.dynamic_index_in_dim(prefix_values, slot, 0, keepdims=False).astype(jnp.float32)
        query_f = query_row.astype(jnp.float32).reshape(KVH, group_size * STEPS, HD)
        pre_scores = jnp.einsum('kqd,lkd->kql', query_f, pre_key) * score_scale
        pre_max = jnp.max(pre_scores, axis=-1)
        pre_exp = jnp.exp(pre_scores - pre_max[..., None])
        pre_sum = jnp.sum(pre_exp, axis=-1)
        pre_weight = lax.optimization_barrier(pre_exp.astype(jnp.bfloat16)).astype(jnp.float32)
        pre_part = jnp.einsum('kql,lkd->kqd', pre_weight, pre_value)
        suf_scores = jnp.einsum('kqd,skd->kqs', query_f, suf_key.astype(jnp.float32)) * score_scale
        new_scores = jnp.einsum('kqd,tkd->kqt', query_f, fresh_key.astype(jnp.float32)) * score_scale
        suf_ok = jnp.broadcast_to((suffix_index < length)[None, None, :], suf_scores.shape)
        new_ok = jnp.broadcast_to((new_index[None, :] <= query_step[:, None])[None], new_scores.shape)
        loc_scores = jnp.concatenate([suf_scores, new_scores], axis=-1)
        loc_ok = jnp.concatenate([suf_ok, new_ok], axis=-1)
        loc_scores = jnp.where(loc_ok, loc_scores, masked_score)
        loc_max = jnp.max(loc_scores, axis=-1)
        loc_exp = jnp.where(loc_ok, jnp.exp(loc_scores - loc_max[..., None]), 0.0)
        loc_sum = jnp.sum(loc_exp, axis=-1)
        loc_weight = lax.optimization_barrier(loc_exp.astype(jnp.bfloat16)).astype(jnp.float32)
        loc_value = jnp.concatenate([suf_value, fresh_value], axis=0).astype(jnp.float32)
        loc_part = jnp.einsum('kqs,skd->kqd', loc_weight, loc_value)
        top_max = jnp.maximum(pre_max, loc_max)
        pre_factor = jnp.exp(pre_max - top_max)
        loc_factor = jnp.exp(loc_max - top_max)
        mixed = (pre_part * pre_factor[..., None] + loc_part * loc_factor[..., None]) / (pre_sum * pre_factor + loc_sum * loc_factor)[..., None]
        return mixed.reshape(HEADS, STEPS, HD).astype(jnp.bfloat16)

    return lax.map(one_row, (queries, suffix_keys, suffix_values, new_keys, new_values, suffix_lengths.astype(jnp.int32), slots))
```

```python
import math

import jax
import jax.numpy as jnp
from jax import lax
from jax.experimental import pallas as pl
from jax.experimental.pallas import tpu as pltpu
from jax.sharding import PartitionSpec as P

MESH = pl.DeviceIdType.MESH
masked_score = -1e30
offsets = (0, 1, 7, 2, 6, 3, 5, 4)
query_groups = ((0, 3), (3, 5))
return_groups = ((0, 3), (3, 2), (5, 2), (7, 1))


def dot_t(a, b):
    return lax.dot_general(a, b, (((1,), (1,)), ((), ())), preferred_element_type=jnp.float32)


def kernel(
    src_ref,
    slot_ref,
    len_ref,
    q4_hbm,
    q2_hbm,
    pk_hbm,
    pv_hbm,
    sk_hbm,
    sv_hbm,
    nk_hbm,
    nv_hbm,
    out_ref,
    q4,
    q2,
    kvk,
    kvv,
    sk,
    sv,
    nk,
    nv,
    qsend,
    qrecv,
    osend,
    orecv,
    ssend,
    srecv,
    snew,
    pnew,
    lpart,
    lmax,
    lsum,
    stage,
    load_sem,
    ring_send,
    ring_recv,
    q_send_sem,
    q_recv_sem,
    o_send_sem,
    o_recv_sem,
    s_send_sem,
    s_recv_sem,
    y_send_sem,
    y_recv_sem,
    own_sem,
):
    pre = lax.axis_index("pre")
    head = lax.axis_index("head")
    z = pre // 8
    me = pre % 8
    plane = z * 8
    right = ((z + 1) % 8) * 8 + me
    left = ((z + 7) % 8) * 8 + me
    to_log2 = 128 ** (-0.5) * math.log2(math.e)

    barrier = pltpu.get_barrier_semaphore()

    def greet(pre_index, head_index):
        pl.semaphore_signal(
            barrier, inc=1, device_id=(pre_index, head_index), device_id_type=MESH
        )

    greet(right, head)
    greet(left, head)
    for i in range(1, 8):
        greet(plane + (me + i) % 8, head)
    for i in range(1, 8):
        greet(pre, (head + i) % 8)

    loads = [
        pltpu.make_async_copy(a, b, load_sem.at[i])
        for i, (a, b) in enumerate(
            (
                (q4_hbm, q4),
                (q2_hbm, q2),
                (nk_hbm, nk),
                (nv_hbm, nv),
                (sk_hbm, sk),
                (sv_hbm, sv),
                (pk_hbm, kvk.at[0]),
                (pv_hbm, kvv.at[0]),
            )
        )
    ]
    for copy in loads:
        copy.start()

    def ring(way, hop, which):
        held, own = ((kvk, pk_hbm), (kvv, pv_hbm))[which]
        if way == 0:
            source, target, device = (9 - hop) % 8, 8 - hop, right
        else:
            source, target, device = hop - 1, hop, left
        return pltpu.make_async_remote_copy(
            src_ref=own if hop == 1 else held.at[source],
            dst_ref=held.at[target],
            send_sem=ring_send.at[way, hop - 1, which],
            recv_sem=ring_recv.at[way, hop - 1, which],
            device_id=(device, head),
            device_id_type=MESH,
        )

    def plane_copy(source, target, group, sends, receives, index, i):
        first, count = group
        peer = (me + i) % 8
        return pltpu.make_async_remote_copy(
            src_ref=source.at[pl.ds(first, count), peer],
            dst_ref=target.at[pl.ds(first, count), me],
            send_sem=sends.at[index, i],
            recv_sem=receives.at[index, i],
            device_id=(plane + peer, head),
            device_id_type=MESH,
        )

    def query_copy(index, i):
        return plane_copy(
            qsend, qrecv, query_groups[index], q_send_sem, q_recv_sem, index, i
        )

    def part_copy(index, i):
        return plane_copy(
            osend, orecv, return_groups[index], o_send_sem, o_recv_sem, index, i
        )

    def stat_copy(index, i):
        return plane_copy(
            ssend, srecv, return_groups[index], s_send_sem, s_recv_sem, index, i
        )

    pl.semaphore_wait(barrier, 16)
    for which in range(2):
        for way in range(2):
            ring(way, 1, which).start()

    loads[0].wait()

    def pack(k, carry):
        for d in range(8):
            first = q4[src_ref[k * 16 + d * 2]].astype(jnp.float32).reshape(24, 128)
            second = q4[src_ref[k * 16 + d * 2 + 1]].astype(jnp.float32).reshape(24, 128)
            qsend[k, d] = jnp.concatenate([first, second], axis=0).astype(jnp.bfloat16)
        return carry

    lax.fori_loop(0, 8, pack, 0)
    qrecv[:, me] = qsend[:, me]

    for index in range(2):
        for i in range(1, 8):
            query_copy(index, i).start()

    loads[1].wait()
    loads[2].wait()
    snew[...] = dot_t(q2[...], nk[...])
    loads[4].wait()
    loads[5].wait()

    def pair(i):
        rows = pl.ds(i * 48, 48)
        keys = pl.ds(i * 192, 192)
        scores = dot_t(q2[rows, :], sk[keys, :])
        row = lax.broadcasted_iota(jnp.int32, (48, 192), 0)
        lane = lax.broadcasted_iota(jnp.int32, (48, 192), 1)
        low = jnp.where(row < 24, 0, 96)
        high = jnp.where(row < 24, len_ref[2 * i], 96 + len_ref[2 * i + 1])
        scores = jnp.where((lane >= low) & (lane < high), scores, masked_score)
        row = lax.broadcasted_iota(jnp.int32, (48, 96), 0)
        lane = lax.broadcasted_iota(jnp.int32, (48, 96), 1)
        second = row >= 24
        place = lane - jnp.where(second, 2 * i + 1, 2 * i)
        within = jnp.where(second, row - 24, row)
        fresh_ok = (
            (place == 0)
            | ((place == 32) & (within >= 8))
            | ((place == 64) & (within >= 16))
        )
        fresh = jnp.where(fresh_ok, snew[rows, :], masked_score)
        top = jnp.maximum(
            jnp.max(scores, axis=1, keepdims=True), jnp.max(fresh, axis=1, keepdims=True)
        )
        scores = jnp.exp2((scores - top) * to_log2)
        fresh = jnp.exp2((fresh - top) * to_log2)
        lmax[rows, :] = top * to_log2
        lsum[rows, :] = jnp.sum(scores, axis=1, keepdims=True) + jnp.sum(
            fresh, axis=1, keepdims=True
        )
        pnew[rows, :] = fresh.astype(jnp.bfloat16)
        lpart[rows, :] = jnp.dot(
            scores.astype(jnp.bfloat16), sv[keys, :], preferred_element_type=jnp.float32
        )

    def pairs(first):
        for j in range(4):
            pair(first + j)

    def pass_on(hop, which):
        for way in range(2):
            ring(way, hop, which).wait_recv()
            if hop < 3 or which == way:
                ring(way, hop + 1, which).start()

    pairs(0)
    pairs(4)
    pass_on(1, 0)
    pairs(8)
    pairs(12)
    pass_on(1, 1)
    loads[3].wait()
    part = lpart[...] + jnp.dot(pnew[...], nv[...], preferred_element_type=jnp.float32)
    lpart[...] = part / lsum[...]
    lmax[...] = lmax[...] + jnp.log2(lsum[...])

    def block(k):
        offset = offsets[k]
        scores = dot_t(qrecv[k].reshape(384, 128), kvk[offset])
        top = jnp.max(scores, axis=1, keepdims=True)
        scores = jnp.exp2((scores - top) * to_log2)
        total = jnp.sum(scores, axis=1, keepdims=True)
        part = jnp.dot(
            scores.astype(jnp.bfloat16), kvv[offset], preferred_element_type=jnp.float32
        )
        part = (part / total).astype(jnp.bfloat16).reshape(8, 48, 128)
        level = top * to_log2 + jnp.log2(total)
        row = lax.broadcasted_iota(jnp.int32, (48, 128), 0)
        lane = lax.broadcasted_iota(jnp.int32, (48, 128), 1)
        osend[k] = part
        for d in range(8):
            ssend[k, d] = jnp.sum(
                jnp.where(row == lane, level[d * 48 : d * 48 + 48], 0.0), axis=0, keepdims=True
            )
        orecv[k, me] = osend[k, me]
        srecv[k, me] = ssend[k, me]

    def send_back(index):
        for i in range(1, 8):
            part_copy(index, i).start()
            stat_copy(index, i).start()

    for i in range(1, 8):
        query_copy(0, i).wait_recv()
    loads[6].wait()
    loads[7].wait()
    block(0)
    block(1)
    block(2)
    send_back(0)
    pass_on(2, 0)
    pass_on(2, 1)
    for i in range(1, 8):
        query_copy(1, i).wait_recv()
    block(3)
    block(4)
    send_back(1)
    pass_on(3, 0)
    pass_on(3, 1)
    block(5)
    block(6)
    send_back(2)
    ring(0, 4, 0).wait_recv()
    ring(1, 4, 1).wait_recv()
    block(7)
    send_back(3)
    for index in range(4):
        for i in range(1, 8):
            part_copy(index, i).wait_recv()
            stat_copy(index, i).wait_recv()

    def head_copy(i):
        peer = (head + i) % 8
        return pltpu.make_async_remote_copy(
            src_ref=stage.at[peer],
            dst_ref=out_ref.at[head],
            send_sem=y_send_sem.at[i],
            recv_sem=y_recv_sem.at[i],
            device_id=(pre, peer),
            device_id_type=MESH,
        )

    def combine(target):
        parts = []
        levels = []
        row = lax.broadcasted_iota(jnp.int32, (24, 128), 0)
        lane = lax.broadcasted_iota(jnp.int32, (24, 128), 1)
        for j in range(4):
            slot = slot_ref[target * 4 + j]
            which = slot % 2
            both = orecv[slot // 16, (slot // 2) % 8].astype(jnp.float32)
            stats = srecv[slot // 16, (slot // 2) % 8]
            parts.append(jnp.where(row * 0 + which == 0, both[:24], both[24:]))
            levels.append(
                jnp.sum(
                    jnp.where(lane == row + 24 * which, stats, 0.0), axis=1, keepdims=True
                )
            )
        parts = jnp.concatenate(parts, axis=0)
        levels = jnp.concatenate(levels, axis=0)
        rows = pl.ds(pl.multiple_of(target * 96, 96), 96)
        local = lmax[rows, :]
        top = jnp.maximum(levels, local)
        pre_factor = jnp.exp2(levels - top)
        local_factor = jnp.exp2(local - top)
        mixed = (parts * pre_factor + lpart[rows, :] * local_factor) / (
            pre_factor + local_factor
        )
        stage[target] = mixed.astype(jnp.bfloat16)

    for batch in ((4, 3, 5, 2), (6, 1, 7, 0)):
        for i in batch:
            combine((head + i) % 8)
        for i in batch:
            if i:
                head_copy(i).start()
    own = pltpu.make_async_copy(stage.at[head], out_ref.at[head], own_sem)
    own.start()

    for hop in range(1, 5):
        for way in range(2):
            for which in range(2):
                if hop < 4 or which == way:
                    ring(way, hop, which).wait_send()
    for index in range(2):
        for i in range(1, 8):
            query_copy(index, i).wait_send()
    for index in range(4):
        for i in range(1, 8):
            part_copy(index, i).wait_send()
            stat_copy(index, i).wait_send()
    own.wait()
    for i in range(1, 8):
        head_copy(i).wait()


def shards(
    queries,
    prefix_keys,
    prefix_values,
    suffix_keys,
    suffix_values,
    new_keys,
    new_values,
    suffix_lengths,
    prefix_of_row,
    owner_of_prefix,
):
    bf16 = jnp.bfloat16
    plane = lax.axis_index("pre") // 8
    row_index = jnp.arange(32, dtype=jnp.int32)
    lookup = prefix_of_row[:, None] == jnp.arange(64, dtype=jnp.int32)[None, :]
    owner = jnp.sum(jnp.where(lookup, owner_of_prefix[None, :], 0), axis=1)
    earlier = (prefix_of_row[:, None] == prefix_of_row[None, :]) & (
        row_index[None, :] < row_index[:, None]
    )
    rank = jnp.sum(earlier.astype(jnp.int32), axis=1)
    offset = (owner // 8 - plane + 8) % 8
    place = jnp.where(offset == 0, 0, jnp.where(offset <= 4, 2 * offset - 1, 16 - 2 * offset))
    slot = place * 16 + (owner % 8) * 2 + rank
    match = slot[None, :] == jnp.arange(128, dtype=jnp.int32)[:, None]
    source = jnp.sum(jnp.where(match, row_index[None, :], 0), axis=1)

    by_step = jnp.transpose(queries, (0, 2, 1, 3))
    smem = pl.BlockSpec(memory_space=pltpu.SMEM)
    anywhere = pl.BlockSpec(memory_space=pltpu.HBM)
    dma = pltpu.SemaphoreType.DMA
    gathered = pl.pallas_call(
        kernel,
        out_shape=jax.ShapeDtypeStruct((8, 96, 128), bf16),
        in_specs=[smem] * 3 + [anywhere] * 8,
        out_specs=anywhere,
        scratch_shapes=[
            pltpu.VMEM((32, 3, 8, 128), bf16),
            pltpu.VMEM((768, 128), bf16),
            pltpu.VMEM((8, 512, 128), bf16),
            pltpu.VMEM((8, 512, 128), bf16),
            pltpu.VMEM((3072, 128), bf16),
            pltpu.VMEM((3072, 128), bf16),
            pltpu.VMEM((96, 128), bf16),
            pltpu.VMEM((96, 128), bf16),
            pltpu.VMEM((8, 8, 48, 128), bf16),
            pltpu.VMEM((8, 8, 48, 128), bf16),
            pltpu.VMEM((8, 8, 48, 128), bf16),
            pltpu.VMEM((8, 8, 48, 128), bf16),
            pltpu.VMEM((8, 8, 1, 128), jnp.float32),
            pltpu.VMEM((8, 8, 1, 128), jnp.float32),
            pltpu.VMEM((768, 96), jnp.float32),
            pltpu.VMEM((768, 96), bf16),
            pltpu.VMEM((768, 128), jnp.float32),
            pltpu.VMEM((768, 1), jnp.float32),
            pltpu.VMEM((768, 1), jnp.float32),
            pltpu.VMEM((8, 96, 128), bf16),
            dma((8,)),
            dma((2, 4, 2)),
            dma((2, 4, 2)),
            dma((2, 8)),
            dma((2, 8)),
            dma((4, 8)),
            dma((4, 8)),
            dma((4, 8)),
            dma((4, 8)),
            dma((8,)),
            dma((8,)),
            dma,
        ],
        compiler_params=pltpu.CompilerParams(
            collective_id=0, has_side_effects=True, vmem_limit_bytes=60 * 1024 * 1024
        ),
        cost_estimate=pl.CostEstimate(
            flops=1_200_000_000, bytes_accessed=3_000_000, transcendentals=1_800_000
        ),
        name="shared_prefix",
    )(
        source,
        slot,
        suffix_lengths,
        by_step,
        by_step.reshape(768, 128),
        prefix_keys.reshape(512, 128),
        prefix_values.reshape(512, 128),
        suffix_keys.reshape(3072, 128),
        suffix_values.reshape(3072, 128),
        jnp.transpose(new_keys, (1, 2, 0, 3)).reshape(96, 128),
        jnp.transpose(new_values, (1, 2, 0, 3)).reshape(96, 128),
    )
    ordered = jnp.transpose(gathered.reshape(8, 4, 3, 8, 128), (1, 0, 3, 2, 4))
    return ordered.reshape(4, 64, 3, 128)


def solution(mesh):
    in_specs = (
        P("pre", "head", None, None),
        P("pre", None, "head", None),
        P("pre", None, "head", None),
        P("pre", None, "head", None),
        P("pre", None, "head", None),
        P("pre", None, "head", None),
        P("pre", None, "head", None),
        P("pre"),
        P("pre"),
        P(),
    )
    out_specs = P(("pre", "head"), None, None, None)
    return jax.shard_map(shards, mesh=mesh, in_specs=in_specs, out_specs=out_specs, check_vma=False)
```

```python
import math

import jax
import jax.numpy as jnp
from jax import lax
from jax.experimental import pallas as pl
from jax.experimental.pallas import tpu as pltpu
from jax.sharding import PartitionSpec as P

MESH = pl.DeviceIdType.MESH
masked_score = -1e30
offsets = (0, 1, 7, 2, 6, 3, 5, 4)
return_groups = ((0, 3), (3, 2), (5, 2), (7, 1))


def dot_t(a, b):
    return lax.dot_general(a, b, (((1,), (1,)), ((), ())), preferred_element_type=jnp.float32)


def kernel(
    prefix_hbm,
    owner_hbm,
    len_hbm,
    q4_hbm,
    q2_hbm,
    pk_hbm,
    pv_hbm,
    sk_hbm,
    sv_hbm,
    nk_hbm,
    nv_hbm,
    out_ref,
    prefix_here,
    owner_here,
    len_ref,
    index_rows,
    index_ref,
    qall,
    q2,
    kvk,
    kvv,
    sk,
    sv,
    nk,
    nv,
    qpack,
    osend,
    orecv,
    ssend,
    srecv,
    snew,
    pnew,
    lpart,
    lmax,
    lsum,
    weights,
    inverse,
    stage,
    load_sem,
    ring_send,
    ring_recv,
    q_send_sem,
    q_recv_sem,
    index_sem,
    o_send_sem,
    o_recv_sem,
    s_send_sem,
    s_recv_sem,
    y_send_sem,
    y_recv_sem,
    own_sem,
):
    pre = lax.axis_index("pre")
    head = lax.axis_index("head")
    z = pre // 8
    me = pre % 8
    plane = z * 8
    right = ((z + 1) % 8) * 8 + me
    left = ((z + 7) % 8) * 8 + me
    column, core = me // 2, me % 2
    ahead = ((column + 1) % 4) * 2 + core
    behind = ((column + 3) % 4) * 2 + core
    opposite = ((column + 2) % 4) * 2 + core
    sibling = column * 2 + 1 - core
    to_log2 = 128 ** (-0.5) * math.log2(math.e)

    barrier = pltpu.get_barrier_semaphore()

    def greet(pre_index, head_index):
        pl.semaphore_signal(
            barrier, inc=1, device_id=(pre_index, head_index), device_id_type=MESH
        )

    greet(right, head)
    greet(left, head)
    for i in range(1, 8):
        greet(plane + (me + i) % 8, head)
    for i in range(1, 8):
        greet(pre, (head + i) % 8)

    loads = [
        pltpu.make_async_copy(a, b, load_sem.at[i])
        for i, (a, b) in enumerate(
            (
                (prefix_hbm, prefix_here),
                (owner_hbm, owner_here),
                (len_hbm, len_ref),
                (q4_hbm, qall.at[me, pl.ds(0, 32)]),
                (q2_hbm, q2),
                (nk_hbm, nk),
                (nv_hbm, nv),
                (sk_hbm, sk),
                (sv_hbm, sv),
                (pk_hbm, kvk.at[0]),
                (pv_hbm, kvv.at[0]),
            )
        )
    ]
    for copy in loads:
        copy.start()

    def ring(way, hop, which):
        held, own = ((kvk, pk_hbm), (kvv, pv_hbm))[which]
        if way == 0:
            source, target, device = (9 - hop) % 8, 8 - hop, right
        else:
            source, target, device = hop - 1, hop, left
        return pltpu.make_async_remote_copy(
            src_ref=own if hop == 1 else held.at[source],
            dst_ref=held.at[target],
            send_sem=ring_send.at[which],
            recv_sem=ring_recv.at[way, hop - 1, which],
            device_id=(device, head),
            device_id_type=MESH,
        )

    def plane_copy(source, target, blocks, send_sem, recv_sem, i):
        peer = (me + i) % 8
        return pltpu.make_async_remote_copy(
            src_ref=source.at[blocks, peer],
            dst_ref=target.at[blocks, me],
            send_sem=send_sem,
            recv_sem=recv_sem,
            device_id=(plane + peer, head),
            device_id_type=MESH,
        )

    def wait_for(block, sem):
        pltpu.make_async_copy(block, block, sem).wait()

    def query_copy(i, source, rows, peer):
        block = qall.at[source, rows]
        return pltpu.make_async_remote_copy(
            src_ref=block,
            dst_ref=block,
            send_sem=q_send_sem.at[i],
            recv_sem=q_recv_sem.at[i],
            device_id=(plane + peer, head),
            device_id_type=MESH,
        )

    every, first_half, second_half = pl.ds(0, 33), pl.ds(0, 16), pl.ds(16, 17)

    seven = pl.ds(0, 7)

    def part_copy(index, i):
        blocks = pl.ds(*return_groups[index])
        return plane_copy(osend, orecv, blocks, o_send_sem.at[index], o_recv_sem.at[index], i)

    def stat_copy(i):
        return plane_copy(ssend, srecv, pl.ds(0, 8), s_send_sem, s_recv_sem, i)

    pl.semaphore_wait(barrier, 16)
    for way in range(2):
        ring(way, 1, 0).start()

    query_sends = [
        query_copy(0, me, every, ahead),
        query_copy(1, me, every, behind),
        query_copy(2, me, every, sibling),
        query_copy(3, behind, first_half, ahead),
        query_copy(4, behind, every, sibling),
        query_copy(5, ahead, second_half, behind),
        query_copy(6, ahead, every, sibling),
        query_copy(7, opposite, first_half, sibling),
        query_copy(8, opposite, second_half, sibling),
    ]
    loads[0].wait()
    qall[me, 32] = jnp.full((3, 8, 128), -1.0, jnp.bfloat16)
    qall[me, 32, 0, :, 0:32] = jnp.broadcast_to(prefix_here[...], (8, 32)).astype(jnp.bfloat16)
    loads[3].wait()
    for copy in query_sends[:3]:
        copy.start()

    loads[1].wait()

    def small_dot(a, b):
        return jnp.dot(
            a.astype(jnp.bfloat16), b.astype(jnp.bfloat16), preferred_element_type=jnp.float32
        )

    def iota(shape, dim):
        return lax.broadcasted_iota(jnp.int32, shape, dim)

    def ones_where(condition):
        return jnp.where(condition, 1.0, 0.0)

    def owner_at(k):
        offset = jnp.where((k & 1) == 1, (k + 1) >> 1, 8 - (k >> 1))
        return ((z + offset) & 7) * 8

    def named_by(d):
        names = qall[d, 32, 0].astype(jnp.float32)[0:1]
        return ones_where(names == iota((64, 128), 0).astype(jnp.float32))

    before = ones_where(iota((128, 128), 0) < iota((128, 128), 1))
    place = iota((64, 64), 0)
    owners = owner_here[...]
    held = ones_where(owners == owner_at(place >> 3) + (place & 7))
    mine = small_dot(held, named_by(me))
    earlier = small_dot(mine, before)
    slots = small_dot(2 * iota((8, 64), 1).astype(jnp.float32), mine) + small_dot(
        jnp.ones((8, 64), jnp.float32), mine * earlier
    )
    index_rows[16:24, :] = slots.astype(jnp.int32)

    loads[4].wait()
    loads[5].wait()
    snew[...] = dot_t(q2[...], nk[...])
    loads[2].wait()
    loads[7].wait()
    loads[8].wait()

    def pair(i):
        rows = pl.ds(i * 48, 48)
        keys = pl.ds(i * 192, 192)
        scores = dot_t(q2[rows, :], sk[keys, :])
        row = lax.broadcasted_iota(jnp.int32, (48, 192), 0)
        lane = lax.broadcasted_iota(jnp.int32, (48, 192), 1)
        low = jnp.where(row < 24, 0, 96)
        high = jnp.where(row < 24, len_ref[0, 2 * i], 96 + len_ref[0, 2 * i + 1])
        scores = jnp.where((lane >= low) & (lane < high), scores, masked_score)
        row = lax.broadcasted_iota(jnp.int32, (48, 96), 0)
        lane = lax.broadcasted_iota(jnp.int32, (48, 96), 1)
        second = row >= 24
        place = lane - jnp.where(second, 2 * i + 1, 2 * i)
        within = jnp.where(second, row - 24, row)
        fresh_ok = (
            (place == 0)
            | ((place == 32) & (within >= 8))
            | ((place == 64) & (within >= 16))
        )
        fresh = jnp.where(fresh_ok, snew[rows, :], masked_score)
        top = jnp.maximum(
            jnp.max(scores, axis=1, keepdims=True), jnp.max(fresh, axis=1, keepdims=True)
        )
        scores = jnp.exp2((scores - top) * to_log2)
        fresh = jnp.exp2((fresh - top) * to_log2)
        lmax[rows, :] = top * to_log2
        lsum[rows, :] = jnp.sum(scores, axis=1, keepdims=True) + jnp.sum(
            fresh, axis=1, keepdims=True
        )
        pnew[rows, :] = fresh.astype(jnp.bfloat16)
        lpart[rows, :] = jnp.dot(
            scores.astype(jnp.bfloat16), sv[keys, :], preferred_element_type=jnp.float32
        )

    def pairs(first):
        for j in range(4):
            pair(first + j)

    def pass_on(hop, which):
        for way in range(2):
            ring(way, hop, which).wait_recv()
            if hop < 3 or which == way:
                ring(way, hop + 1, which).start()

    pairs(0)
    for way in range(2):
        ring(way, 1, 1).start()
    pairs(4)
    pass_on(1, 0)
    pairs(8)
    query_sends[0].wait_recv()
    query_sends[3].start()
    query_sends[4].start()
    query_sends[1].wait_recv()
    query_sends[5].start()
    query_sends[6].start()
    pairs(12)
    loads[6].wait()
    part = lpart[...] + jnp.dot(pnew[...], nv[...], preferred_element_type=jnp.float32)
    lpart[...] = part / lsum[...]
    lmax[...] = lmax[...] + jnp.log2(lsum[...])

    def index_at(table, place, last):
        return jnp.minimum(jnp.maximum(index_ref[table * 8, place], 0), last)

    def weigh(k):
        for d in range(8):
            rows = [qall[d, index_at(rank, d * 8 + k, 31)] for rank in range(2)]
            both = [row.astype(jnp.float32).reshape(24, 128) for row in rows]
            qpack[k, d] = jnp.concatenate(both, axis=0).astype(jnp.bfloat16)
        scores = dot_t(qpack[k].reshape(384, 128), kvk[offsets[k]])
        top = jnp.max(scores, axis=1, keepdims=True)
        scores = jnp.exp2((scores - top) * to_log2)
        total = jnp.sum(scores, axis=1, keepdims=True)
        weights[k] = scores.astype(jnp.bfloat16)
        inverse[k] = 1.0 / total
        level = top * to_log2 + jnp.log2(total)
        row = iota((48, 128), 0)
        lane = iota((48, 128), 1)
        for d in range(8):
            ssend[k, d] = jnp.sum(
                jnp.where(row == lane, level[d * 48 : d * 48 + 48], 0.0), axis=0, keepdims=True
            )
        srecv[k, me] = ssend[k, me]

    def blend(k):
        part = jnp.dot(weights[k], kvv[offsets[k]], preferred_element_type=jnp.float32)
        osend[k] = (part * inverse[k]).astype(jnp.bfloat16).reshape(8, 48, 128)
        orecv[k, me] = osend[k, me]

    def send_back(index):
        for i in range(1, 8):
            part_copy(index, i).start()

    pass_on(1, 1)
    query_sends[3].wait_recv()
    query_sends[7].start()
    query_sends[5].wait_recv()
    query_sends[8].start()
    pass_on(2, 0)
    for i in (2, 4, 6, 7, 8):
        query_sends[i].wait_recv()
    here = ones_where(owners == owner_at(iota((8, 64), 0)) + me)
    match = jnp.concatenate(
        [small_dot(here, named_by(d)) for d in range(8)], axis=0
    )
    earlier = small_dot(match, before)
    numbers = iota((8, 128), 1).astype(jnp.bfloat16)
    for rank in range(2):
        chosen = jnp.where(earlier == rank, match, 0.0).astype(jnp.bfloat16)
        index_rows[rank * 8 : rank * 8 + 8, 0:64] = dot_t(numbers, chosen).astype(jnp.int32)
    index_copy = pltpu.make_async_copy(index_rows, index_ref, index_sem)
    index_copy.start()
    index_copy.wait()
    loads[9].wait()
    loads[10].wait()
    weigh(0)
    blend(0)
    weigh(1)
    weigh(2)
    blend(1)
    blend(2)
    send_back(0)
    weigh(3)
    weigh(4)
    pass_on(2, 1)
    blend(3)
    blend(4)
    send_back(1)
    pass_on(3, 0)
    weigh(5)
    weigh(6)
    pass_on(3, 1)
    blend(5)
    blend(6)
    send_back(2)
    ring(0, 4, 0).wait_recv()
    weigh(7)
    for i in range(1, 8):
        stat_copy(i).start()
    ring(1, 4, 1).wait_recv()
    blend(7)
    send_back(3)
    for index in range(4):
        wait_for(orecv.at[pl.ds(*return_groups[index]), seven], o_recv_sem.at[index])
    wait_for(srecv.at[:, seven], s_recv_sem)

    def head_copy(i):
        peer = (head + i) % 8
        return pltpu.make_async_remote_copy(
            src_ref=stage.at[peer],
            dst_ref=out_ref.at[head],
            send_sem=y_send_sem,
            recv_sem=y_recv_sem,
            device_id=(pre, peer),
            device_id_type=MESH,
        )

    def combine(target):
        parts = []
        levels = []
        row = lax.broadcasted_iota(jnp.int32, (24, 128), 0)
        lane = lax.broadcasted_iota(jnp.int32, (24, 128), 1)
        for j in range(4):
            slot = index_at(2, target * 4 + j, 127)
            which = slot % 2
            both = orecv[slot // 16, (slot // 2) % 8].astype(jnp.float32)
            stats = srecv[slot // 16, (slot // 2) % 8]
            parts.append(jnp.where(row * 0 + which == 0, both[:24], both[24:]))
            levels.append(
                jnp.sum(
                    jnp.where(lane == row + 24 * which, stats, 0.0), axis=1, keepdims=True
                )
            )
        parts = jnp.concatenate(parts, axis=0)
        levels = jnp.concatenate(levels, axis=0)
        rows = pl.ds(pl.multiple_of(target * 96, 96), 96)
        local = lmax[rows, :]
        top = jnp.maximum(levels, local)
        pre_factor = jnp.exp2(levels - top)
        local_factor = jnp.exp2(local - top)
        mixed = (parts * pre_factor + lpart[rows, :] * local_factor) / (
            pre_factor + local_factor
        )
        stage[target] = mixed.astype(jnp.bfloat16)

    for batch in ((4, 3, 5, 2), (6, 1, 7, 0)):
        for i in batch:
            combine((head + i) % 8)
        for i in batch:
            if i:
                head_copy(i).start()
    own = pltpu.make_async_copy(stage.at[head], out_ref.at[head], own_sem)
    own.start()

    for which in range(2):
        wait_for((kvk, kvv)[which].at[seven], ring_send.at[which])
    for copy in query_sends:
        copy.wait_send()
    for index in range(4):
        wait_for(osend.at[pl.ds(*return_groups[index]), seven], o_send_sem.at[index])
    wait_for(ssend.at[:, seven], s_send_sem)
    wait_for(stage.at[seven], y_send_sem)
    own.wait()
    wait_for(out_ref.at[seven], y_recv_sem)


def shards(
    queries,
    prefix_keys,
    prefix_values,
    suffix_keys,
    suffix_values,
    new_keys,
    new_values,
    suffix_lengths,
    prefix_of_row,
    owner_of_prefix,
):
    bf16 = jnp.bfloat16
    by_step = jnp.transpose(queries, (0, 2, 1, 3))
    anywhere = pl.BlockSpec(memory_space=pltpu.HBM)
    dma = pltpu.SemaphoreType.DMA
    gathered = pl.pallas_call(
        kernel,
        out_shape=jax.ShapeDtypeStruct((8, 96, 128), bf16),
        in_specs=[anywhere] * 11,
        out_specs=anywhere,
        scratch_shapes=[
            pltpu.VMEM((1, 32), jnp.int32),
            pltpu.VMEM((1, 64), jnp.int32),
            pltpu.SMEM((1, 32), jnp.int32),
            pltpu.VMEM((24, 128), jnp.int32),
            pltpu.SMEM((24, 128), jnp.int32),
            pltpu.VMEM((8, 33, 3, 8, 128), bf16),
            pltpu.VMEM((768, 128), bf16),
            pltpu.VMEM((8, 512, 128), bf16),
            pltpu.VMEM((8, 512, 128), bf16),
            pltpu.VMEM((3072, 128), bf16),
            pltpu.VMEM((3072, 128), bf16),
            pltpu.VMEM((96, 128), bf16),
            pltpu.VMEM((96, 128), bf16),
            pltpu.VMEM((8, 8, 48, 128), bf16),
            pltpu.VMEM((8, 8, 48, 128), bf16),
            pltpu.VMEM((8, 8, 48, 128), bf16),
            pltpu.VMEM((8, 8, 1, 128), jnp.float32),
            pltpu.VMEM((8, 8, 1, 128), jnp.float32),
            pltpu.VMEM((768, 96), jnp.float32),
            pltpu.VMEM((768, 96), bf16),
            pltpu.VMEM((768, 128), jnp.float32),
            pltpu.VMEM((768, 1), jnp.float32),
            pltpu.VMEM((768, 1), jnp.float32),
            pltpu.VMEM((8, 384, 512), bf16),
            pltpu.VMEM((8, 384, 1), jnp.float32),
            pltpu.VMEM((8, 96, 128), bf16),
            dma((11,)),
            dma((2,)),
            dma((2, 4, 2)),
            dma((9,)),
            dma((9,)),
            dma,
            dma((4,)),
            dma((4,)),
            dma,
            dma,
            dma,
            dma,
            dma,
        ],
        compiler_params=pltpu.CompilerParams(
            collective_id=0, has_side_effects=True, vmem_limit_bytes=60 * 1024 * 1024
        ),
        cost_estimate=pl.CostEstimate(
            flops=1_200_000_000, bytes_accessed=3_000_000, transcendentals=1_800_000
        ),
        name="shared_prefix",
    )(
        prefix_of_row.reshape(1, 32),
        owner_of_prefix.reshape(1, 64),
        suffix_lengths.reshape(1, 32),
        by_step,
        by_step.reshape(768, 128),
        prefix_keys.reshape(512, 128),
        prefix_values.reshape(512, 128),
        suffix_keys.reshape(3072, 128),
        suffix_values.reshape(3072, 128),
        jnp.transpose(new_keys, (1, 2, 0, 3)).reshape(96, 128),
        jnp.transpose(new_values, (1, 2, 0, 3)).reshape(96, 128),
    )
    ordered = jnp.transpose(gathered.reshape(8, 4, 3, 8, 128), (1, 0, 3, 2, 4))
    return ordered.reshape(4, 64, 3, 128)


def solution(mesh):
    in_specs = (
        P("pre", "head", None, None),
        P("pre", None, "head", None),
        P("pre", None, "head", None),
        P("pre", None, "head", None),
        P("pre", None, "head", None),
        P("pre", None, "head", None),
        P("pre", None, "head", None),
        P("pre"),
        P("pre"),
        P(),
    )
    out_specs = P(("pre", "head"), None, None, None)
    return jax.shard_map(shards, mesh=mesh, in_specs=in_specs, out_specs=out_specs, check_vma=False)
```

```python
import math

import jax
import jax.numpy as jnp
from jax import lax
from jax.experimental import pallas as pl
from jax.experimental.pallas import tpu as pltpu
from jax.sharding import PartitionSpec as P

MESH = pl.DeviceIdType.MESH
masked_score = -1e30
offsets = (0, 1, 7, 2, 6, 3, 5, 4)
return_groups = ((0, 3), (3, 2), (5, 2), (7, 1))


def dot_t(a, b):
    return lax.dot_general(a, b, (((1,), (1,)), ((), ())), preferred_element_type=jnp.float32)


def kernel(
    prefix_hbm,
    owner_hbm,
    len_hbm,
    q4_hbm,
    q2_hbm,
    pk_hbm,
    pv_hbm,
    sk_hbm,
    sv_hbm,
    nk_hbm,
    nv_hbm,
    out_ref,
    prefix_here,
    owner_here,
    len_ref,
    index_rows,
    index_ref,
    qall,
    q2,
    kvk,
    kvv,
    sk,
    sv,
    nk,
    nv,
    qpack,
    osend,
    orecv,
    ssend,
    srecv,
    snew,
    pnew,
    lpart,
    lmax,
    lsum,
    weights,
    inverse,
    stage,
    load_sem,
    ring_send,
    ring_recv,
    q_send_sem,
    q_recv_sem,
    index_sem,
    o_send_sem,
    o_recv_sem,
    s_send_sem,
    s_recv_sem,
    y_send_sem,
    y_recv_sem,
    own_sem,
    above_here,
    below_here,
):
    pre = lax.axis_index("pre")
    head = lax.axis_index("head")
    z = pre // 8
    me = pre % 8
    plane = z * 8
    right = ((z + 1) % 8) * 8 + me
    left = ((z + 7) % 8) * 8 + me
    column, core = me // 2, me % 2
    ahead = ((column + 1) % 4) * 2 + core
    behind = ((column + 3) % 4) * 2 + core
    opposite = ((column + 2) % 4) * 2 + core
    sibling = column * 2 + 1 - core
    to_log2 = 128 ** (-0.5) * math.log2(math.e)

    barrier = pltpu.get_barrier_semaphore()

    def greet(pre_index, head_index):
        pl.semaphore_signal(
            barrier, inc=1, device_id=(pre_index, head_index), device_id_type=MESH
        )

    above, below = (head + 1) % 8, (head + 7) % 8
    for peer in (right, left, plane + ahead, plane + behind, plane + sibling):
        greet(peer, head)
    greet(pre, above)
    greet(pre, below)

    loads = [
        pltpu.make_async_copy(a, b, load_sem.at[i])
        for i, (a, b) in enumerate(
            (
                (prefix_hbm, prefix_here),
                (owner_hbm, owner_here),
                (len_hbm, len_ref),
                (q4_hbm, qall.at[me, pl.ds(0, 32)]),
                (q2_hbm, q2),
                (nk_hbm, nk),
                (nv_hbm, nv),
                (sk_hbm, sk),
                (sv_hbm, sv),
                (pk_hbm, kvk.at[0]),
                (pv_hbm, kvv.at[0]),
            )
        )
    ]
    for copy in loads:
        copy.start()

    def ring(way, hop, which):
        held, own = ((kvk, pk_hbm), (kvv, pv_hbm))[which]
        if way == 0:
            source, target, device = (9 - hop) % 8, 8 - hop, right
        else:
            source, target, device = hop - 1, hop, left
        return pltpu.make_async_remote_copy(
            src_ref=own if hop == 1 else held.at[source],
            dst_ref=held.at[target],
            send_sem=ring_send.at[which],
            recv_sem=ring_recv.at[way, hop - 1, which],
            device_id=(device, head),
            device_id_type=MESH,
        )

    def plane_copy(source, target, blocks, send_sem, recv_sem, i):
        peer = (me + i) % 8
        return pltpu.make_async_remote_copy(
            src_ref=source.at[blocks, peer],
            dst_ref=target.at[blocks, me],
            send_sem=send_sem,
            recv_sem=recv_sem,
            device_id=(plane + peer, head),
            device_id_type=MESH,
        )

    def wait_for(block, sem):
        pltpu.make_async_copy(block, block, sem).wait()

    def query_copy(i, source, rows, peer):
        block = qall.at[source, rows]
        return pltpu.make_async_remote_copy(
            src_ref=block,
            dst_ref=block,
            send_sem=q_send_sem.at[i],
            recv_sem=q_recv_sem.at[i],
            device_id=(plane + peer, head),
            device_id_type=MESH,
        )

    every, first_half, second_half = pl.ds(0, 33), pl.ds(0, 16), pl.ds(16, 17)

    seven = pl.ds(0, 7)

    def part_copy(index, i):
        blocks = pl.ds(*return_groups[index])
        return plane_copy(osend, orecv, blocks, o_send_sem.at[index], o_recv_sem.at[index], i)

    def stat_copy(i):
        return plane_copy(ssend, srecv, pl.ds(0, 8), s_send_sem, s_recv_sem, i)

    pl.semaphore_wait(barrier, 7)
    for way in range(2):
        ring(way, 1, 0).start()

    def token(from_above, step):
        tokens, peer = (above_here, below) if from_above else (below_here, above)
        pl.semaphore_signal(
            tokens.at[step], inc=1, device_id=(pre, peer), device_id_type=MESH
        )

    token(True, 0)
    token(False, 0)

    query_sends = [
        query_copy(0, me, every, ahead),
        query_copy(1, me, every, behind),
        query_copy(2, me, every, sibling),
        query_copy(3, behind, first_half, ahead),
        query_copy(4, behind, every, sibling),
        query_copy(5, ahead, second_half, behind),
        query_copy(6, ahead, every, sibling),
        query_copy(7, opposite, first_half, sibling),
        query_copy(8, opposite, second_half, sibling),
    ]
    loads[0].wait()
    qall[me, 32] = jnp.full((3, 8, 128), -1.0, jnp.bfloat16)
    qall[me, 32, 0, :, 0:32] = jnp.broadcast_to(prefix_here[...], (8, 32)).astype(jnp.bfloat16)
    loads[3].wait()
    for copy in query_sends[:3]:
        copy.start()

    loads[1].wait()

    def small_dot(a, b):
        return jnp.dot(
            a.astype(jnp.bfloat16), b.astype(jnp.bfloat16), preferred_element_type=jnp.float32
        )

    def iota(shape, dim):
        return lax.broadcasted_iota(jnp.int32, shape, dim)

    def ones_where(condition):
        return jnp.where(condition, 1.0, 0.0)

    def owner_at(k):
        offset = jnp.where((k & 1) == 1, (k + 1) >> 1, 8 - (k >> 1))
        return ((z + offset) & 7) * 8

    def named_by(d):
        names = qall[d, 32, 0].astype(jnp.float32)[0:1]
        return ones_where(names == iota((64, 128), 0).astype(jnp.float32))

    before = ones_where(iota((128, 128), 0) < iota((128, 128), 1))
    place = iota((64, 64), 0)
    owners = owner_here[...]
    held = ones_where(owners == owner_at(place >> 3) + (place & 7))
    mine = small_dot(held, named_by(me))
    earlier = small_dot(mine, before)
    slots = small_dot(2 * iota((8, 64), 1).astype(jnp.float32), mine) + small_dot(
        jnp.ones((8, 64), jnp.float32), mine * earlier
    )
    index_rows[16:24, :] = slots.astype(jnp.int32)

    loads[4].wait()
    loads[5].wait()
    snew[...] = dot_t(q2[...], nk[...])
    loads[2].wait()
    loads[7].wait()
    loads[8].wait()

    def pair(i):
        rows = pl.ds(i * 48, 48)
        keys = pl.ds(i * 192, 192)
        scores = dot_t(q2[rows, :], sk[keys, :])
        row = lax.broadcasted_iota(jnp.int32, (48, 192), 0)
        lane = lax.broadcasted_iota(jnp.int32, (48, 192), 1)
        low = jnp.where(row < 24, 0, 96)
        high = jnp.where(row < 24, len_ref[0, 2 * i], 96 + len_ref[0, 2 * i + 1])
        scores = jnp.where((lane >= low) & (lane < high), scores, masked_score)
        row = lax.broadcasted_iota(jnp.int32, (48, 96), 0)
        lane = lax.broadcasted_iota(jnp.int32, (48, 96), 1)
        second = row >= 24
        place = lane - jnp.where(second, 2 * i + 1, 2 * i)
        within = jnp.where(second, row - 24, row)
        fresh_ok = (
            (place == 0)
            | ((place == 32) & (within >= 8))
            | ((place == 64) & (within >= 16))
        )
        fresh = jnp.where(fresh_ok, snew[rows, :], masked_score)
        top = jnp.maximum(
            jnp.max(scores, axis=1, keepdims=True), jnp.max(fresh, axis=1, keepdims=True)
        )
        scores = jnp.exp2((scores - top) * to_log2)
        fresh = jnp.exp2((fresh - top) * to_log2)
        lmax[rows, :] = top * to_log2
        lsum[rows, :] = jnp.sum(scores, axis=1, keepdims=True) + jnp.sum(
            fresh, axis=1, keepdims=True
        )
        pnew[rows, :] = fresh.astype(jnp.bfloat16)
        lpart[rows, :] = jnp.dot(
            scores.astype(jnp.bfloat16), sv[keys, :], preferred_element_type=jnp.float32
        )

    def pairs(first):
        for j in range(4):
            pair(first + j)

    def pass_on(hop, which):
        for way in range(2):
            ring(way, hop, which).wait_recv()
            if hop < 3 or which == way:
                ring(way, hop + 1, which).start()

    pairs(0)
    for way in range(2):
        ring(way, 1, 1).start()
    pairs(4)
    pass_on(1, 0)
    pairs(8)
    query_sends[0].wait_recv()
    query_sends[3].start()
    query_sends[4].start()
    query_sends[1].wait_recv()
    query_sends[5].start()
    query_sends[6].start()
    pairs(12)
    loads[6].wait()
    part = lpart[...] + jnp.dot(pnew[...], nv[...], preferred_element_type=jnp.float32)
    lpart[...] = part / lsum[...]
    lmax[...] = lmax[...] + jnp.log2(lsum[...])

    def index_at(table, place, last):
        return jnp.minimum(jnp.maximum(index_ref[table * 8, place], 0), last)

    def weigh(k):
        for d in range(8):
            rows = [qall[d, index_at(rank, d * 8 + k, 31)] for rank in range(2)]
            both = [row.astype(jnp.float32).reshape(24, 128) for row in rows]
            qpack[k, d] = jnp.concatenate(both, axis=0).astype(jnp.bfloat16)
        scores = dot_t(qpack[k].reshape(384, 128), kvk[offsets[k]])
        top = jnp.max(scores, axis=1, keepdims=True)
        scores = jnp.exp2((scores - top) * to_log2)
        total = jnp.sum(scores, axis=1, keepdims=True)
        weights[k] = scores.astype(jnp.bfloat16)
        inverse[k] = 1.0 / total
        level = top * to_log2 + jnp.log2(total)
        row = iota((48, 128), 0)
        lane = iota((48, 128), 1)
        for d in range(8):
            ssend[k, d] = jnp.sum(
                jnp.where(row == lane, level[d * 48 : d * 48 + 48], 0.0), axis=0, keepdims=True
            )
        srecv[k, me] = ssend[k, me]

    def blend(k):
        part = jnp.dot(weights[k], kvv[offsets[k]], preferred_element_type=jnp.float32)
        osend[k] = (part * inverse[k]).astype(jnp.bfloat16).reshape(8, 48, 128)
        orecv[k, me] = osend[k, me]

    def send_back(index):
        for i in range(1, 8):
            part_copy(index, i).start()

    pass_on(1, 1)
    query_sends[3].wait_recv()
    query_sends[7].start()
    query_sends[5].wait_recv()
    query_sends[8].start()
    pass_on(2, 0)
    for i in (2, 4, 6, 7, 8):
        query_sends[i].wait_recv()
    here = ones_where(owners == owner_at(iota((8, 64), 0)) + me)
    match = jnp.concatenate(
        [small_dot(here, named_by(d)) for d in range(8)], axis=0
    )
    earlier = small_dot(match, before)
    numbers = iota((8, 128), 1).astype(jnp.bfloat16)
    for rank in range(2):
        chosen = jnp.where(earlier == rank, match, 0.0).astype(jnp.bfloat16)
        index_rows[rank * 8 : rank * 8 + 8, 0:64] = dot_t(numbers, chosen).astype(jnp.int32)
    index_copy = pltpu.make_async_copy(index_rows, index_ref, index_sem)
    index_copy.start()
    index_copy.wait()
    loads[9].wait()
    loads[10].wait()
    weigh(0)
    blend(0)
    weigh(1)
    weigh(2)
    blend(1)
    blend(2)
    send_back(0)
    weigh(3)
    weigh(4)
    pass_on(2, 1)
    pl.semaphore_wait(above_here.at[0], 1)
    token(True, 1)
    pl.semaphore_wait(below_here.at[0], 1)
    token(False, 1)
    blend(3)
    blend(4)
    send_back(1)
    pass_on(3, 0)
    weigh(5)
    weigh(6)
    pass_on(3, 1)
    pl.semaphore_wait(above_here.at[1], 1)
    token(True, 2)
    pl.semaphore_wait(below_here.at[1], 1)
    blend(5)
    blend(6)
    send_back(2)
    ring(0, 4, 0).wait_recv()
    weigh(7)
    for i in range(1, 8):
        stat_copy(i).start()
    ring(1, 4, 1).wait_recv()
    blend(7)
    send_back(3)
    for index in range(4):
        wait_for(orecv.at[pl.ds(*return_groups[index]), seven], o_recv_sem.at[index])
    wait_for(srecv.at[:, seven], s_recv_sem)

    def head_copy(i):
        peer = (head + i) % 8
        return pltpu.make_async_remote_copy(
            src_ref=stage.at[peer],
            dst_ref=out_ref.at[head],
            send_sem=y_send_sem,
            recv_sem=y_recv_sem,
            device_id=(pre, peer),
            device_id_type=MESH,
        )

    def combine(target):
        parts = []
        levels = []
        row = lax.broadcasted_iota(jnp.int32, (24, 128), 0)
        lane = lax.broadcasted_iota(jnp.int32, (24, 128), 1)
        for j in range(4):
            slot = index_at(2, target * 4 + j, 127)
            which = slot % 2
            both = orecv[slot // 16, (slot // 2) % 8].astype(jnp.float32)
            stats = srecv[slot // 16, (slot // 2) % 8]
            parts.append(jnp.where(row * 0 + which == 0, both[:24], both[24:]))
            levels.append(
                jnp.sum(
                    jnp.where(lane == row + 24 * which, stats, 0.0), axis=1, keepdims=True
                )
            )
        parts = jnp.concatenate(parts, axis=0)
        levels = jnp.concatenate(levels, axis=0)
        rows = pl.ds(pl.multiple_of(target * 96, 96), 96)
        local = lmax[rows, :]
        top = jnp.maximum(levels, local)
        pre_factor = jnp.exp2(levels - top)
        local_factor = jnp.exp2(local - top)
        mixed = (parts * pre_factor + lpart[rows, :] * local_factor) / (
            pre_factor + local_factor
        )
        stage[target] = mixed.astype(jnp.bfloat16)

    pl.semaphore_wait(above_here.at[2], 1)
    for batch in ((4, 3, 5, 2), (6, 1, 7, 0)):
        for i in batch:
            combine((head + i) % 8)
        for i in batch:
            if i:
                head_copy(i).start()
    own = pltpu.make_async_copy(stage.at[head], out_ref.at[head], own_sem)
    own.start()

    for which in range(2):
        wait_for((kvk, kvv)[which].at[seven], ring_send.at[which])
    for copy in query_sends:
        copy.wait_send()
    for index in range(4):
        wait_for(osend.at[pl.ds(*return_groups[index]), seven], o_send_sem.at[index])
    wait_for(ssend.at[:, seven], s_send_sem)
    wait_for(stage.at[seven], y_send_sem)
    own.wait()
    wait_for(out_ref.at[seven], y_recv_sem)


def shards(
    queries,
    prefix_keys,
    prefix_values,
    suffix_keys,
    suffix_values,
    new_keys,
    new_values,
    suffix_lengths,
    prefix_of_row,
    owner_of_prefix,
):
    bf16 = jnp.bfloat16
    by_step = jnp.transpose(queries, (0, 2, 1, 3))
    anywhere = pl.BlockSpec(memory_space=pltpu.HBM)
    dma = pltpu.SemaphoreType.DMA
    gathered = pl.pallas_call(
        kernel,
        out_shape=jax.ShapeDtypeStruct((8, 96, 128), bf16),
        in_specs=[anywhere] * 11,
        out_specs=anywhere,
        scratch_shapes=[
            pltpu.VMEM((1, 32), jnp.int32),
            pltpu.VMEM((1, 64), jnp.int32),
            pltpu.SMEM((1, 32), jnp.int32),
            pltpu.VMEM((24, 128), jnp.int32),
            pltpu.SMEM((24, 128), jnp.int32),
            pltpu.VMEM((8, 33, 3, 8, 128), bf16),
            pltpu.VMEM((768, 128), bf16),
            pltpu.VMEM((8, 512, 128), bf16),
            pltpu.VMEM((8, 512, 128), bf16),
            pltpu.VMEM((3072, 128), bf16),
            pltpu.VMEM((3072, 128), bf16),
            pltpu.VMEM((96, 128), bf16),
            pltpu.VMEM((96, 128), bf16),
            pltpu.VMEM((8, 8, 48, 128), bf16),
            pltpu.VMEM((8, 8, 48, 128), bf16),
            pltpu.VMEM((8, 8, 48, 128), bf16),
            pltpu.VMEM((8, 8, 1, 128), jnp.float32),
            pltpu.VMEM((8, 8, 1, 128), jnp.float32),
            pltpu.VMEM((768, 96), jnp.float32),
            pltpu.VMEM((768, 96), bf16),
            pltpu.VMEM((768, 128), jnp.float32),
            pltpu.VMEM((768, 1), jnp.float32),
            pltpu.VMEM((768, 1), jnp.float32),
            pltpu.VMEM((8, 384, 512), bf16),
            pltpu.VMEM((8, 384, 1), jnp.float32),
            pltpu.VMEM((8, 96, 128), bf16),
            dma((11,)),
            dma((2,)),
            dma((2, 4, 2)),
            dma((9,)),
            dma((9,)),
            dma,
            dma((4,)),
            dma((4,)),
            dma,
            dma,
            dma,
            dma,
            dma,
            pltpu.SemaphoreType.REGULAR((3,)),
            pltpu.SemaphoreType.REGULAR((2,)),
        ],
        compiler_params=pltpu.CompilerParams(
            collective_id=0, has_side_effects=True, vmem_limit_bytes=60 * 1024 * 1024
        ),
        cost_estimate=pl.CostEstimate(
            flops=1_200_000_000, bytes_accessed=3_000_000, transcendentals=1_800_000
        ),
        name="shared_prefix",
    )(
        prefix_of_row.reshape(1, 32),
        owner_of_prefix.reshape(1, 64),
        suffix_lengths.reshape(1, 32),
        by_step,
        by_step.reshape(768, 128),
        prefix_keys.reshape(512, 128),
        prefix_values.reshape(512, 128),
        suffix_keys.reshape(3072, 128),
        suffix_values.reshape(3072, 128),
        jnp.transpose(new_keys, (1, 2, 0, 3)).reshape(96, 128),
        jnp.transpose(new_values, (1, 2, 0, 3)).reshape(96, 128),
    )
    ordered = jnp.transpose(gathered.reshape(8, 4, 3, 8, 128), (1, 0, 3, 2, 4))
    return ordered.reshape(4, 64, 3, 128)


def solution(mesh):
    in_specs = (
        P("pre", "head", None, None),
        P("pre", None, "head", None),
        P("pre", None, "head", None),
        P("pre", None, "head", None),
        P("pre", None, "head", None),
        P("pre", None, "head", None),
        P("pre", None, "head", None),
        P("pre"),
        P("pre"),
        P(),
    )
    out_specs = P(("pre", "head"), None, None, None)
    return jax.shard_map(shards, mesh=mesh, in_specs=in_specs, out_specs=out_specs, check_vma=False)
```

```python
import math

import jax
import jax.numpy as jnp
from jax import lax
from jax.experimental import pallas as pl
from jax.experimental.pallas import tpu as pltpu
from jax.sharding import PartitionSpec as P

MESH = pl.DeviceIdType.MESH
masked_score = -1e30
offsets = (0, 1, 7, 2, 6, 3, 5, 4)
return_groups = ((0, 3), (3, 2), (5, 2), (7, 1))


def dot_t(a, b):
    return lax.dot_general(a, b, (((1,), (1,)), ((), ())), preferred_element_type=jnp.float32)


def kernel(
    prefix_hbm,
    owner_hbm,
    len_hbm,
    q4_hbm,
    q2_hbm,
    pk_hbm,
    pv_hbm,
    sk_hbm,
    sv_hbm,
    nk_hbm,
    nv_hbm,
    out_ref,
    prefix_here,
    owner_here,
    len_ref,
    index_rows,
    index_ref,
    qall,
    q2,
    kvk,
    kvv,
    sk,
    sv,
    nk,
    nv,
    qpack,
    osend,
    orecv,
    ssend,
    srecv,
    snew,
    pnew,
    lpart,
    lmax,
    lsum,
    weights,
    inverse,
    stage,
    load_sem,
    ring_send,
    ring_recv,
    q_send_sem,
    q_recv_sem,
    index_sem,
    o_send_sem,
    o_recv_sem,
    s_send_sem,
    s_recv_sem,
    y_send_sem,
    y_recv_sem,
    own_sem,
    above_here,
    below_here,
):
    pre = lax.axis_index("pre")
    head = lax.axis_index("head")
    z = pre // 8
    me = pre % 8
    plane = z * 8
    right = ((z + 1) % 8) * 8 + me
    left = ((z + 7) % 8) * 8 + me
    column, core = me // 2, me % 2
    ahead = ((column + 1) % 4) * 2 + core
    behind = ((column + 3) % 4) * 2 + core
    opposite = ((column + 2) % 4) * 2 + core
    sibling = column * 2 + 1 - core
    to_log2 = 128 ** (-0.5) * math.log2(math.e)

    barrier = pltpu.get_barrier_semaphore()

    def greet(pre_index, head_index):
        pl.semaphore_signal(
            barrier, inc=1, device_id=(pre_index, head_index), device_id_type=MESH
        )

    above, below = (head + 1) % 8, (head + 7) % 8
    for peer in (right, left, plane + ahead, plane + behind, plane + sibling):
        greet(peer, head)
    greet(pre, above)
    greet(pre, below)

    loads = [
        pltpu.make_async_copy(a, b, load_sem.at[i])
        for i, (a, b) in enumerate(
            (
                (prefix_hbm, prefix_here),
                (owner_hbm, owner_here),
                (len_hbm, len_ref),
                (q4_hbm, qall.at[me, pl.ds(1, 32)]),
                (q2_hbm, q2),
                (nk_hbm, nk),
                (nv_hbm, nv),
                (sk_hbm, sk),
                (sv_hbm, sv),
                (pk_hbm, kvk.at[0]),
                (pv_hbm, kvv.at[0]),
            )
        )
    ]
    for i in (0, 1, 3):
        loads[i].start()

    def ring(way, hop, which):
        held, own = ((kvk, pk_hbm), (kvv, pv_hbm))[which]
        if way == 0:
            source, target, device = (9 - hop) % 8, 8 - hop, right
        else:
            source, target, device = hop - 1, hop, left
        return pltpu.make_async_remote_copy(
            src_ref=own if hop == 1 else held.at[source],
            dst_ref=held.at[target],
            send_sem=ring_send.at[which],
            recv_sem=ring_recv.at[way, hop - 1, which],
            device_id=(device, head),
            device_id_type=MESH,
        )

    def plane_copy(source, target, blocks, send_sem, recv_sem, i):
        peer = (me + i) % 8
        return pltpu.make_async_remote_copy(
            src_ref=source.at[blocks, peer],
            dst_ref=target.at[blocks, me],
            send_sem=send_sem,
            recv_sem=recv_sem,
            device_id=(plane + peer, head),
            device_id_type=MESH,
        )

    def wait_for(block, sem):
        pltpu.make_async_copy(block, block, sem).wait()

    def query_copy(i, source, rows, peer):
        block = qall.at[source, rows]
        return pltpu.make_async_remote_copy(
            src_ref=block,
            dst_ref=block,
            send_sem=q_send_sem.at[i],
            recv_sem=q_recv_sem.at[i],
            device_id=(plane + peer, head),
            device_id_type=MESH,
        )

    every, first_half, second_half = pl.ds(0, 33), pl.ds(0, 17), pl.ds(17, 16)

    seven = pl.ds(0, 7)

    def part_copy(index, i):
        blocks = pl.ds(*return_groups[index])
        return plane_copy(osend, orecv, blocks, o_send_sem.at[index], o_recv_sem.at[index], i)

    def stat_copy(i):
        return plane_copy(ssend, srecv, pl.ds(0, 8), s_send_sem, s_recv_sem, i)

    pl.semaphore_wait(barrier, 7)
    for way in range(2):
        ring(way, 1, 0).start()
    for i in (4, 5, 2, 7, 8, 6, 9, 10):
        loads[i].start()

    def token(from_above, step):
        tokens, peer = (above_here, below) if from_above else (below_here, above)
        pl.semaphore_signal(
            tokens.at[step], inc=1, device_id=(pre, peer), device_id_type=MESH
        )

    token(True, 0)
    token(False, 0)

    query_sends = [
        query_copy(0, me, first_half, ahead),
        query_copy(1, me, first_half, behind),
        query_copy(2, me, second_half, ahead),
        query_copy(3, me, second_half, behind),
        query_copy(4, me, every, sibling),
        query_copy(5, behind, first_half, ahead),
        query_copy(6, ahead, second_half, behind),
        query_copy(7, behind, first_half, sibling),
        query_copy(8, ahead, first_half, sibling),
        query_copy(9, behind, second_half, sibling),
        query_copy(10, ahead, second_half, sibling),
        query_copy(11, opposite, first_half, sibling),
        query_copy(12, opposite, second_half, sibling),
    ]

    def hand_on(arrived, onward):
        query_sends[arrived].wait_recv()
        for i in onward:
            query_sends[i].start()

    loads[0].wait()
    qall[me, 0] = jnp.full((3, 8, 128), -1.0, jnp.bfloat16)
    qall[me, 0, 0, :, 0:32] = jnp.broadcast_to(prefix_here[...], (8, 32)).astype(jnp.bfloat16)
    loads[3].wait()
    for copy in query_sends[:5]:
        copy.start()

    loads[1].wait()

    def small_dot(a, b):
        return jnp.dot(
            a.astype(jnp.bfloat16), b.astype(jnp.bfloat16), preferred_element_type=jnp.float32
        )

    def iota(shape, dim):
        return lax.broadcasted_iota(jnp.int32, shape, dim)

    def ones_where(condition):
        return jnp.where(condition, 1.0, 0.0)

    def owner_at(k):
        offset = jnp.where((k & 1) == 1, (k + 1) >> 1, 8 - (k >> 1))
        return ((z + offset) & 7) * 8

    def named_by(d):
        names = qall[d, 0, 0].astype(jnp.float32)[0:1]
        return ones_where(names == iota((64, 128), 0).astype(jnp.float32))

    before = ones_where(iota((128, 128), 0) < iota((128, 128), 1))
    place = iota((64, 64), 0)
    owners = owner_here[...]
    held = ones_where(owners == owner_at(place >> 3) + (place & 7))
    mine = small_dot(held, named_by(me))
    earlier = small_dot(mine, before)
    slots = small_dot(2 * iota((8, 64), 1).astype(jnp.float32), mine) + small_dot(
        jnp.ones((8, 64), jnp.float32), mine * earlier
    )
    index_rows[16:24, :] = slots.astype(jnp.int32)

    loads[4].wait()
    loads[5].wait()
    snew[...] = dot_t(q2[...], nk[...])
    loads[2].wait()
    loads[7].wait()
    loads[8].wait()

    def pair(i):
        rows = pl.ds(i * 48, 48)
        keys = pl.ds(i * 192, 192)
        scores = dot_t(q2[rows, :], sk[keys, :])
        row = lax.broadcasted_iota(jnp.int32, (48, 192), 0)
        lane = lax.broadcasted_iota(jnp.int32, (48, 192), 1)
        low = jnp.where(row < 24, 0, 96)
        high = jnp.where(row < 24, len_ref[0, 2 * i], 96 + len_ref[0, 2 * i + 1])
        scores = jnp.where((lane >= low) & (lane < high), scores, masked_score)
        row = lax.broadcasted_iota(jnp.int32, (48, 96), 0)
        lane = lax.broadcasted_iota(jnp.int32, (48, 96), 1)
        second = row >= 24
        place = lane - jnp.where(second, 2 * i + 1, 2 * i)
        within = jnp.where(second, row - 24, row)
        fresh_ok = (
            (place == 0)
            | ((place == 32) & (within >= 8))
            | ((place == 64) & (within >= 16))
        )
        fresh = jnp.where(fresh_ok, snew[rows, :], masked_score)
        top = jnp.maximum(
            jnp.max(scores, axis=1, keepdims=True), jnp.max(fresh, axis=1, keepdims=True)
        )
        scores = jnp.exp2((scores - top) * to_log2)
        fresh = jnp.exp2((fresh - top) * to_log2)
        lmax[rows, :] = top * to_log2
        lsum[rows, :] = jnp.sum(scores, axis=1, keepdims=True) + jnp.sum(
            fresh, axis=1, keepdims=True
        )
        pnew[rows, :] = fresh.astype(jnp.bfloat16)
        lpart[rows, :] = jnp.dot(
            scores.astype(jnp.bfloat16), sv[keys, :], preferred_element_type=jnp.float32
        )

    def pairs(first):
        for j in range(4):
            pair(first + j)

    def pass_on(hop, which):
        for way in range(2):
            ring(way, hop, which).wait_recv()
            if hop < 3 or which == way:
                ring(way, hop + 1, which).start()

    pairs(0)
    for way in range(2):
        ring(way, 1, 1).start()
    hand_on(0, (5, 7))
    hand_on(1, (8,))
    pass_on(1, 0)
    pairs(4)
    hand_on(2, (9,))
    hand_on(3, (6, 10))

    def index_at(table, place, last):
        return jnp.minimum(jnp.maximum(index_ref[table * 8, place], 0), last)

    def weigh(k):
        for d in range(8):
            rows = [qall[d, 1 + index_at(rank, d * 8 + k, 31)] for rank in range(2)]
            both = [row.astype(jnp.float32).reshape(24, 128) for row in rows]
            qpack[k, d] = jnp.concatenate(both, axis=0).astype(jnp.bfloat16)
        scores = dot_t(qpack[k].reshape(384, 128), kvk[offsets[k]])
        top = jnp.max(scores, axis=1, keepdims=True)
        scores = jnp.exp2((scores - top) * to_log2)
        weights[k] = scores.astype(jnp.bfloat16)
        total = jnp.dot(
            weights[k], jnp.ones((512, 128), jnp.bfloat16), preferred_element_type=jnp.float32
        )
        inverse[k] = 1.0 / total
        level = top * to_log2 + jnp.log2(total)
        row = iota((48, 128), 0)
        lane = iota((48, 128), 1)
        for d in range(8):
            ssend[k, d] = jnp.sum(
                jnp.where(row == lane, level[d * 48 : d * 48 + 48], 0.0), axis=0, keepdims=True
            )
        srecv[k, me] = ssend[k, me]

    def blend(k):
        part = jnp.dot(weights[k], kvv[offsets[k]], preferred_element_type=jnp.float32)
        osend[k] = (part * inverse[k]).astype(jnp.bfloat16).reshape(8, 48, 128)
        orecv[k, me] = osend[k, me]

    def send_back(index):
        for i in range(1, 8):
            part_copy(index, i).start()

    hand_on(5, (11,))
    pass_on(1, 1)
    hand_on(6, (12,))
    for i in (4, 7, 8, 11):
        query_sends[i].wait_recv()
    here = ones_where(owners == owner_at(iota((8, 64), 0)) + me)
    match = jnp.concatenate(
        [small_dot(here, named_by(d)) for d in range(8)], axis=0
    )
    earlier = small_dot(match, before)
    numbers = iota((8, 128), 1).astype(jnp.bfloat16)
    for rank in range(2):
        chosen = jnp.where(earlier == rank, match, 0.0).astype(jnp.bfloat16)
        index_rows[rank * 8 : rank * 8 + 8, 0:64] = dot_t(numbers, chosen).astype(jnp.int32)
    index_copy = pltpu.make_async_copy(index_rows, index_ref, index_sem)
    index_copy.start()
    pass_on(2, 0)
    for i in (9, 10, 12):
        query_sends[i].wait_recv()
    index_copy.wait()
    loads[9].wait()
    loads[10].wait()
    weigh(0)
    blend(0)
    weigh(1)
    weigh(2)
    blend(1)
    blend(2)
    send_back(0)
    weigh(3)
    weigh(4)
    pairs(8)
    pass_on(2, 1)
    pl.semaphore_wait(above_here.at[0], 1)
    token(True, 1)
    pl.semaphore_wait(below_here.at[0], 1)
    token(False, 1)
    blend(3)
    blend(4)
    send_back(1)
    pairs(12)
    pass_on(3, 0)
    weigh(5)
    weigh(6)
    pass_on(3, 1)
    pl.semaphore_wait(above_here.at[1], 1)
    token(True, 2)
    pl.semaphore_wait(below_here.at[1], 1)
    blend(5)
    blend(6)
    send_back(2)
    loads[6].wait()
    part = lpart[...] + jnp.dot(pnew[...], nv[...], preferred_element_type=jnp.float32)
    lpart[...] = part / lsum[...]
    lmax[...] = lmax[...] + jnp.log2(lsum[...])
    ring(0, 4, 0).wait_recv()
    weigh(7)
    for i in range(1, 8):
        stat_copy(i).start()
    ring(1, 4, 1).wait_recv()
    blend(7)
    send_back(3)
    for index in range(4):
        wait_for(orecv.at[pl.ds(*return_groups[index]), seven], o_recv_sem.at[index])
    wait_for(srecv.at[:, seven], s_recv_sem)

    def head_copy(i):
        peer = (head + i) % 8
        return pltpu.make_async_remote_copy(
            src_ref=stage.at[peer],
            dst_ref=out_ref.at[head],
            send_sem=y_send_sem,
            recv_sem=y_recv_sem,
            device_id=(pre, peer),
            device_id_type=MESH,
        )

    def combine(target):
        parts = []
        levels = []
        row = lax.broadcasted_iota(jnp.int32, (24, 128), 0)
        lane = lax.broadcasted_iota(jnp.int32, (24, 128), 1)
        for j in range(4):
            slot = index_at(2, target * 4 + j, 127)
            which = slot % 2
            both = orecv[slot // 16, (slot // 2) % 8].astype(jnp.float32)
            stats = srecv[slot // 16, (slot // 2) % 8]
            parts.append(jnp.where(row * 0 + which == 0, both[:24], both[24:]))
            levels.append(
                jnp.sum(
                    jnp.where(lane == row + 24 * which, stats, 0.0), axis=1, keepdims=True
                )
            )
        parts = jnp.concatenate(parts, axis=0)
        levels = jnp.concatenate(levels, axis=0)
        rows = pl.ds(pl.multiple_of(target * 96, 96), 96)
        local = lmax[rows, :]
        top = jnp.maximum(levels, local)
        pre_factor = jnp.exp2(levels - top)
        local_factor = jnp.exp2(local - top)
        mixed = (parts * pre_factor + lpart[rows, :] * local_factor) / (
            pre_factor + local_factor
        )
        stage[target] = mixed.astype(jnp.bfloat16)

    pl.semaphore_wait(above_here.at[2], 1)
    for batch in ((4, 3), (5, 2), (6, 1), (7, 0)):
        for i in batch:
            combine((head + i) % 8)
        for i in batch:
            if i:
                head_copy(i).start()
    own = pltpu.make_async_copy(stage.at[head], out_ref.at[head], own_sem)
    own.start()

    for which in range(2):
        wait_for((kvk, kvv)[which].at[seven], ring_send.at[which])
    for copy in query_sends:
        copy.wait_send()
    for index in range(4):
        wait_for(osend.at[pl.ds(*return_groups[index]), seven], o_send_sem.at[index])
    wait_for(ssend.at[:, seven], s_send_sem)
    wait_for(stage.at[seven], y_send_sem)
    own.wait()
    wait_for(out_ref.at[seven], y_recv_sem)


def shards(
    queries,
    prefix_keys,
    prefix_values,
    suffix_keys,
    suffix_values,
    new_keys,
    new_values,
    suffix_lengths,
    prefix_of_row,
    owner_of_prefix,
):
    bf16 = jnp.bfloat16
    by_step = jnp.transpose(queries, (0, 2, 1, 3))
    anywhere = pl.BlockSpec(memory_space=pltpu.HBM)
    dma = pltpu.SemaphoreType.DMA
    gathered = pl.pallas_call(
        kernel,
        out_shape=jax.ShapeDtypeStruct((8, 96, 128), bf16),
        in_specs=[anywhere] * 11,
        out_specs=anywhere,
        scratch_shapes=[
            pltpu.VMEM((1, 32), jnp.int32),
            pltpu.VMEM((1, 64), jnp.int32),
            pltpu.SMEM((1, 32), jnp.int32),
            pltpu.VMEM((24, 128), jnp.int32),
            pltpu.SMEM((24, 128), jnp.int32),
            pltpu.VMEM((8, 33, 3, 8, 128), bf16),
            pltpu.VMEM((768, 128), bf16),
            pltpu.VMEM((8, 512, 128), bf16),
            pltpu.VMEM((8, 512, 128), bf16),
            pltpu.VMEM((3072, 128), bf16),
            pltpu.VMEM((3072, 128), bf16),
            pltpu.VMEM((96, 128), bf16),
            pltpu.VMEM((96, 128), bf16),
            pltpu.VMEM((8, 8, 48, 128), bf16),
            pltpu.VMEM((8, 8, 48, 128), bf16),
            pltpu.VMEM((8, 8, 48, 128), bf16),
            pltpu.VMEM((8, 8, 1, 128), jnp.float32),
            pltpu.VMEM((8, 8, 1, 128), jnp.float32),
            pltpu.VMEM((768, 96), jnp.float32),
            pltpu.VMEM((768, 96), bf16),
            pltpu.VMEM((768, 128), jnp.float32),
            pltpu.VMEM((768, 1), jnp.float32),
            pltpu.VMEM((768, 1), jnp.float32),
            pltpu.VMEM((8, 384, 512), bf16),
            pltpu.VMEM((8, 384, 128), jnp.float32),
            pltpu.VMEM((8, 96, 128), bf16),
            dma((11,)),
            dma((2,)),
            dma((2, 4, 2)),
            dma((13,)),
            dma((13,)),
            dma,
            dma((4,)),
            dma((4,)),
            dma,
            dma,
            dma,
            dma,
            dma,
            pltpu.SemaphoreType.REGULAR((3,)),
            pltpu.SemaphoreType.REGULAR((2,)),
        ],
        compiler_params=pltpu.CompilerParams(
            collective_id=0, has_side_effects=True, vmem_limit_bytes=60 * 1024 * 1024
        ),
        cost_estimate=pl.CostEstimate(
            flops=1_200_000_000, bytes_accessed=3_000_000, transcendentals=1_800_000
        ),
        name="shared_prefix",
    )(
        prefix_of_row.reshape(1, 32),
        owner_of_prefix.reshape(1, 64),
        suffix_lengths.reshape(1, 32),
        by_step,
        by_step.reshape(768, 128),
        prefix_keys.reshape(512, 128),
        prefix_values.reshape(512, 128),
        suffix_keys.reshape(3072, 128),
        suffix_values.reshape(3072, 128),
        jnp.transpose(new_keys, (1, 2, 0, 3)).reshape(96, 128),
        jnp.transpose(new_values, (1, 2, 0, 3)).reshape(96, 128),
    )
    ordered = jnp.transpose(gathered.reshape(8, 4, 3, 8, 128), (1, 0, 3, 2, 4))
    return ordered.reshape(4, 64, 3, 128)


def solution(mesh):
    in_specs = (
        P("pre", "head", None, None),
        P("pre", None, "head", None),
        P("pre", None, "head", None),
        P("pre", None, "head", None),
        P("pre", None, "head", None),
        P("pre", None, "head", None),
        P("pre", None, "head", None),
        P("pre"),
        P("pre"),
        P(),
    )
    out_specs = P(("pre", "head"), None, None, None)
    return jax.shard_map(shards, mesh=mesh, in_specs=in_specs, out_specs=out_specs, check_vma=False)
```

```python
import math

import jax
import jax.numpy as jnp
from jax import lax
from jax.experimental import pallas as pl
from jax.experimental.pallas import tpu as pltpu
from jax.sharding import PartitionSpec as P

MESH = pl.DeviceIdType.MESH
masked_score = -1e30
offsets = (0, 1, 7, 2, 3, 6, 4, 5)
hops = (3, 4)
return_groups = ((0, 3), (3, 2), (5, 2), (7, 1))


def dot_t(a, b):
    return lax.dot_general(a, b, (((1,), (1,)), ((), ())), preferred_element_type=jnp.float32)


def kernel(
    prefix_hbm,
    owner_hbm,
    len_hbm,
    q4_hbm,
    q2_hbm,
    pk_hbm,
    pv_hbm,
    sk_hbm,
    sv_hbm,
    nk_hbm,
    nv_hbm,
    out_ref,
    prefix_here,
    owner_here,
    len_ref,
    index_rows,
    index_ref,
    qall,
    q2,
    kvk,
    kvv,
    sk,
    sv,
    nk,
    nv,
    qpack,
    osend,
    orecv,
    ssend,
    srecv,
    snew,
    pnew,
    lpart,
    lmax,
    lsum,
    weights,
    inverse,
    stage,
    load_sem,
    ring_send,
    ring_recv,
    q_send_sem,
    q_recv_sem,
    index_sem,
    o_send_sem,
    o_recv_sem,
    s_send_sem,
    s_recv_sem,
    y_send_sem,
    y_recv_sem,
    own_sem,
    above_here,
    below_here,
):
    pre = lax.axis_index("pre")
    head = lax.axis_index("head")
    z = pre // 8
    me = pre % 8
    plane = z * 8
    right = ((z + 1) % 8) * 8 + me
    left = ((z + 7) % 8) * 8 + me
    column, core = me // 2, me % 2
    ahead = ((column + 1) % 4) * 2 + core
    behind = ((column + 3) % 4) * 2 + core
    opposite = ((column + 2) % 4) * 2 + core
    sibling = column * 2 + 1 - core
    to_log2 = 128 ** (-0.5) * math.log2(math.e)

    barrier = pltpu.get_barrier_semaphore()

    def greet(pre_index, head_index):
        pl.semaphore_signal(
            barrier, inc=1, device_id=(pre_index, head_index), device_id_type=MESH
        )

    above, below = (head + 1) % 8, (head + 7) % 8
    for peer in (right, left, plane + ahead, plane + behind, plane + sibling):
        greet(peer, head)
    greet(pre, above)
    greet(pre, below)

    loads = [
        pltpu.make_async_copy(a, b, load_sem.at[i])
        for i, (a, b) in enumerate(
            (
                (prefix_hbm, prefix_here),
                (owner_hbm, owner_here),
                (len_hbm, len_ref),
                (q4_hbm, qall.at[me, pl.ds(1, 32)]),
                (q2_hbm, q2),
                (nk_hbm, nk),
                (nv_hbm, nv),
                (sk_hbm, sk),
                (sv_hbm, sv),
                (pk_hbm, kvk.at[0]),
                (pv_hbm, kvv.at[0]),
            )
        )
    ]
    for i in (0, 1, 3):
        loads[i].start()

    def ring(way, hop, which):
        held, own = ((kvk, pk_hbm), (kvv, pv_hbm))[which]
        if way == 0:
            source, target, device = (9 - hop) % 8, 8 - hop, right
        else:
            source, target, device = hop - 1, hop, left
        return pltpu.make_async_remote_copy(
            src_ref=own if hop == 1 else held.at[source],
            dst_ref=held.at[target],
            send_sem=ring_send.at[which],
            recv_sem=ring_recv.at[way, hop - 1, which],
            device_id=(device, head),
            device_id_type=MESH,
        )

    def plane_copy(source, target, blocks, send_sem, recv_sem, i):
        peer = (me + i) % 8
        return pltpu.make_async_remote_copy(
            src_ref=source.at[blocks, peer],
            dst_ref=target.at[blocks, me],
            send_sem=send_sem,
            recv_sem=recv_sem,
            device_id=(plane + peer, head),
            device_id_type=MESH,
        )

    def wait_for(block, sem):
        pltpu.make_async_copy(block, block, sem).wait()

    def query_copy(i, source, rows, peer):
        block = qall.at[source, rows]
        return pltpu.make_async_remote_copy(
            src_ref=block,
            dst_ref=block,
            send_sem=q_send_sem.at[i],
            recv_sem=q_recv_sem.at[i],
            device_id=(plane + peer, head),
            device_id_type=MESH,
        )

    every, first_half, second_half = pl.ds(0, 33), pl.ds(0, 17), pl.ds(17, 16)

    seven = pl.ds(0, 7)

    def part_copy(index, i):
        blocks = pl.ds(*return_groups[index])
        return plane_copy(osend, orecv, blocks, o_send_sem.at[index], o_recv_sem.at[index], i)

    def stat_copy(i):
        return plane_copy(ssend, srecv, pl.ds(0, 8), s_send_sem, s_recv_sem, i)

    pl.semaphore_wait(barrier, 7)
    for way in range(2):
        ring(way, 1, 0).start()
    for i in (4, 5, 2, 7, 8, 6, 9, 10):
        loads[i].start()

    def token(from_above, step):
        tokens, peer = (above_here, below) if from_above else (below_here, above)
        pl.semaphore_signal(
            tokens.at[step], inc=1, device_id=(pre, peer), device_id_type=MESH
        )

    token(True, 0)
    token(False, 0)

    query_sends = [
        query_copy(0, me, first_half, ahead),
        query_copy(1, me, first_half, behind),
        query_copy(2, me, second_half, ahead),
        query_copy(3, me, second_half, behind),
        query_copy(4, me, every, sibling),
        query_copy(5, behind, first_half, ahead),
        query_copy(6, ahead, second_half, behind),
        query_copy(7, behind, first_half, sibling),
        query_copy(8, ahead, first_half, sibling),
        query_copy(9, behind, second_half, sibling),
        query_copy(10, ahead, second_half, sibling),
        query_copy(11, opposite, first_half, sibling),
        query_copy(12, opposite, second_half, sibling),
    ]

    def hand_on(arrived, onward):
        query_sends[arrived].wait_recv()
        for i in onward:
            query_sends[i].start()

    loads[0].wait()
    qall[me, 0] = jnp.full((3, 8, 128), -1.0, jnp.bfloat16)
    qall[me, 0, 0, :, 0:32] = jnp.broadcast_to(prefix_here[...], (8, 32)).astype(jnp.bfloat16)
    loads[3].wait()
    for copy in query_sends[:5]:
        copy.start()

    loads[1].wait()

    def small_dot(a, b):
        return jnp.dot(
            a.astype(jnp.bfloat16), b.astype(jnp.bfloat16), preferred_element_type=jnp.float32
        )

    def iota(shape, dim):
        return lax.broadcasted_iota(jnp.int32, shape, dim)

    def ones_where(condition):
        return jnp.where(condition, 1.0, 0.0)

    def owner_at(k):
        offset = jnp.zeros_like(k)
        for place, value in enumerate(offsets):
            offset = jnp.where(k == place, value, offset)
        return ((z + offset) & 7) * 8

    def named_by(d):
        names = qall[d, 0, 0].astype(jnp.float32)[0:1]
        return ones_where(names == iota((64, 128), 0).astype(jnp.float32))

    before = ones_where(iota((128, 128), 0) < iota((128, 128), 1))
    place = iota((64, 64), 0)
    owners = owner_here[...]
    held = ones_where(owners == owner_at(place >> 3) + (place & 7))
    mine = small_dot(held, named_by(me))
    earlier = small_dot(mine, before)
    slots = small_dot(2 * iota((8, 64), 1).astype(jnp.float32), mine) + small_dot(
        jnp.ones((8, 64), jnp.float32), mine * earlier
    )
    index_rows[16:24, :] = slots.astype(jnp.int32)

    loads[4].wait()
    loads[5].wait()
    snew[...] = dot_t(q2[...], nk[...])
    loads[2].wait()
    loads[7].wait()
    loads[8].wait()

    def pair(i):
        rows = pl.ds(i * 48, 48)
        keys = pl.ds(i * 192, 192)
        scores = dot_t(q2[rows, :], sk[keys, :])
        row = lax.broadcasted_iota(jnp.int32, (48, 192), 0)
        lane = lax.broadcasted_iota(jnp.int32, (48, 192), 1)
        low = jnp.where(row < 24, 0, 96)
        high = jnp.where(row < 24, len_ref[0, 2 * i], 96 + len_ref[0, 2 * i + 1])
        scores = jnp.where((lane >= low) & (lane < high), scores, masked_score)
        row = lax.broadcasted_iota(jnp.int32, (48, 96), 0)
        lane = lax.broadcasted_iota(jnp.int32, (48, 96), 1)
        second = row >= 24
        place = lane - jnp.where(second, 2 * i + 1, 2 * i)
        within = jnp.where(second, row - 24, row)
        fresh_ok = (
            (place == 0)
            | ((place == 32) & (within >= 8))
            | ((place == 64) & (within >= 16))
        )
        fresh = jnp.where(fresh_ok, snew[rows, :], masked_score)
        top = jnp.maximum(
            jnp.max(scores, axis=1, keepdims=True), jnp.max(fresh, axis=1, keepdims=True)
        )
        scores = jnp.exp2((scores - top) * to_log2)
        fresh = jnp.exp2((fresh - top) * to_log2)
        lmax[rows, :] = top * to_log2
        lsum[rows, :] = jnp.sum(scores, axis=1, keepdims=True) + jnp.sum(
            fresh, axis=1, keepdims=True
        )
        pnew[rows, :] = fresh.astype(jnp.bfloat16)
        lpart[rows, :] = jnp.dot(
            scores.astype(jnp.bfloat16), sv[keys, :], preferred_element_type=jnp.float32
        )

    def pairs(first):
        for j in range(4):
            pair(first + j)

    def pass_on(way, hop, which):
        ring(way, hop, which).wait_recv()
        if hop < hops[way]:
            ring(way, hop + 1, which).start()

    pairs(0)
    for way in range(2):
        ring(way, 1, 1).start()
    pairs(4)
    hand_on(0, (5, 7))
    hand_on(1, (8,))
    pass_on(1, 1, 0)
    pass_on(0, 1, 0)
    pairs(8)
    hand_on(2, (9,))
    hand_on(3, (6, 10))
    pairs(12)
    loads[6].wait()
    part = lpart[...] + jnp.dot(pnew[...], nv[...], preferred_element_type=jnp.float32)
    lpart[...] = part / lsum[...]
    lmax[...] = lmax[...] + jnp.log2(lsum[...])

    def index_at(table, place, last):
        return jnp.minimum(jnp.maximum(index_ref[table * 8, place], 0), last)

    def weigh(k):
        for d in range(8):
            rows = [qall[d, 1 + index_at(rank, d * 8 + k, 31)] for rank in range(2)]
            both = [row.astype(jnp.float32).reshape(24, 128) for row in rows]
            qpack[k, d] = jnp.concatenate(both, axis=0).astype(jnp.bfloat16)
        scores = dot_t(qpack[k].reshape(384, 128), kvk[offsets[k]])
        top = jnp.max(scores, axis=1, keepdims=True)
        scores = jnp.exp2((scores - top) * to_log2)
        weights[k] = scores.astype(jnp.bfloat16)
        total = jnp.dot(
            weights[k], jnp.ones((512, 128), jnp.bfloat16), preferred_element_type=jnp.float32
        )
        inverse[k] = 1.0 / total
        level = top * to_log2 + jnp.log2(total)
        row = iota((48, 128), 0)
        lane = iota((48, 128), 1)
        for d in range(8):
            ssend[k, d] = jnp.sum(
                jnp.where(row == lane, level[d * 48 : d * 48 + 48], 0.0), axis=0, keepdims=True
            )
        srecv[k, me] = ssend[k, me]

    def blend(k):
        part = jnp.dot(weights[k], kvv[offsets[k]], preferred_element_type=jnp.float32)
        osend[k] = (part * inverse[k]).astype(jnp.bfloat16).reshape(8, 48, 128)
        orecv[k, me] = osend[k, me]

    def send_back(index):
        for i in range(1, 8):
            part_copy(index, i).start()

    hand_on(5, (11,))
    pass_on(1, 1, 1)
    pass_on(0, 1, 1)
    hand_on(6, (12,))
    for i in (4, 7, 8, 11):
        query_sends[i].wait_recv()
    here = ones_where(owners == owner_at(iota((8, 64), 0)) + me)
    match = jnp.concatenate(
        [small_dot(here, named_by(d)) for d in range(8)], axis=0
    )
    earlier = small_dot(match, before)
    numbers = iota((8, 128), 1).astype(jnp.bfloat16)
    for rank in range(2):
        chosen = jnp.where(earlier == rank, match, 0.0).astype(jnp.bfloat16)
        index_rows[rank * 8 : rank * 8 + 8, 0:64] = dot_t(numbers, chosen).astype(jnp.int32)
    index_copy = pltpu.make_async_copy(index_rows, index_ref, index_sem)
    index_copy.start()
    pass_on(1, 2, 0)
    for i in (9, 10, 12):
        query_sends[i].wait_recv()
    index_copy.wait()
    loads[9].wait()
    loads[10].wait()
    weigh(0)
    blend(0)
    weigh(1)
    weigh(2)
    pass_on(0, 2, 0)
    blend(1)
    blend(2)
    send_back(0)
    weigh(3)
    pass_on(1, 2, 1)
    blend(3)
    pl.semaphore_wait(above_here.at[0], 1)
    token(True, 1)
    pl.semaphore_wait(below_here.at[0], 1)
    token(False, 1)
    pass_on(1, 3, 0)
    weigh(4)
    pass_on(0, 2, 1)
    weigh(5)
    blend(5)
    pass_on(1, 3, 1)
    blend(4)
    send_back(1)
    pl.semaphore_wait(above_here.at[1], 1)
    token(True, 2)
    pl.semaphore_wait(below_here.at[1], 1)
    pass_on(1, 4, 0)
    weigh(6)
    pass_on(0, 3, 0)
    weigh(7)
    for i in range(1, 8):
        stat_copy(i).start()
    pass_on(1, 4, 1)
    blend(6)
    send_back(2)
    pass_on(0, 3, 1)
    blend(7)
    send_back(3)
    for index in range(4):
        wait_for(orecv.at[pl.ds(*return_groups[index]), seven], o_recv_sem.at[index])
    wait_for(srecv.at[:, seven], s_recv_sem)

    def head_copy(i):
        peer = (head + i) % 8
        return pltpu.make_async_remote_copy(
            src_ref=stage.at[peer],
            dst_ref=out_ref.at[head],
            send_sem=y_send_sem,
            recv_sem=y_recv_sem,
            device_id=(pre, peer),
            device_id_type=MESH,
        )

    def combine(target):
        parts = []
        levels = []
        row = lax.broadcasted_iota(jnp.int32, (24, 128), 0)
        lane = lax.broadcasted_iota(jnp.int32, (24, 128), 1)
        for j in range(4):
            slot = index_at(2, target * 4 + j, 127)
            which = slot % 2
            both = orecv[slot // 16, (slot // 2) % 8].astype(jnp.float32)
            stats = srecv[slot // 16, (slot // 2) % 8]
            parts.append(jnp.where(row * 0 + which == 0, both[:24], both[24:]))
            levels.append(
                jnp.sum(
                    jnp.where(lane == row + 24 * which, stats, 0.0), axis=1, keepdims=True
                )
            )
        parts = jnp.concatenate(parts, axis=0)
        levels = jnp.concatenate(levels, axis=0)
        rows = pl.ds(pl.multiple_of(target * 96, 96), 96)
        local = lmax[rows, :]
        top = jnp.maximum(levels, local)
        pre_factor = jnp.exp2(levels - top)
        local_factor = jnp.exp2(local - top)
        mixed = (parts * pre_factor + lpart[rows, :] * local_factor) / (
            pre_factor + local_factor
        )
        stage[target] = mixed.astype(jnp.bfloat16)

    pl.semaphore_wait(above_here.at[2], 1)
    for batch in ((4, 3), (5, 2), (6, 1), (7, 0)):
        for i in batch:
            combine((head + i) % 8)
        for i in batch:
            if i:
                head_copy(i).start()
    own = pltpu.make_async_copy(stage.at[head], out_ref.at[head], own_sem)
    own.start()

    for which in range(2):
        wait_for((kvk, kvv)[which].at[seven], ring_send.at[which])
    for copy in query_sends:
        copy.wait_send()
    for index in range(4):
        wait_for(osend.at[pl.ds(*return_groups[index]), seven], o_send_sem.at[index])
    wait_for(ssend.at[:, seven], s_send_sem)
    wait_for(stage.at[seven], y_send_sem)
    own.wait()
    wait_for(out_ref.at[seven], y_recv_sem)


def shards(
    queries,
    prefix_keys,
    prefix_values,
    suffix_keys,
    suffix_values,
    new_keys,
    new_values,
    suffix_lengths,
    prefix_of_row,
    owner_of_prefix,
):
    bf16 = jnp.bfloat16
    by_step = jnp.transpose(queries, (0, 2, 1, 3))
    anywhere = pl.BlockSpec(memory_space=pltpu.HBM)
    dma = pltpu.SemaphoreType.DMA
    gathered = pl.pallas_call(
        kernel,
        out_shape=jax.ShapeDtypeStruct((8, 96, 128), bf16),
        in_specs=[anywhere] * 11,
        out_specs=anywhere,
        scratch_shapes=[
            pltpu.VMEM((1, 32), jnp.int32),
            pltpu.VMEM((1, 64), jnp.int32),
            pltpu.SMEM((1, 32), jnp.int32),
            pltpu.VMEM((24, 128), jnp.int32),
            pltpu.SMEM((24, 128), jnp.int32),
            pltpu.VMEM((8, 33, 3, 8, 128), bf16),
            pltpu.VMEM((768, 128), bf16),
            pltpu.VMEM((8, 512, 128), bf16),
            pltpu.VMEM((8, 512, 128), bf16),
            pltpu.VMEM((3072, 128), bf16),
            pltpu.VMEM((3072, 128), bf16),
            pltpu.VMEM((96, 128), bf16),
            pltpu.VMEM((96, 128), bf16),
            pltpu.VMEM((8, 8, 48, 128), bf16),
            pltpu.VMEM((8, 8, 48, 128), bf16),
            pltpu.VMEM((8, 8, 48, 128), bf16),
            pltpu.VMEM((8, 8, 1, 128), jnp.float32),
            pltpu.VMEM((8, 8, 1, 128), jnp.float32),
            pltpu.VMEM((768, 96), jnp.float32),
            pltpu.VMEM((768, 96), bf16),
            pltpu.VMEM((768, 128), jnp.float32),
            pltpu.VMEM((768, 1), jnp.float32),
            pltpu.VMEM((768, 1), jnp.float32),
            pltpu.VMEM((8, 384, 512), bf16),
            pltpu.VMEM((8, 384, 128), jnp.float32),
            pltpu.VMEM((8, 96, 128), bf16),
            dma((11,)),
            dma((2,)),
            dma((2, 4, 2)),
            dma((13,)),
            dma((13,)),
            dma,
            dma((4,)),
            dma((4,)),
            dma,
            dma,
            dma,
            dma,
            dma,
            pltpu.SemaphoreType.REGULAR((3,)),
            pltpu.SemaphoreType.REGULAR((2,)),
        ],
        compiler_params=pltpu.CompilerParams(
            collective_id=0, has_side_effects=True, vmem_limit_bytes=60 * 1024 * 1024
        ),
        cost_estimate=pl.CostEstimate(
            flops=1_200_000_000, bytes_accessed=3_000_000, transcendentals=1_800_000
        ),
        name="shared_prefix",
    )(
        prefix_of_row.reshape(1, 32),
        owner_of_prefix.reshape(1, 64),
        suffix_lengths.reshape(1, 32),
        by_step,
        by_step.reshape(768, 128),
        prefix_keys.reshape(512, 128),
        prefix_values.reshape(512, 128),
        suffix_keys.reshape(3072, 128),
        suffix_values.reshape(3072, 128),
        jnp.transpose(new_keys, (1, 2, 0, 3)).reshape(96, 128),
        jnp.transpose(new_values, (1, 2, 0, 3)).reshape(96, 128),
    )
    ordered = jnp.transpose(gathered.reshape(8, 4, 3, 8, 128), (1, 0, 3, 2, 4))
    return ordered.reshape(4, 64, 3, 128)


def solution(mesh):
    in_specs = (
        P("pre", "head", None, None),
        P("pre", None, "head", None),
        P("pre", None, "head", None),
        P("pre", None, "head", None),
        P("pre", None, "head", None),
        P("pre", None, "head", None),
        P("pre", None, "head", None),
        P("pre"),
        P("pre"),
        P(),
    )
    out_specs = P(("pre", "head"), None, None, None)
    return jax.shard_map(shards, mesh=mesh, in_specs=in_specs, out_specs=out_specs, check_vma=False)
```

```python
import math

import jax
import jax.numpy as jnp
from jax import lax
from jax.experimental import pallas as pl
from jax.experimental.pallas import tpu as pltpu
from jax.sharding import PartitionSpec as P

MESH = pl.DeviceIdType.MESH
masked_score = -1e30
offsets = (0, 1, 7, 2, 6, 3, 5, 4)
return_groups = ((0, 3), (3, 2), (5, 2), (7, 1))


def dot_t(a, b):
    return lax.dot_general(a, b, (((1,), (1,)), ((), ())), preferred_element_type=jnp.float32)


def kernel(
    prefix_hbm,
    owner_hbm,
    len_hbm,
    q4_hbm,
    q2_hbm,
    pk_hbm,
    pv_hbm,
    sk_hbm,
    sv_hbm,
    nk_hbm,
    nv_hbm,
    out_ref,
    prefix_here,
    owner_here,
    len_ref,
    index_rows,
    index_ref,
    qall,
    q2,
    kvk,
    kvv,
    sk,
    sv,
    nk,
    nv,
    qpack,
    osend,
    orecv,
    ssend,
    srecv,
    snew,
    pnew,
    lpart,
    lmax,
    lsum,
    weights,
    inverse,
    stage,
    load_sem,
    ring_send,
    ring_recv,
    q_send_sem,
    q_recv_sem,
    index_sem,
    o_send_sem,
    o_recv_sem,
    s_send_sem,
    s_recv_sem,
    y_send_sem,
    y_recv_sem,
    own_sem,
    above_here,
    below_here,
):
    pre = lax.axis_index("pre")
    head = lax.axis_index("head")
    z = pre // 8
    me = pre % 8
    plane = z * 8
    right = ((z + 1) % 8) * 8 + me
    left = ((z + 7) % 8) * 8 + me
    column, core = me // 2, me % 2
    ahead = ((column + 1) % 4) * 2 + core
    behind = ((column + 3) % 4) * 2 + core
    opposite = ((column + 2) % 4) * 2 + core
    sibling = column * 2 + 1 - core
    to_log2 = 128 ** (-0.5) * math.log2(math.e)

    barrier = pltpu.get_barrier_semaphore()

    def greet(pre_index, head_index):
        pl.semaphore_signal(
            barrier, inc=1, device_id=(pre_index, head_index), device_id_type=MESH
        )

    above, below = (head + 1) % 8, (head + 7) % 8
    for peer in (right, left, plane + ahead, plane + behind, plane + sibling):
        greet(peer, head)
    greet(pre, above)
    greet(pre, below)

    loads = [
        pltpu.make_async_copy(a, b, load_sem.at[i])
        for i, (a, b) in enumerate(
            (
                (prefix_hbm, prefix_here),
                (owner_hbm, owner_here),
                (len_hbm, len_ref),
                (q4_hbm, qall.at[me, pl.ds(1, 32)]),
                (q2_hbm, q2),
                (nk_hbm, nk),
                (nv_hbm, nv),
                (sk_hbm, sk),
                (sv_hbm, sv),
                (pk_hbm, kvk.at[0]),
                (pv_hbm, kvv.at[0]),
            )
        )
    ]
    for i in (0, 1, 3):
        loads[i].start()

    def ring(way, hop, which):
        held, own = ((kvk, pk_hbm), (kvv, pv_hbm))[which]
        if way == 0:
            source, target, device = (9 - hop) % 8, 8 - hop, right
        else:
            source, target, device = hop - 1, hop, left
        return pltpu.make_async_remote_copy(
            src_ref=own if hop == 1 else held.at[source],
            dst_ref=held.at[target],
            send_sem=ring_send.at[which],
            recv_sem=ring_recv.at[way, hop - 1, which],
            device_id=(device, head),
            device_id_type=MESH,
        )

    def plane_copy(source, target, blocks, send_sem, recv_sem, i):
        peer = (me + i) % 8
        return pltpu.make_async_remote_copy(
            src_ref=source.at[blocks, peer],
            dst_ref=target.at[blocks, me],
            send_sem=send_sem,
            recv_sem=recv_sem,
            device_id=(plane + peer, head),
            device_id_type=MESH,
        )

    def wait_for(block, sem):
        pltpu.make_async_copy(block, block, sem).wait()

    def query_copy(i, source, rows, peer):
        block = qall.at[source, rows]
        return pltpu.make_async_remote_copy(
            src_ref=block,
            dst_ref=block,
            send_sem=q_send_sem.at[i],
            recv_sem=q_recv_sem.at[i],
            device_id=(plane + peer, head),
            device_id_type=MESH,
        )

    every, first_half, second_half = pl.ds(0, 33), pl.ds(0, 17), pl.ds(17, 16)

    seven = pl.ds(0, 7)

    def part_copy(index, i):
        blocks = pl.ds(*return_groups[index])
        return plane_copy(osend, orecv, blocks, o_send_sem.at[index], o_recv_sem.at[index], i)

    def stat_copy(i):
        return plane_copy(ssend, srecv, pl.ds(0, 8), s_send_sem, s_recv_sem, i)

    pl.semaphore_wait(barrier, 7)
    for way in range(2):
        ring(way, 1, 0).start()
    for i in (4, 5, 2, 7, 8, 6, 9, 10):
        loads[i].start()

    def token(from_above, step):
        tokens, peer = (above_here, below) if from_above else (below_here, above)
        pl.semaphore_signal(
            tokens.at[step], inc=1, device_id=(pre, peer), device_id_type=MESH
        )

    token(True, 0)
    token(False, 0)

    query_sends = [
        query_copy(0, me, first_half, ahead),
        query_copy(1, me, first_half, behind),
        query_copy(2, me, second_half, ahead),
        query_copy(3, me, second_half, behind),
        query_copy(4, me, every, sibling),
        query_copy(5, behind, first_half, ahead),
        query_copy(6, ahead, second_half, behind),
        query_copy(7, behind, first_half, sibling),
        query_copy(8, ahead, first_half, sibling),
        query_copy(9, behind, second_half, sibling),
        query_copy(10, ahead, second_half, sibling),
        query_copy(11, opposite, first_half, sibling),
        query_copy(12, opposite, second_half, sibling),
    ]

    def hand_on(arrived, onward):
        query_sends[arrived].wait_recv()
        for i in onward:
            query_sends[i].start()

    loads[0].wait()
    qall[me, 0] = jnp.full((3, 8, 128), -1.0, jnp.bfloat16)
    qall[me, 0, 0, :, 0:32] = jnp.broadcast_to(prefix_here[...], (8, 32)).astype(jnp.bfloat16)
    loads[3].wait()
    for copy in query_sends[:5]:
        copy.start()

    loads[1].wait()

    def small_dot(a, b):
        return jnp.dot(
            a.astype(jnp.bfloat16), b.astype(jnp.bfloat16), preferred_element_type=jnp.float32
        )

    def iota(shape, dim):
        return lax.broadcasted_iota(jnp.int32, shape, dim)

    def ones_where(condition):
        return jnp.where(condition, 1.0, 0.0)

    def owner_at(k):
        offset = jnp.zeros_like(k)
        for place, value in enumerate(offsets):
            offset = jnp.where(k == place, value, offset)
        return ((z + offset) & 7) * 8

    def named_by(d):
        names = qall[d, 0, 0].astype(jnp.float32)[0:1]
        return ones_where(names == iota((64, 128), 0).astype(jnp.float32))

    before = ones_where(iota((128, 128), 0) < iota((128, 128), 1))
    place = iota((64, 64), 0)
    owners = owner_here[...]
    held = ones_where(owners == owner_at(place >> 3) + (place & 7))
    mine = small_dot(held, named_by(me))
    earlier = small_dot(mine, before)
    slots = small_dot(2 * iota((8, 64), 1).astype(jnp.float32), mine) + small_dot(
        jnp.ones((8, 64), jnp.float32), mine * earlier
    )
    index_rows[16:24, :] = slots.astype(jnp.int32)

    for way in range(2):
        ring(way, 1, 1).start()

    loads[4].wait()
    loads[5].wait()
    snew[...] = dot_t(q2[...], nk[...])
    loads[2].wait()
    loads[7].wait()
    loads[8].wait()

    def pair(i):
        rows = pl.ds(i * 48, 48)
        keys = pl.ds(i * 192, 192)
        scores = dot_t(q2[rows, :], sk[keys, :])
        row = lax.broadcasted_iota(jnp.int32, (48, 192), 0)
        lane = lax.broadcasted_iota(jnp.int32, (48, 192), 1)
        low = jnp.where(row < 24, 0, 96)
        high = jnp.where(row < 24, len_ref[0, 2 * i], 96 + len_ref[0, 2 * i + 1])
        scores = jnp.where((lane >= low) & (lane < high), scores, masked_score)
        row = lax.broadcasted_iota(jnp.int32, (48, 96), 0)
        lane = lax.broadcasted_iota(jnp.int32, (48, 96), 1)
        second = row >= 24
        place = lane - jnp.where(second, 2 * i + 1, 2 * i)
        within = jnp.where(second, row - 24, row)
        fresh_ok = (
            (place == 0)
            | ((place == 32) & (within >= 8))
            | ((place == 64) & (within >= 16))
        )
        fresh = jnp.where(fresh_ok, snew[rows, :], masked_score)
        top = jnp.maximum(
            jnp.max(scores, axis=1, keepdims=True), jnp.max(fresh, axis=1, keepdims=True)
        )
        scores = jnp.exp2((scores - top) * to_log2)
        fresh = jnp.exp2((fresh - top) * to_log2)
        lmax[rows, :] = top * to_log2
        lsum[rows, :] = jnp.sum(scores, axis=1, keepdims=True) + jnp.sum(
            fresh, axis=1, keepdims=True
        )
        pnew[rows, :] = fresh.astype(jnp.bfloat16)
        lpart[rows, :] = jnp.dot(
            scores.astype(jnp.bfloat16), sv[keys, :], preferred_element_type=jnp.float32
        )

    def pairs(first):
        for j in range(4):
            pair(first + j)

    def pass_on(hop, which):
        for way in range(2):
            ring(way, hop, which).wait_recv()
            if hop < 3 or which == way:
                ring(way, hop + 1, which).start()

    pairs(0)
    pairs(4)
    pass_on(1, 0)
    hand_on(0, (5, 7))
    hand_on(1, (8,))
    pairs(8)
    hand_on(2, (9,))
    hand_on(3, (6, 10))
    pass_on(1, 1)
    pairs(12)
    loads[6].wait()
    part = lpart[...] + jnp.dot(pnew[...], nv[...], preferred_element_type=jnp.float32)
    lpart[...] = part / lsum[...]
    lmax[...] = lmax[...] + jnp.log2(lsum[...])

    def index_at(table, place, last):
        return jnp.minimum(jnp.maximum(index_ref[table * 8, place], 0), last)

    def weigh(k):
        for d in range(8):
            rows = [qall[d, 1 + index_at(rank, d * 8 + k, 31)] for rank in range(2)]
            both = [row.astype(jnp.float32).reshape(24, 128) for row in rows]
            qpack[k, d] = jnp.concatenate(both, axis=0).astype(jnp.bfloat16)
        scores = dot_t(qpack[k].reshape(384, 128), kvk[offsets[k]])
        top = jnp.max(scores, axis=1, keepdims=True)
        scores = jnp.exp2((scores - top) * to_log2)
        weights[k] = scores.astype(jnp.bfloat16)
        total = jnp.dot(
            weights[k], jnp.ones((512, 128), jnp.bfloat16), preferred_element_type=jnp.float32
        )
        inverse[k] = 1.0 / total
        level = top * to_log2 + jnp.log2(total)
        row = iota((48, 128), 0)
        lane = iota((48, 128), 1)
        for d in range(8):
            ssend[k, d] = jnp.sum(
                jnp.where(row == lane, level[d * 48 : d * 48 + 48], 0.0), axis=0, keepdims=True
            )
        srecv[k, me] = ssend[k, me]

    def blend(k):
        part = jnp.dot(weights[k], kvv[offsets[k]], preferred_element_type=jnp.float32)
        osend[k] = (part * inverse[k]).astype(jnp.bfloat16).reshape(8, 48, 128)
        orecv[k, me] = osend[k, me]

    def send_back(index):
        for i in range(1, 8):
            part_copy(index, i).start()

    hand_on(5, (11,))
    hand_on(6, (12,))
    pass_on(2, 0)
    for i in (4, 7, 8, 11):
        query_sends[i].wait_recv()
    here = ones_where(owners == owner_at(iota((8, 64), 0)) + me)
    match = jnp.concatenate(
        [small_dot(here, named_by(d)) for d in range(8)], axis=0
    )
    earlier = small_dot(match, before)
    numbers = iota((8, 128), 1).astype(jnp.bfloat16)
    for rank in range(2):
        chosen = jnp.where(earlier == rank, match, 0.0).astype(jnp.bfloat16)
        index_rows[rank * 8 : rank * 8 + 8, 0:64] = dot_t(numbers, chosen).astype(jnp.int32)
    index_copy = pltpu.make_async_copy(index_rows, index_ref, index_sem)
    index_copy.start()
    for i in (9, 10, 12):
        query_sends[i].wait_recv()
    index_copy.wait()
    loads[9].wait()
    loads[10].wait()
    weigh(0)
    blend(0)
    pass_on(2, 1)
    weigh(1)
    blend(1)
    weigh(2)
    blend(2)
    send_back(0)
    pass_on(3, 0)
    pl.semaphore_wait(above_here.at[0], 1)
    token(True, 1)
    pl.semaphore_wait(below_here.at[0], 1)
    token(False, 1)
    weigh(3)
    weigh(4)
    blend(3)
    blend(4)
    send_back(1)
    pass_on(3, 1)
    pl.semaphore_wait(above_here.at[1], 1)
    token(True, 2)
    pl.semaphore_wait(below_here.at[1], 1)
    weigh(5)
    weigh(6)
    blend(5)
    blend(6)
    send_back(2)
    ring(0, 4, 0).wait_recv()
    weigh(7)
    for i in range(1, 8):
        stat_copy(i).start()
    ring(1, 4, 1).wait_recv()
    blend(7)
    send_back(3)
    for index in range(4):
        wait_for(orecv.at[pl.ds(*return_groups[index]), seven], o_recv_sem.at[index])
    wait_for(srecv.at[:, seven], s_recv_sem)

    def head_copy(i):
        peer = (head + i) % 8
        return pltpu.make_async_remote_copy(
            src_ref=stage.at[peer],
            dst_ref=out_ref.at[head],
            send_sem=y_send_sem,
            recv_sem=y_recv_sem,
            device_id=(pre, peer),
            device_id_type=MESH,
        )

    def combine(target):
        parts = []
        levels = []
        row = lax.broadcasted_iota(jnp.int32, (24, 128), 0)
        lane = lax.broadcasted_iota(jnp.int32, (24, 128), 1)
        for j in range(4):
            slot = index_at(2, target * 4 + j, 127)
            which = slot % 2
            both = orecv[slot // 16, (slot // 2) % 8].astype(jnp.float32)
            stats = srecv[slot // 16, (slot // 2) % 8]
            parts.append(jnp.where(row * 0 + which == 0, both[:24], both[24:]))
            levels.append(
                jnp.sum(
                    jnp.where(lane == row + 24 * which, stats, 0.0), axis=1, keepdims=True
                )
            )
        parts = jnp.concatenate(parts, axis=0)
        levels = jnp.concatenate(levels, axis=0)
        rows = pl.ds(pl.multiple_of(target * 96, 96), 96)
        local = lmax[rows, :]
        top = jnp.maximum(levels, local)
        pre_factor = jnp.exp2(levels - top)
        local_factor = jnp.exp2(local - top)
        mixed = (parts * pre_factor + lpart[rows, :] * local_factor) / (
            pre_factor + local_factor
        )
        stage[target] = mixed.astype(jnp.bfloat16)

    pl.semaphore_wait(above_here.at[2], 1)
    for batch in ((4, 3), (5, 2), (6, 1), (7, 0)):
        for i in batch:
            combine((head + i) % 8)
        for i in batch:
            if i:
                head_copy(i).start()
    own = pltpu.make_async_copy(stage.at[head], out_ref.at[head], own_sem)
    own.start()

    for which in range(2):
        wait_for((kvk, kvv)[which].at[seven], ring_send.at[which])
    for copy in query_sends:
        copy.wait_send()
    for index in range(4):
        wait_for(osend.at[pl.ds(*return_groups[index]), seven], o_send_sem.at[index])
    wait_for(ssend.at[:, seven], s_send_sem)
    wait_for(stage.at[seven], y_send_sem)
    own.wait()
    wait_for(out_ref.at[seven], y_recv_sem)


def shards(
    queries,
    prefix_keys,
    prefix_values,
    suffix_keys,
    suffix_values,
    new_keys,
    new_values,
    suffix_lengths,
    prefix_of_row,
    owner_of_prefix,
):
    bf16 = jnp.bfloat16
    by_step = jnp.transpose(queries, (0, 2, 1, 3))
    anywhere = pl.BlockSpec(memory_space=pltpu.HBM)
    dma = pltpu.SemaphoreType.DMA
    gathered = pl.pallas_call(
        kernel,
        out_shape=jax.ShapeDtypeStruct((8, 96, 128), bf16),
        in_specs=[anywhere] * 11,
        out_specs=anywhere,
        scratch_shapes=[
            pltpu.VMEM((1, 32), jnp.int32),
            pltpu.VMEM((1, 64), jnp.int32),
            pltpu.SMEM((1, 32), jnp.int32),
            pltpu.VMEM((24, 128), jnp.int32),
            pltpu.SMEM((24, 128), jnp.int32),
            pltpu.VMEM((8, 33, 3, 8, 128), bf16),
            pltpu.VMEM((768, 128), bf16),
            pltpu.VMEM((8, 512, 128), bf16),
            pltpu.VMEM((8, 512, 128), bf16),
            pltpu.VMEM((3072, 128), bf16),
            pltpu.VMEM((3072, 128), bf16),
            pltpu.VMEM((96, 128), bf16),
            pltpu.VMEM((96, 128), bf16),
            pltpu.VMEM((8, 8, 48, 128), bf16),
            pltpu.VMEM((8, 8, 48, 128), bf16),
            pltpu.VMEM((8, 8, 48, 128), bf16),
            pltpu.VMEM((8, 8, 1, 128), jnp.float32),
            pltpu.VMEM((8, 8, 1, 128), jnp.float32),
            pltpu.VMEM((768, 96), jnp.float32),
            pltpu.VMEM((768, 96), bf16),
            pltpu.VMEM((768, 128), jnp.float32),
            pltpu.VMEM((768, 1), jnp.float32),
            pltpu.VMEM((768, 1), jnp.float32),
            pltpu.VMEM((8, 384, 512), bf16),
            pltpu.VMEM((8, 384, 128), jnp.float32),
            pltpu.VMEM((8, 96, 128), bf16),
            dma((11,)),
            dma((2,)),
            dma((2, 4, 2)),
            dma((13,)),
            dma((13,)),
            dma,
            dma((4,)),
            dma((4,)),
            dma,
            dma,
            dma,
            dma,
            dma,
            pltpu.SemaphoreType.REGULAR((3,)),
            pltpu.SemaphoreType.REGULAR((2,)),
        ],
        compiler_params=pltpu.CompilerParams(
            collective_id=0, has_side_effects=True, vmem_limit_bytes=60 * 1024 * 1024
        ),
        cost_estimate=pl.CostEstimate(
            flops=1_200_000_000, bytes_accessed=3_000_000, transcendentals=1_800_000
        ),
        name="shared_prefix",
    )(
        prefix_of_row.reshape(1, 32),
        owner_of_prefix.reshape(1, 64),
        suffix_lengths.reshape(1, 32),
        by_step,
        by_step.reshape(768, 128),
        prefix_keys.reshape(512, 128),
        prefix_values.reshape(512, 128),
        suffix_keys.reshape(3072, 128),
        suffix_values.reshape(3072, 128),
        jnp.transpose(new_keys, (1, 2, 0, 3)).reshape(96, 128),
        jnp.transpose(new_values, (1, 2, 0, 3)).reshape(96, 128),
    )
    ordered = jnp.transpose(gathered.reshape(8, 4, 3, 8, 128), (1, 0, 3, 2, 4))
    return ordered.reshape(4, 64, 3, 128)


def solution(mesh):
    in_specs = (
        P("pre", "head", None, None),
        P("pre", None, "head", None),
        P("pre", None, "head", None),
        P("pre", None, "head", None),
        P("pre", None, "head", None),
        P("pre", None, "head", None),
        P("pre", None, "head", None),
        P("pre"),
        P("pre"),
        P(),
    )
    out_specs = P(("pre", "head"), None, None, None)
    return jax.shard_map(shards, mesh=mesh, in_specs=in_specs, out_specs=out_specs, check_vma=False)
```

```python
import math

import jax
import jax.numpy as jnp
from jax import lax
from jax.experimental import pallas as pl
from jax.experimental.pallas import tpu as pltpu
from jax.sharding import PartitionSpec as P

MESH = pl.DeviceIdType.MESH
masked_score = -1e30
offsets = (0, 1, 7, 2, 6, 3, 5, 4)
return_groups = ((0, 3), (3, 2), (5, 2), (7, 1))


def dot_t(a, b):
    return lax.dot_general(a, b, (((1,), (1,)), ((), ())), preferred_element_type=jnp.float32)


def kernel(
    prefix_hbm,
    owner_hbm,
    len_hbm,
    q4_hbm,
    q2_hbm,
    pk_hbm,
    pv_hbm,
    sk_hbm,
    sv_hbm,
    nk_hbm,
    nv_hbm,
    out_ref,
    prefix_here,
    owner_here,
    len_ref,
    index_rows,
    index_ref,
    qall,
    q2,
    kvk,
    kvv,
    sk,
    sv,
    nk,
    nv,
    qpack,
    osend,
    orecv,
    ssend,
    srecv,
    snew,
    pnew,
    lpart,
    lmax,
    share,
    lsum,
    weights,
    inverse,
    stage,
    load_sem,
    ring_send,
    ring_recv,
    q_send_sem,
    q_recv_sem,
    index_sem,
    o_send_sem,
    o_recv_sem,
    s_send_sem,
    s_recv_sem,
    y_send_sem,
    y_recv_sem,
    own_sem,
    above_here,
    below_here,
):
    pre = lax.axis_index("pre")
    head = lax.axis_index("head")
    z = pre // 8
    me = pre % 8
    plane = z * 8
    right = ((z + 1) % 8) * 8 + me
    left = ((z + 7) % 8) * 8 + me
    column, core = me // 2, me % 2
    ahead = ((column + 1) % 4) * 2 + core
    behind = ((column + 3) % 4) * 2 + core
    opposite = ((column + 2) % 4) * 2 + core
    sibling = column * 2 + 1 - core
    to_log2 = 128 ** (-0.5) * math.log2(math.e)

    barrier = pltpu.get_barrier_semaphore()

    def greet(pre_index, head_index):
        pl.semaphore_signal(
            barrier, inc=1, device_id=(pre_index, head_index), device_id_type=MESH
        )

    above, below = (head + 1) % 8, (head + 7) % 8
    for peer in (right, left, plane + ahead, plane + behind, plane + sibling):
        greet(peer, head)
    greet(pre, above)
    greet(pre, below)

    loads = [
        pltpu.make_async_copy(a, b, load_sem.at[i])
        for i, (a, b) in enumerate(
            (
                (prefix_hbm, prefix_here),
                (owner_hbm, owner_here),
                (len_hbm, len_ref),
                (q4_hbm, qall.at[me, pl.ds(1, 32)]),
                (q2_hbm, q2),
                (nk_hbm, nk),
                (nv_hbm, nv),
                (sk_hbm, sk),
                (sv_hbm, sv),
                (pk_hbm, kvk.at[0]),
                (pv_hbm, kvv.at[0]),
            )
        )
    ]
    for i in (0, 1, 3):
        loads[i].start()

    def ring(way, hop, which):
        held, own = ((kvk, pk_hbm), (kvv, pv_hbm))[which]
        if way == 0:
            source, target, device = (9 - hop) % 8, 8 - hop, right
        else:
            source, target, device = hop - 1, hop, left
        return pltpu.make_async_remote_copy(
            src_ref=own if hop == 1 else held.at[source],
            dst_ref=held.at[target],
            send_sem=ring_send.at[which],
            recv_sem=ring_recv.at[way, hop - 1, which],
            device_id=(device, head),
            device_id_type=MESH,
        )

    def plane_copy(source, target, blocks, send_sem, recv_sem, i):
        peer = (me + i) % 8
        return pltpu.make_async_remote_copy(
            src_ref=source.at[blocks, peer],
            dst_ref=target.at[blocks, me],
            send_sem=send_sem,
            recv_sem=recv_sem,
            device_id=(plane + peer, head),
            device_id_type=MESH,
        )

    def wait_for(block, sem):
        pltpu.make_async_copy(block, block, sem).wait()

    def query_copy(i, source, rows, peer):
        block = qall.at[source, rows]
        return pltpu.make_async_remote_copy(
            src_ref=block,
            dst_ref=block,
            send_sem=q_send_sem.at[i],
            recv_sem=q_recv_sem.at[i],
            device_id=(plane + peer, head),
            device_id_type=MESH,
        )

    every, first_half, second_half = pl.ds(0, 33), pl.ds(0, 17), pl.ds(17, 16)

    seven = pl.ds(0, 7)

    def part_copy(index, i):
        blocks = pl.ds(*return_groups[index])
        return plane_copy(osend, orecv, blocks, o_send_sem.at[index], o_recv_sem.at[index], i)

    def stat_copy(i):
        return plane_copy(ssend, srecv, pl.ds(0, 8), s_send_sem, s_recv_sem, i)

    pl.semaphore_wait(barrier, 7)
    for way in range(2):
        ring(way, 1, 0).start()
    for i in (4, 5, 2, 7, 8, 6, 9, 10):
        loads[i].start()

    def token(from_above, step):
        tokens, peer = (above_here, below) if from_above else (below_here, above)
        pl.semaphore_signal(
            tokens.at[step], inc=1, device_id=(pre, peer), device_id_type=MESH
        )

    token(True, 0)
    token(False, 0)

    query_sends = [
        query_copy(0, me, first_half, ahead),
        query_copy(1, me, first_half, behind),
        query_copy(2, me, second_half, ahead),
        query_copy(3, me, second_half, behind),
        query_copy(4, me, every, sibling),
        query_copy(5, behind, first_half, ahead),
        query_copy(6, ahead, second_half, behind),
        query_copy(7, behind, first_half, sibling),
        query_copy(8, ahead, first_half, sibling),
        query_copy(9, behind, second_half, sibling),
        query_copy(10, ahead, second_half, sibling),
        query_copy(11, opposite, first_half, sibling),
        query_copy(12, opposite, second_half, sibling),
    ]

    def hand_on(arrived, onward):
        query_sends[arrived].wait_recv()
        for i in onward:
            query_sends[i].start()

    loads[0].wait()
    qall[me, 0] = jnp.full((3, 8, 128), -1.0, jnp.bfloat16)
    qall[me, 0, 0, :, 0:32] = jnp.broadcast_to(prefix_here[...], (8, 32)).astype(jnp.bfloat16)
    loads[3].wait()
    for copy in query_sends[:5]:
        copy.start()

    loads[1].wait()

    def small_dot(a, b):
        return jnp.dot(
            a.astype(jnp.bfloat16), b.astype(jnp.bfloat16), preferred_element_type=jnp.float32
        )

    def iota(shape, dim):
        return lax.broadcasted_iota(jnp.int32, shape, dim)

    def ones_where(condition):
        return jnp.where(condition, 1.0, 0.0)

    def owner_at(k):
        offset = jnp.zeros_like(k)
        for place, value in enumerate(offsets):
            offset = jnp.where(k == place, value, offset)
        return ((z + offset) & 7) * 8

    def named_by(d):
        names = qall[d, 0, 0].astype(jnp.float32)[0:1]
        return ones_where(names == iota((64, 128), 0).astype(jnp.float32))

    before = ones_where(iota((128, 128), 0) < iota((128, 128), 1))
    place = iota((64, 64), 0)
    owners = owner_here[...]
    held = ones_where(owners == owner_at(place >> 3) + (place & 7))
    mine = small_dot(held, named_by(me))
    earlier = small_dot(mine, before)
    slots = small_dot(2 * iota((8, 64), 1).astype(jnp.float32), mine) + small_dot(
        jnp.ones((8, 64), jnp.float32), mine * earlier
    )
    index_rows[16:24, :] = slots.astype(jnp.int32)

    for way in range(2):
        ring(way, 1, 1).start()

    loads[4].wait()
    loads[5].wait()
    snew[...] = dot_t(q2[...], nk[...])
    loads[2].wait()
    loads[7].wait()
    loads[8].wait()

    def pair(i):
        rows = pl.ds(i * 48, 48)
        keys = pl.ds(i * 192, 192)
        scores = dot_t(q2[rows, :], sk[keys, :])
        row = lax.broadcasted_iota(jnp.int32, (48, 192), 0)
        lane = lax.broadcasted_iota(jnp.int32, (48, 192), 1)
        low = jnp.where(row < 24, 0, 96)
        high = jnp.where(row < 24, len_ref[0, 2 * i], 96 + len_ref[0, 2 * i + 1])
        scores = jnp.where((lane >= low) & (lane < high), scores, masked_score)
        row = lax.broadcasted_iota(jnp.int32, (48, 96), 0)
        lane = lax.broadcasted_iota(jnp.int32, (48, 96), 1)
        second = row >= 24
        place = lane - jnp.where(second, 2 * i + 1, 2 * i)
        within = jnp.where(second, row - 24, row)
        fresh_ok = (
            (place == 0)
            | ((place == 32) & (within >= 8))
            | ((place == 64) & (within >= 16))
        )
        fresh = jnp.where(fresh_ok, snew[rows, :], masked_score)
        top = jnp.maximum(
            jnp.max(scores, axis=1, keepdims=True), jnp.max(fresh, axis=1, keepdims=True)
        )
        scores = jnp.exp2((scores - top) * to_log2)
        fresh = jnp.exp2((fresh - top) * to_log2)
        lmax[rows, :] = top * to_log2
        lsum[rows, :] = jnp.sum(scores, axis=1, keepdims=True) + jnp.sum(
            fresh, axis=1, keepdims=True
        )
        pnew[rows, :] = fresh.astype(jnp.bfloat16)
        lpart[rows, :] = jnp.dot(
            scores.astype(jnp.bfloat16), sv[keys, :], preferred_element_type=jnp.float32
        )

    def pairs(first):
        for j in range(4):
            pair(first + j)

    def pass_on(hop, which):
        for way in range(2):
            ring(way, hop, which).wait_recv()
            if hop < 3 or which == way:
                ring(way, hop + 1, which).start()

    pairs(0)
    pairs(4)
    pass_on(1, 0)
    hand_on(0, (5, 7))
    hand_on(1, (8,))
    pairs(8)
    hand_on(2, (9,))
    hand_on(3, (6, 10))
    pass_on(1, 1)
    pairs(12)
    loads[6].wait()
    part = lpart[...] + jnp.dot(pnew[...], nv[...], preferred_element_type=jnp.float32)
    lpart[...] = part / lsum[...]
    lmax[...] = lmax[...] + jnp.log2(lsum[...])

    def index_at(table, place, last):
        return jnp.minimum(jnp.maximum(index_ref[table * 8, place], 0), last)

    def weigh(k):
        for d in range(8):
            rows = [qall[d, 1 + index_at(rank, d * 8 + k, 31)] for rank in range(2)]
            both = [row.astype(jnp.float32).reshape(24, 128) for row in rows]
            qpack[k, d] = jnp.concatenate(both, axis=0).astype(jnp.bfloat16)
        scores = dot_t(qpack[k].reshape(384, 128), kvk[offsets[k]])
        top = jnp.max(scores, axis=1, keepdims=True)
        scores = jnp.exp2((scores - top) * to_log2)
        weights[k] = scores.astype(jnp.bfloat16)
        total = jnp.dot(
            weights[k], jnp.ones((512, 128), jnp.bfloat16), preferred_element_type=jnp.float32
        )
        inverse[k] = 1.0 / total
        level = top * to_log2 + jnp.log2(total)
        row = iota((48, 128), 0)
        lane = iota((48, 128), 1)
        for d in range(8):
            ssend[k, d] = jnp.sum(
                jnp.where(row == lane, level[d * 48 : d * 48 + 48], 0.0), axis=0, keepdims=True
            )
        srecv[k, me] = ssend[k, me]

    def blend(k):
        part = jnp.dot(weights[k], kvv[offsets[k]], preferred_element_type=jnp.float32)
        osend[k] = (part * inverse[k]).astype(jnp.bfloat16).reshape(8, 48, 128)
        orecv[k, me] = osend[k, me]

    def send_back(index):
        for i in range(1, 8):
            part_copy(index, i).start()

    hand_on(5, (11,))
    hand_on(6, (12,))
    pass_on(2, 0)
    for i in (4, 7, 8, 11):
        query_sends[i].wait_recv()
    here = ones_where(owners == owner_at(iota((8, 64), 0)) + me)
    match = jnp.concatenate(
        [small_dot(here, named_by(d)) for d in range(8)], axis=0
    )
    earlier = small_dot(match, before)
    numbers = iota((8, 128), 1).astype(jnp.bfloat16)
    for rank in range(2):
        chosen = jnp.where(earlier == rank, match, 0.0).astype(jnp.bfloat16)
        index_rows[rank * 8 : rank * 8 + 8, 0:64] = dot_t(numbers, chosen).astype(jnp.int32)
    index_copy = pltpu.make_async_copy(index_rows, index_ref, index_sem)
    index_copy.start()
    for i in (9, 10, 12):
        query_sends[i].wait_recv()
    index_copy.wait()
    loads[9].wait()
    loads[10].wait()
    weigh(0)
    blend(0)
    pass_on(2, 1)
    weigh(1)
    blend(1)
    weigh(2)
    blend(2)
    send_back(0)
    pass_on(3, 0)
    pl.semaphore_wait(above_here.at[0], 1)
    token(True, 1)
    pl.semaphore_wait(below_here.at[0], 1)
    token(False, 1)
    weigh(3)
    weigh(4)
    blend(3)
    blend(4)
    send_back(1)
    pass_on(3, 1)
    pl.semaphore_wait(above_here.at[1], 1)
    token(True, 2)
    pl.semaphore_wait(below_here.at[1], 1)
    weigh(5)
    weigh(6)
    blend(5)
    blend(6)
    send_back(2)
    ring(0, 4, 0).wait_recv()
    weigh(7)
    for i in range(1, 8):
        stat_copy(i).start()
    ring(1, 4, 1).wait_recv()
    blend(7)
    send_back(3)
    def head_copy(i):
        peer = (head + i) % 8
        return pltpu.make_async_remote_copy(
            src_ref=stage.at[peer],
            dst_ref=out_ref.at[head],
            send_sem=y_send_sem,
            recv_sem=y_recv_sem,
            device_id=(pre, peer),
            device_id_type=MESH,
        )

    def settle(target):
        levels = []
        row = iota((24, 128), 0)
        lane = iota((24, 128), 1)
        for j in range(4):
            slot = index_at(2, target * 4 + j, 127)
            stats = srecv[slot // 16, (slot // 2) % 8]
            levels.append(
                jnp.sum(
                    jnp.where(lane == row + 24 * (slot % 2), stats, 0.0), axis=1, keepdims=True
                )
            )
        levels = jnp.concatenate(levels, axis=0)
        rows = pl.ds(target * 96, 96)
        local = lmax[rows, :]
        top = jnp.maximum(levels, local)
        pre_factor = jnp.exp2(levels - top)
        local_factor = jnp.exp2(local - top)
        inverse_sum = 1.0 / (pre_factor + local_factor)
        share[rows, :] = pre_factor * inverse_sum
        lpart[rows, :] = lpart[rows, :] * (local_factor * inverse_sum)

    def combine(target):
        parts = []
        row = iota((24, 128), 0)
        for j in range(4):
            slot = index_at(2, target * 4 + j, 127)
            both = orecv[slot // 16, (slot // 2) % 8].astype(jnp.float32)
            parts.append(jnp.where(row * 0 + slot % 2 == 0, both[:24], both[24:]))
        rows = pl.ds(pl.multiple_of(target * 96, 96), 96)
        mixed = jnp.concatenate(parts, axis=0) * share[rows, :] + lpart[rows, :]
        stage[target] = mixed.astype(jnp.bfloat16)

    wait_for(srecv.at[:, seven], s_recv_sem)
    for target in range(8):
        settle(target)
    for index in range(4):
        wait_for(orecv.at[pl.ds(*return_groups[index]), seven], o_recv_sem.at[index])
    pl.semaphore_wait(above_here.at[2], 1)
    for batch in ((4, 3), (5, 2), (6, 1), (7, 0)):
        for i in batch:
            combine((head + i) % 8)
        for i in batch:
            if i:
                head_copy(i).start()
    own = pltpu.make_async_copy(stage.at[head], out_ref.at[head], own_sem)
    own.start()

    for which in range(2):
        wait_for((kvk, kvv)[which].at[seven], ring_send.at[which])
    for copy in query_sends:
        copy.wait_send()
    for index in range(4):
        wait_for(osend.at[pl.ds(*return_groups[index]), seven], o_send_sem.at[index])
    wait_for(ssend.at[:, seven], s_send_sem)
    wait_for(stage.at[seven], y_send_sem)
    own.wait()
    wait_for(out_ref.at[seven], y_recv_sem)


def shards(
    queries,
    prefix_keys,
    prefix_values,
    suffix_keys,
    suffix_values,
    new_keys,
    new_values,
    suffix_lengths,
    prefix_of_row,
    owner_of_prefix,
):
    bf16 = jnp.bfloat16
    by_step = jnp.transpose(queries, (0, 2, 1, 3))
    anywhere = pl.BlockSpec(memory_space=pltpu.HBM)
    dma = pltpu.SemaphoreType.DMA
    gathered = pl.pallas_call(
        kernel,
        out_shape=jax.ShapeDtypeStruct((8, 96, 128), bf16),
        in_specs=[anywhere] * 11,
        out_specs=anywhere,
        scratch_shapes=[
            pltpu.VMEM((1, 32), jnp.int32),
            pltpu.VMEM((1, 64), jnp.int32),
            pltpu.SMEM((1, 32), jnp.int32),
            pltpu.VMEM((24, 128), jnp.int32),
            pltpu.SMEM((24, 128), jnp.int32),
            pltpu.VMEM((8, 33, 3, 8, 128), bf16),
            pltpu.VMEM((768, 128), bf16),
            pltpu.VMEM((8, 512, 128), bf16),
            pltpu.VMEM((8, 512, 128), bf16),
            pltpu.VMEM((3072, 128), bf16),
            pltpu.VMEM((3072, 128), bf16),
            pltpu.VMEM((96, 128), bf16),
            pltpu.VMEM((96, 128), bf16),
            pltpu.VMEM((8, 8, 48, 128), bf16),
            pltpu.VMEM((8, 8, 48, 128), bf16),
            pltpu.VMEM((8, 8, 48, 128), bf16),
            pltpu.VMEM((8, 8, 1, 128), jnp.float32),
            pltpu.VMEM((8, 8, 1, 128), jnp.float32),
            pltpu.VMEM((768, 96), jnp.float32),
            pltpu.VMEM((768, 96), bf16),
            pltpu.VMEM((768, 128), jnp.float32),
            pltpu.VMEM((768, 1), jnp.float32),
            pltpu.VMEM((768, 1), jnp.float32),
            pltpu.VMEM((768, 1), jnp.float32),
            pltpu.VMEM((8, 384, 512), bf16),
            pltpu.VMEM((8, 384, 128), jnp.float32),
            pltpu.VMEM((8, 96, 128), bf16),
            dma((11,)),
            dma((2,)),
            dma((2, 4, 2)),
            dma((13,)),
            dma((13,)),
            dma,
            dma((4,)),
            dma((4,)),
            dma,
            dma,
            dma,
            dma,
            dma,
            pltpu.SemaphoreType.REGULAR((3,)),
            pltpu.SemaphoreType.REGULAR((2,)),
        ],
        compiler_params=pltpu.CompilerParams(
            collective_id=0, has_side_effects=True, vmem_limit_bytes=60 * 1024 * 1024
        ),
        cost_estimate=pl.CostEstimate(
            flops=1_200_000_000, bytes_accessed=3_000_000, transcendentals=1_800_000
        ),
        name="shared_prefix",
    )(
        prefix_of_row.reshape(1, 32),
        owner_of_prefix.reshape(1, 64),
        suffix_lengths.reshape(1, 32),
        by_step,
        by_step.reshape(768, 128),
        prefix_keys.reshape(512, 128),
        prefix_values.reshape(512, 128),
        suffix_keys.reshape(3072, 128),
        suffix_values.reshape(3072, 128),
        jnp.transpose(new_keys, (1, 2, 0, 3)).reshape(96, 128),
        jnp.transpose(new_values, (1, 2, 0, 3)).reshape(96, 128),
    )
    ordered = jnp.transpose(gathered.reshape(8, 4, 3, 8, 128), (1, 0, 3, 2, 4))
    return ordered.reshape(4, 64, 3, 128)


def solution(mesh):
    in_specs = (
        P("pre", "head", None, None),
        P("pre", None, "head", None),
        P("pre", None, "head", None),
        P("pre", None, "head", None),
        P("pre", None, "head", None),
        P("pre", None, "head", None),
        P("pre", None, "head", None),
        P("pre"),
        P("pre"),
        P(),
    )
    out_specs = P(("pre", "head"), None, None, None)
    return jax.shard_map(shards, mesh=mesh, in_specs=in_specs, out_specs=out_specs, check_vma=False)
```

```python
import math

import jax
import jax.numpy as jnp
from jax import lax
from jax.experimental import pallas as pl
from jax.experimental.pallas import tpu as pltpu
from jax.sharding import PartitionSpec as P

MESH = pl.DeviceIdType.MESH
masked_score = -1e30
offsets = (0, 1, 7, 2, 6, 3, 5, 4)
return_groups = ((0, 3), (3, 2), (5, 2))


def dot_t(a, b):
    return lax.dot_general(a, b, (((1,), (1,)), ((), ())), preferred_element_type=jnp.float32)


def kernel(
    prefix_hbm,
    owner_hbm,
    len_hbm,
    q4_hbm,
    q2_hbm,
    pk_hbm,
    pv_hbm,
    sk_hbm,
    sv_hbm,
    nk_hbm,
    nv_hbm,
    out_ref,
    prefix_here,
    owner_here,
    len_ref,
    index_rows,
    index_ref,
    qall,
    q2,
    kvk,
    kvv,
    sk,
    sv,
    nk,
    nv,
    qpack,
    osend,
    orecv,
    ssend,
    srecv,
    snew,
    pnew,
    lpart,
    lmax,
    share,
    lsum,
    weights,
    inverse,
    stage,
    load_sem,
    ring_send,
    ring_recv,
    q_send_sem,
    q_recv_sem,
    index_sem,
    o_send_sem,
    o_recv_sem,
    s_send_sem,
    s_recv_sem,
    y_send_sem,
    y_recv_sem,
    own_sem,
    above_here,
    below_here,
    far_q_send_sem,
    far_q_recv_sem,
    far_o_send_sem,
    far_o_recv_sem,
    far_s_send_sem,
    far_s_recv_sem,
):
    pre = lax.axis_index("pre")
    head = lax.axis_index("head")
    z = pre // 8
    me = pre % 8
    plane = z * 8
    right = ((z + 1) % 8) * 8 + me
    left = ((z + 7) % 8) * 8 + me
    column, core = me // 2, me % 2
    ahead = ((column + 1) % 4) * 2 + core
    behind = ((column + 3) % 4) * 2 + core
    opposite = ((column + 2) % 4) * 2 + core
    sibling = column * 2 + 1 - core
    to_log2 = 128 ** (-0.5) * math.log2(math.e)

    barrier = pltpu.get_barrier_semaphore()

    def greet(pre_index, head_index):
        pl.semaphore_signal(
            barrier, inc=1, device_id=(pre_index, head_index), device_id_type=MESH
        )

    above, below = (head + 1) % 8, (head + 7) % 8
    for peer in (right, left, plane + ahead, plane + behind, plane + sibling):
        greet(peer, head)
    greet(pre, above)
    greet(pre, below)

    loads = [
        pltpu.make_async_copy(a, b, load_sem.at[i])
        for i, (a, b) in enumerate(
            (
                (prefix_hbm, prefix_here),
                (owner_hbm, owner_here),
                (len_hbm, len_ref),
                (q4_hbm, qall.at[me, pl.ds(1, 32)]),
                (q2_hbm, q2),
                (nk_hbm, nk),
                (nv_hbm, nv),
                (sk_hbm, sk),
                (sv_hbm, sv),
                (pk_hbm, kvk.at[0]),
                (pv_hbm, kvv.at[0]),
            )
        )
    ]
    for i in (0, 1, 3):
        loads[i].start()

    def ring(way, hop, which):
        held, own = ((kvk, pk_hbm), (kvv, pv_hbm))[which]
        if way == 0:
            source, target, device = (9 - hop) % 8, 8 - hop, right
        else:
            source, target, device = hop - 1, hop, left
        return pltpu.make_async_remote_copy(
            src_ref=own if hop == 1 else held.at[source],
            dst_ref=held.at[target],
            send_sem=ring_send.at[which],
            recv_sem=ring_recv.at[way, hop - 1, which],
            device_id=(device, head),
            device_id_type=MESH,
        )

    def plane_copy(source, target, blocks, send_sem, recv_sem, i):
        peer = (me + i) % 8
        return pltpu.make_async_remote_copy(
            src_ref=source.at[blocks, peer],
            dst_ref=target.at[blocks, me],
            send_sem=send_sem,
            recv_sem=recv_sem,
            device_id=(plane + peer, head),
            device_id_type=MESH,
        )

    def wait_for(block, sem):
        pltpu.make_async_copy(block, block, sem).wait()

    def query_copy(i, source, rows, peer):
        block = qall.at[source, rows]
        return pltpu.make_async_remote_copy(
            src_ref=block,
            dst_ref=block,
            send_sem=q_send_sem.at[i],
            recv_sem=q_recv_sem.at[i],
            device_id=(plane + peer, head),
            device_id_type=MESH,
        )

    every, first_half, second_half = pl.ds(0, 33), pl.ds(0, 17), pl.ds(17, 16)

    seven = pl.ds(0, 7)

    def part_copy(index, i):
        blocks = pl.ds(*return_groups[index])
        return plane_copy(osend, orecv, blocks, o_send_sem.at[index], o_recv_sem.at[index], i)

    def stat_copy(i):
        return plane_copy(ssend, srecv, seven, s_send_sem, s_recv_sem, i)

    def far_query(way):
        return pltpu.make_async_remote_copy(
            src_ref=qpack.at[7, pl.ds(4 * way, 4)],
            dst_ref=qpack.at[5 + way, pl.ds(8, 4)],
            send_sem=far_q_send_sem.at[way],
            recv_sem=far_q_recv_sem.at[way],
            device_id=((right, left)[way], head),
            device_id_type=MESH,
        )

    def far_copy(source, target, send_sem, recv_sem, d):
        return pltpu.make_async_remote_copy(
            src_ref=source.at[7, d],
            dst_ref=target.at[7, me],
            send_sem=send_sem,
            recv_sem=recv_sem,
            device_id=((left if d < 4 else right) - me + d, head),
            device_id_type=MESH,
        )

    pl.semaphore_wait(barrier, 7)
    for way in range(2):
        ring(way, 1, 0).start()
    for i in (4, 5, 2, 7, 8, 6, 9, 10):
        loads[i].start()

    def token(from_above, step):
        tokens, peer = (above_here, below) if from_above else (below_here, above)
        pl.semaphore_signal(
            tokens.at[step], inc=1, device_id=(pre, peer), device_id_type=MESH
        )

    token(True, 0)
    token(False, 0)

    query_sends = [
        query_copy(0, me, first_half, ahead),
        query_copy(1, me, first_half, behind),
        query_copy(2, me, second_half, ahead),
        query_copy(3, me, second_half, behind),
        query_copy(4, me, every, sibling),
        query_copy(5, behind, first_half, ahead),
        query_copy(6, ahead, second_half, behind),
        query_copy(7, behind, first_half, sibling),
        query_copy(8, ahead, first_half, sibling),
        query_copy(9, behind, second_half, sibling),
        query_copy(10, ahead, second_half, sibling),
        query_copy(11, opposite, first_half, sibling),
        query_copy(12, opposite, second_half, sibling),
    ]

    def hand_on(arrived, onward):
        query_sends[arrived].wait_recv()
        for i in onward:
            query_sends[i].start()

    loads[0].wait()
    qall[me, 0] = jnp.full((3, 8, 128), -1.0, jnp.bfloat16)
    qall[me, 0, 0, :, 0:32] = jnp.broadcast_to(prefix_here[...], (8, 32)).astype(jnp.bfloat16)
    loads[3].wait()
    for copy in query_sends[:5]:
        copy.start()

    loads[1].wait()

    def small_dot(a, b):
        return jnp.dot(
            a.astype(jnp.bfloat16), b.astype(jnp.bfloat16), preferred_element_type=jnp.float32
        )

    def iota(shape, dim):
        return lax.broadcasted_iota(jnp.int32, shape, dim)

    def ones_where(condition):
        return jnp.where(condition, 1.0, 0.0)

    def owner_at(k):
        offset = jnp.zeros_like(k)
        for place, value in enumerate(offsets):
            offset = jnp.where(k == place, value, offset)
        return ((z + offset) & 7) * 8

    def named_by(d):
        names = qall[d, 0, 0].astype(jnp.float32)[0:1]
        return ones_where(names == iota((64, 128), 0).astype(jnp.float32))

    before = ones_where(iota((128, 128), 0) < iota((128, 128), 1))
    place = iota((64, 64), 0)
    owners = owner_here[...]
    held = ones_where(owners == owner_at(place >> 3) + (place & 7))
    mine = small_dot(held, named_by(me))
    earlier = small_dot(mine, before)
    slots = small_dot(2 * iota((8, 64), 1).astype(jnp.float32), mine) + small_dot(
        jnp.ones((8, 64), jnp.float32), mine * earlier
    )
    index_rows[16:24, :] = slots.astype(jnp.int32)

    for way in range(2):
        ring(way, 1, 1).start()

    loads[4].wait()
    loads[5].wait()
    snew[...] = dot_t(q2[...], nk[...])
    loads[2].wait()
    loads[7].wait()
    loads[8].wait()

    def pair(i):
        rows = pl.ds(i * 48, 48)
        keys = pl.ds(i * 192, 192)
        scores = dot_t(q2[rows, :], sk[keys, :])
        row = lax.broadcasted_iota(jnp.int32, (48, 192), 0)
        lane = lax.broadcasted_iota(jnp.int32, (48, 192), 1)
        low = jnp.where(row < 24, 0, 96)
        high = jnp.where(row < 24, len_ref[0, 2 * i], 96 + len_ref[0, 2 * i + 1])
        scores = jnp.where((lane >= low) & (lane < high), scores, masked_score)
        row = lax.broadcasted_iota(jnp.int32, (48, 96), 0)
        lane = lax.broadcasted_iota(jnp.int32, (48, 96), 1)
        second = row >= 24
        place = lane - jnp.where(second, 2 * i + 1, 2 * i)
        within = jnp.where(second, row - 24, row)
        fresh_ok = (
            (place == 0)
            | ((place == 32) & (within >= 8))
            | ((place == 64) & (within >= 16))
        )
        fresh = jnp.where(fresh_ok, snew[rows, :], masked_score)
        top = jnp.maximum(
            jnp.max(scores, axis=1, keepdims=True), jnp.max(fresh, axis=1, keepdims=True)
        )
        scores = jnp.exp2((scores - top) * to_log2)
        fresh = jnp.exp2((fresh - top) * to_log2)
        lmax[rows, :] = top * to_log2
        lsum[rows, :] = jnp.sum(scores, axis=1, keepdims=True) + jnp.sum(
            fresh, axis=1, keepdims=True
        )
        pnew[rows, :] = fresh.astype(jnp.bfloat16)
        lpart[rows, :] = jnp.dot(
            scores.astype(jnp.bfloat16), sv[keys, :], preferred_element_type=jnp.float32
        )

    def pairs(first):
        for j in range(4):
            pair(first + j)

    def pass_on(hop, which):
        for way in range(2):
            ring(way, hop, which).wait_recv()
            if hop < 3:
                ring(way, hop + 1, which).start()

    pairs(0)
    pairs(4)
    pass_on(1, 0)
    hand_on(0, (5, 7))
    hand_on(1, (8,))
    pairs(8)
    hand_on(2, (9,))
    hand_on(3, (6, 10))
    pass_on(1, 1)
    pairs(12)
    loads[6].wait()
    part = lpart[...] + jnp.dot(pnew[...], nv[...], preferred_element_type=jnp.float32)
    lpart[...] = part / lsum[...]
    lmax[...] = lmax[...] + jnp.log2(lsum[...])

    def index_at(table, place, last):
        return jnp.minimum(jnp.maximum(index_ref[table * 8, place], 0), last)

    def pack(k):
        for d in range(8):
            rows = [qall[d, 1 + index_at(rank, d * 8 + k, 31)] for rank in range(2)]
            both = [row.astype(jnp.float32).reshape(24, 128) for row in rows]
            qpack[k, d] = jnp.concatenate(both, axis=0).astype(jnp.bfloat16)

    def sources(k):
        return 12 if k in (5, 6) else 8

    def weigh(k):
        pack(k)
        count = sources(k)
        scores = dot_t(qpack[k, 0:count].reshape(count * 48, 128), kvk[offsets[k]])
        top = jnp.max(scores, axis=1, keepdims=True)
        scores = jnp.exp2((scores - top) * to_log2)
        weights[k, 0 : count * 48] = scores.astype(jnp.bfloat16)
        total = jnp.dot(
            weights[k, 0 : count * 48],
            jnp.ones((512, 128), jnp.bfloat16),
            preferred_element_type=jnp.float32,
        )
        inverse[k, 0 : count * 48] = 1.0 / total
        level = top * to_log2 + jnp.log2(total)
        row = iota((48, 128), 0)
        lane = iota((48, 128), 1)
        for d in range(count):
            block, place = (k, d) if d < 8 else (7, d - 8 + 4 * (k - 5))
            ssend[block, place] = jnp.sum(
                jnp.where(row == lane, level[d * 48 : d * 48 + 48], 0.0), axis=0, keepdims=True
            )
        srecv[k, me] = ssend[k, me]

    def blend(k):
        count = sources(k)
        part = jnp.dot(
            weights[k, 0 : count * 48], kvv[offsets[k]], preferred_element_type=jnp.float32
        )
        part = (part * inverse[k, 0 : count * 48]).astype(jnp.bfloat16).reshape(count, 48, 128)
        osend[k] = part[0:8]
        if count > 8:
            osend[7, 4 * (k - 5) : 4 * (k - 5) + 4] = part[8:12]
        orecv[k, me] = osend[k, me]

    def send_back(index):
        for i in range(1, 8):
            part_copy(index, i).start()

    hand_on(5, (11,))
    hand_on(6, (12,))
    pass_on(2, 0)
    for i in (4, 7, 8, 11):
        query_sends[i].wait_recv()
    here = ones_where(owners == owner_at(iota((8, 64), 0)) + me)
    match = jnp.concatenate(
        [small_dot(here, named_by(d)) for d in range(8)], axis=0
    )
    earlier = small_dot(match, before)
    numbers = iota((8, 128), 1).astype(jnp.bfloat16)
    for rank in range(2):
        chosen = jnp.where(earlier == rank, match, 0.0).astype(jnp.bfloat16)
        index_rows[rank * 8 : rank * 8 + 8, 0:64] = dot_t(numbers, chosen).astype(jnp.int32)
    index_copy = pltpu.make_async_copy(index_rows, index_ref, index_sem)
    index_copy.start()
    for i in (9, 10, 12):
        query_sends[i].wait_recv()
    index_copy.wait()
    loads[9].wait()
    loads[10].wait()
    pack(7)
    for way in range(2):
        far_query(way).start()
    weigh(0)
    blend(0)
    pass_on(2, 1)
    weigh(1)
    blend(1)
    weigh(2)
    blend(2)
    send_back(0)
    pass_on(3, 0)
    pl.semaphore_wait(above_here.at[0], 1)
    token(True, 1)
    pl.semaphore_wait(below_here.at[0], 1)
    token(False, 1)
    weigh(3)
    weigh(4)
    blend(3)
    blend(4)
    send_back(1)
    for way in range(2):
        far_query(way).wait_recv()
    weigh(5)
    weigh(6)
    for d in range(8):
        far_copy(ssend, srecv, far_s_send_sem, far_s_recv_sem, d).start()
    for i in range(1, 8):
        stat_copy(i).start()
    pl.semaphore_wait(above_here.at[1], 1)
    token(True, 2)
    pl.semaphore_wait(below_here.at[1], 1)
    pass_on(3, 1)
    for k in (5, 6):
        blend(k)
        for d in range(4 * (k - 5), 4 * (k - 5) + 4):
            far_copy(osend, orecv, far_o_send_sem, far_o_recv_sem, d).start()
    send_back(2)

    def head_copy(i):
        peer = (head + i) % 8
        return pltpu.make_async_remote_copy(
            src_ref=stage.at[peer],
            dst_ref=out_ref.at[head],
            send_sem=y_send_sem,
            recv_sem=y_recv_sem,
            device_id=(pre, peer),
            device_id_type=MESH,
        )

    def settle(target):
        levels = []
        row = iota((24, 128), 0)
        lane = iota((24, 128), 1)
        for j in range(4):
            slot = index_at(2, target * 4 + j, 127)
            stats = srecv[slot // 16, (slot // 2) % 8]
            levels.append(
                jnp.sum(
                    jnp.where(lane == row + 24 * (slot % 2), stats, 0.0), axis=1, keepdims=True
                )
            )
        levels = jnp.concatenate(levels, axis=0)
        rows = pl.ds(target * 96, 96)
        local = lmax[rows, :]
        top = jnp.maximum(levels, local)
        pre_factor = jnp.exp2(levels - top)
        local_factor = jnp.exp2(local - top)
        inverse_sum = 1.0 / (pre_factor + local_factor)
        share[rows, :] = pre_factor * inverse_sum
        lpart[rows, :] = lpart[rows, :] * (local_factor * inverse_sum)

    def combine(target):
        parts = []
        row = iota((24, 128), 0)
        for j in range(4):
            slot = index_at(2, target * 4 + j, 127)
            both = orecv[slot // 16, (slot // 2) % 8].astype(jnp.float32)
            parts.append(jnp.where(row * 0 + slot % 2 == 0, both[:24], both[24:]))
        rows = pl.ds(pl.multiple_of(target * 96, 96), 96)
        mixed = jnp.concatenate(parts, axis=0) * share[rows, :] + lpart[rows, :]
        stage[target] = mixed.astype(jnp.bfloat16)

    wait_for(srecv.at[seven, seven], s_recv_sem)
    wait_for(srecv.at[7], far_s_recv_sem)
    for target in range(8):
        settle(target)
    for index in range(3):
        wait_for(orecv.at[pl.ds(*return_groups[index]), seven], o_recv_sem.at[index])
    wait_for(orecv.at[7], far_o_recv_sem)
    pl.semaphore_wait(above_here.at[2], 1)
    for batch in ((4, 3), (5, 2), (6, 1), (7, 0)):
        for i in batch:
            combine((head + i) % 8)
        for i in batch:
            if i:
                head_copy(i).start()
    own = pltpu.make_async_copy(stage.at[head], out_ref.at[head], own_sem)
    own.start()

    for which in range(2):
        wait_for((kvk, kvv)[which].at[pl.ds(0, 6)], ring_send.at[which])
    for copy in query_sends:
        copy.wait_send()
    for index in range(3):
        wait_for(osend.at[pl.ds(*return_groups[index]), seven], o_send_sem.at[index])
    wait_for(ssend.at[seven, seven], s_send_sem)
    for way in range(2):
        far_query(way).wait_send()
    wait_for(osend.at[7], far_o_send_sem)
    wait_for(ssend.at[7], far_s_send_sem)
    wait_for(stage.at[seven], y_send_sem)
    own.wait()
    wait_for(out_ref.at[seven], y_recv_sem)


def shards(
    queries,
    prefix_keys,
    prefix_values,
    suffix_keys,
    suffix_values,
    new_keys,
    new_values,
    suffix_lengths,
    prefix_of_row,
    owner_of_prefix,
):
    bf16 = jnp.bfloat16
    by_step = jnp.transpose(queries, (0, 2, 1, 3))
    anywhere = pl.BlockSpec(memory_space=pltpu.HBM)
    dma = pltpu.SemaphoreType.DMA
    gathered = pl.pallas_call(
        kernel,
        out_shape=jax.ShapeDtypeStruct((8, 96, 128), bf16),
        in_specs=[anywhere] * 11,
        out_specs=anywhere,
        scratch_shapes=[
            pltpu.VMEM((1, 32), jnp.int32),
            pltpu.VMEM((1, 64), jnp.int32),
            pltpu.SMEM((1, 32), jnp.int32),
            pltpu.VMEM((24, 128), jnp.int32),
            pltpu.SMEM((24, 128), jnp.int32),
            pltpu.VMEM((8, 33, 3, 8, 128), bf16),
            pltpu.VMEM((768, 128), bf16),
            pltpu.VMEM((8, 512, 128), bf16),
            pltpu.VMEM((8, 512, 128), bf16),
            pltpu.VMEM((3072, 128), bf16),
            pltpu.VMEM((3072, 128), bf16),
            pltpu.VMEM((96, 128), bf16),
            pltpu.VMEM((96, 128), bf16),
            pltpu.VMEM((8, 12, 48, 128), bf16),
            pltpu.VMEM((8, 8, 48, 128), bf16),
            pltpu.VMEM((8, 8, 48, 128), bf16),
            pltpu.VMEM((8, 8, 1, 128), jnp.float32),
            pltpu.VMEM((8, 8, 1, 128), jnp.float32),
            pltpu.VMEM((768, 96), jnp.float32),
            pltpu.VMEM((768, 96), bf16),
            pltpu.VMEM((768, 128), jnp.float32),
            pltpu.VMEM((768, 1), jnp.float32),
            pltpu.VMEM((768, 1), jnp.float32),
            pltpu.VMEM((768, 1), jnp.float32),
            pltpu.VMEM((8, 576, 512), bf16),
            pltpu.VMEM((8, 576, 128), jnp.float32),
            pltpu.VMEM((8, 96, 128), bf16),
            dma((11,)),
            dma((2,)),
            dma((2, 4, 2)),
            dma((13,)),
            dma((13,)),
            dma,
            dma((4,)),
            dma((4,)),
            dma,
            dma,
            dma,
            dma,
            dma,
            pltpu.SemaphoreType.REGULAR((3,)),
            pltpu.SemaphoreType.REGULAR((2,)),
            dma((2,)),
            dma((2,)),
            dma,
            dma,
            dma,
            dma,
        ],
        compiler_params=pltpu.CompilerParams(
            collective_id=0, has_side_effects=True, vmem_limit_bytes=60 * 1024 * 1024
        ),
        cost_estimate=pl.CostEstimate(
            flops=1_200_000_000, bytes_accessed=3_000_000, transcendentals=1_800_000
        ),
        name="shared_prefix",
    )(
        prefix_of_row.reshape(1, 32),
        owner_of_prefix.reshape(1, 64),
        suffix_lengths.reshape(1, 32),
        by_step,
        by_step.reshape(768, 128),
        prefix_keys.reshape(512, 128),
        prefix_values.reshape(512, 128),
        suffix_keys.reshape(3072, 128),
        suffix_values.reshape(3072, 128),
        jnp.transpose(new_keys, (1, 2, 0, 3)).reshape(96, 128),
        jnp.transpose(new_values, (1, 2, 0, 3)).reshape(96, 128),
    )
    ordered = jnp.transpose(gathered.reshape(8, 4, 3, 8, 128), (1, 0, 3, 2, 4))
    return ordered.reshape(4, 64, 3, 128)


def solution(mesh):
    in_specs = (
        P("pre", "head", None, None),
        P("pre", None, "head", None),
        P("pre", None, "head", None),
        P("pre", None, "head", None),
        P("pre", None, "head", None),
        P("pre", None, "head", None),
        P("pre", None, "head", None),
        P("pre"),
        P("pre"),
        P(),
    )
    out_specs = P(("pre", "head"), None, None, None)
    return jax.shard_map(shards, mesh=mesh, in_specs=in_specs, out_specs=out_specs, check_vma=False)
```

```python
import math

import jax
import jax.numpy as jnp
from jax import lax
from jax.experimental import pallas as pl
from jax.experimental.pallas import tpu as pltpu
from jax.sharding import PartitionSpec as P

MESH = pl.DeviceIdType.MESH
masked_score = -1e30
offsets = (0, 1, 7, 2, 6, 3, 5, 4)
return_groups = ((0, 3), (3, 2), (5, 2))


def dot_t(a, b):
    return lax.dot_general(a, b, (((1,), (1,)), ((), ())), preferred_element_type=jnp.float32)


def kernel(
    prefix_hbm,
    owner_hbm,
    len_hbm,
    q4_hbm,
    q2_hbm,
    pk_hbm,
    pv_hbm,
    sk_hbm,
    sv_hbm,
    nk_hbm,
    nv_hbm,
    out_ref,
    prefix_here,
    owner_here,
    len_ref,
    index_rows,
    index_ref,
    qall,
    q2,
    kvk,
    kvv,
    sk,
    sv,
    nk,
    nv,
    qpack,
    osend,
    orecv,
    ssend,
    srecv,
    snew,
    pnew,
    lpart,
    lmax,
    share,
    lsum,
    weights,
    inverse,
    stage,
    load_sem,
    ring_send,
    ring_recv,
    q_send_sem,
    q_recv_sem,
    index_sem,
    o_send_sem,
    o_recv_sem,
    s_send_sem,
    s_recv_sem,
    y_send_sem,
    y_recv_sem,
    own_sem,
    above_here,
    below_here,
    far_q_send_sem,
    far_q_recv_sem,
    far_o_send_sem,
    far_o_recv_sem,
    far_s_send_sem,
    far_s_recv_sem,
):
    pre = lax.axis_index("pre")
    head = lax.axis_index("head")
    z = pre // 8
    me = pre % 8
    plane = z * 8
    right = ((z + 1) % 8) * 8 + me
    left = ((z + 7) % 8) * 8 + me
    column, core = me // 2, me % 2
    ahead = ((column + 1) % 4) * 2 + core
    behind = ((column + 3) % 4) * 2 + core
    opposite = ((column + 2) % 4) * 2 + core
    sibling = column * 2 + 1 - core
    to_log2 = 128 ** (-0.5) * math.log2(math.e)

    barrier = pltpu.get_barrier_semaphore()

    def greet(pre_index, head_index):
        pl.semaphore_signal(
            barrier, inc=1, device_id=(pre_index, head_index), device_id_type=MESH
        )

    above, below = (head + 1) % 8, (head + 7) % 8
    for peer in (right, left, plane + ahead, plane + behind, plane + sibling):
        greet(peer, head)
    greet(pre, above)
    greet(pre, below)

    loads = [
        pltpu.make_async_copy(a, b, load_sem.at[i])
        for i, (a, b) in enumerate(
            (
                (prefix_hbm, prefix_here),
                (owner_hbm, owner_here),
                (len_hbm, len_ref),
                (q4_hbm, qall.at[me, pl.ds(1, 32)]),
                (q2_hbm, q2),
                (nk_hbm, nk),
                (nv_hbm, nv),
                (sk_hbm, sk),
                (sv_hbm, sv),
                (pk_hbm, kvk.at[0]),
                (pv_hbm, kvv.at[0]),
            )
        )
    ]
    for i in (0, 1, 3):
        loads[i].start()

    def ring(way, hop, which):
        held, own = ((kvk, pk_hbm), (kvv, pv_hbm))[which]
        if way == 0:
            source, target, device = (9 - hop) % 8, 8 - hop, right
        else:
            source, target, device = hop - 1, hop, left
        return pltpu.make_async_remote_copy(
            src_ref=own if hop == 1 else held.at[source],
            dst_ref=held.at[target],
            send_sem=ring_send.at[which],
            recv_sem=ring_recv.at[way, hop - 1, which],
            device_id=(device, head),
            device_id_type=MESH,
        )

    def plane_copy(source, target, blocks, send_sem, recv_sem, i):
        peer = (me + i) % 8
        return pltpu.make_async_remote_copy(
            src_ref=source.at[blocks, peer],
            dst_ref=target.at[blocks, me],
            send_sem=send_sem,
            recv_sem=recv_sem,
            device_id=(plane + peer, head),
            device_id_type=MESH,
        )

    def wait_for(block, sem):
        pltpu.make_async_copy(block, block, sem).wait()

    def query_copy(i, source, rows, peer):
        block = qall.at[source, rows]
        return pltpu.make_async_remote_copy(
            src_ref=block,
            dst_ref=block,
            send_sem=q_send_sem.at[i],
            recv_sem=q_recv_sem.at[i],
            device_id=(plane + peer, head),
            device_id_type=MESH,
        )

    every, first_half, second_half = pl.ds(0, 33), pl.ds(0, 17), pl.ds(17, 16)

    seven = pl.ds(0, 7)

    def part_copy(index, i):
        blocks = pl.ds(*return_groups[index])
        return plane_copy(osend, orecv, blocks, o_send_sem.at[index], o_recv_sem.at[index], i)

    def stat_copy(i):
        return plane_copy(ssend, srecv, seven, s_send_sem, s_recv_sem, i)

    def far_query(way):
        return pltpu.make_async_remote_copy(
            src_ref=qpack.at[7, pl.ds(4 * way, 4)],
            dst_ref=qpack.at[5 + way, pl.ds(8, 4)],
            send_sem=far_q_send_sem.at[way],
            recv_sem=far_q_recv_sem.at[way],
            device_id=((right, left)[way], head),
            device_id_type=MESH,
        )

    def far_copy(source, target, send_sem, recv_sem, d):
        return pltpu.make_async_remote_copy(
            src_ref=source.at[7, d],
            dst_ref=target.at[7, me],
            send_sem=send_sem,
            recv_sem=recv_sem,
            device_id=((left if d < 4 else right) - me + d, head),
            device_id_type=MESH,
        )

    pl.semaphore_wait(barrier, 7)
    for way in range(2):
        ring(way, 1, 0).start()
    for i in (4, 5, 2, 7, 8, 6, 9, 10):
        loads[i].start()

    def token(from_above, step):
        tokens, peer = (above_here, below) if from_above else (below_here, above)
        pl.semaphore_signal(
            tokens.at[step], inc=1, device_id=(pre, peer), device_id_type=MESH
        )

    token(True, 0)
    token(False, 0)

    query_sends = [
        query_copy(0, me, first_half, ahead),
        query_copy(1, me, first_half, behind),
        query_copy(2, me, second_half, ahead),
        query_copy(3, me, second_half, behind),
        query_copy(4, me, every, sibling),
        query_copy(5, behind, first_half, ahead),
        query_copy(6, ahead, second_half, behind),
        query_copy(7, behind, first_half, sibling),
        query_copy(8, ahead, first_half, sibling),
        query_copy(9, behind, second_half, sibling),
        query_copy(10, ahead, second_half, sibling),
        query_copy(11, opposite, first_half, sibling),
        query_copy(12, opposite, second_half, sibling),
    ]

    def hand_on(arrived, onward):
        query_sends[arrived].wait_recv()
        for i in onward:
            query_sends[i].start()

    loads[0].wait()
    qall[me, 0] = jnp.full((3, 8, 128), -1.0, jnp.bfloat16)
    qall[me, 0, 0, :, 0:32] = jnp.broadcast_to(prefix_here[...], (8, 32)).astype(jnp.bfloat16)
    loads[3].wait()
    for copy in query_sends[:5]:
        copy.start()

    loads[1].wait()

    def small_dot(a, b):
        return jnp.dot(
            a.astype(jnp.bfloat16), b.astype(jnp.bfloat16), preferred_element_type=jnp.float32
        )

    def iota(shape, dim):
        return lax.broadcasted_iota(jnp.int32, shape, dim)

    def ones_where(condition):
        return jnp.where(condition, 1.0, 0.0)

    def owner_at(k):
        offset = jnp.zeros_like(k)
        for place, value in enumerate(offsets):
            offset = jnp.where(k == place, value, offset)
        return ((z + offset) & 7) * 8

    def named_by(d):
        names = qall[d, 0, 0].astype(jnp.float32)[0:1]
        return ones_where(names == iota((64, 128), 0).astype(jnp.float32))

    before = ones_where(iota((128, 128), 0) < iota((128, 128), 1))
    place = iota((64, 64), 0)
    owners = owner_here[...]
    held = ones_where(owners == owner_at(place >> 3) + (place & 7))
    mine = small_dot(held, named_by(me))
    earlier = small_dot(mine, before)
    slots = small_dot(2 * iota((8, 64), 1).astype(jnp.float32), mine) + small_dot(
        jnp.ones((8, 64), jnp.float32), mine * earlier
    )
    index_rows[16:24, :] = slots.astype(jnp.int32)

    for way in range(2):
        ring(way, 1, 1).start()

    loads[4].wait()
    loads[5].wait()
    snew[...] = dot_t(q2[...], nk[...])
    loads[2].wait()
    loads[7].wait()
    loads[8].wait()

    def pair(i):
        rows = pl.ds(i * 48, 48)
        keys = pl.ds(i * 192, 192)
        scores = dot_t(q2[rows, :], sk[keys, :])
        row = lax.broadcasted_iota(jnp.int32, (48, 192), 0)
        lane = lax.broadcasted_iota(jnp.int32, (48, 192), 1)
        low = jnp.where(row < 24, 0, 96)
        high = jnp.where(row < 24, len_ref[0, 2 * i], 96 + len_ref[0, 2 * i + 1])
        scores = jnp.where((lane >= low) & (lane < high), scores, masked_score)
        row = lax.broadcasted_iota(jnp.int32, (48, 96), 0)
        lane = lax.broadcasted_iota(jnp.int32, (48, 96), 1)
        second = row >= 24
        place = lane - jnp.where(second, 2 * i + 1, 2 * i)
        within = jnp.where(second, row - 24, row)
        fresh_ok = (
            (place == 0)
            | ((place == 32) & (within >= 8))
            | ((place == 64) & (within >= 16))
        )
        fresh = jnp.where(fresh_ok, snew[rows, :], masked_score)
        top = jnp.maximum(
            jnp.max(scores, axis=1, keepdims=True), jnp.max(fresh, axis=1, keepdims=True)
        )
        scores = jnp.exp2((scores - top) * to_log2)
        fresh = jnp.exp2((fresh - top) * to_log2)
        lmax[rows, :] = top * to_log2
        lsum[rows, :] = jnp.sum(scores, axis=1, keepdims=True) + jnp.sum(
            fresh, axis=1, keepdims=True
        )
        pnew[rows, :] = fresh.astype(jnp.bfloat16)
        lpart[rows, :] = jnp.dot(
            scores.astype(jnp.bfloat16), sv[keys, :], preferred_element_type=jnp.float32
        )

    def pairs(first):
        for j in range(4):
            pair(first + j)

    def pass_on(hop, which):
        for way in (1, 0):
            ring(way, hop, which).wait_recv()
            if hop < 3:
                ring(way, hop + 1, which).start()

    pairs(0)
    pairs(4)
    pass_on(1, 0)
    hand_on(0, (5, 7))
    hand_on(1, (8,))
    pairs(8)
    hand_on(2, (9,))
    hand_on(3, (6, 10))
    pass_on(1, 1)
    pairs(12)
    loads[6].wait()
    part = lpart[...] + jnp.dot(pnew[...], nv[...], preferred_element_type=jnp.float32)
    lpart[...] = part / lsum[...]
    lmax[...] = lmax[...] + jnp.log2(lsum[...])

    def index_at(table, place, last):
        return jnp.minimum(jnp.maximum(index_ref[table * 8, place], 0), last)

    def pack(k):
        for d in range(8):
            rows = [qall[d, 1 + index_at(rank, d * 8 + k, 31)] for rank in range(2)]
            both = [row.astype(jnp.float32).reshape(24, 128) for row in rows]
            qpack[k, d] = jnp.concatenate(both, axis=0).astype(jnp.bfloat16)

    def sources(k):
        return 12 if k in (5, 6) else 8

    def weigh(k):
        pack(k)
        count = sources(k)
        scores = dot_t(qpack[k, 0:count].reshape(count * 48, 128), kvk[offsets[k]])
        top = jnp.max(scores, axis=1, keepdims=True)
        scores = jnp.exp2((scores - top) * to_log2)
        weights[k, 0 : count * 48] = scores.astype(jnp.bfloat16)
        total = jnp.dot(
            weights[k, 0 : count * 48],
            jnp.ones((512, 128), jnp.bfloat16),
            preferred_element_type=jnp.float32,
        )
        inverse[k, 0 : count * 48] = 1.0 / total
        level = top * to_log2 + jnp.log2(total)
        row = iota((48, 128), 0)
        lane = iota((48, 128), 1)
        for d in range(count):
            block, place = (k, d) if d < 8 else (7, d - 8 + 4 * (k - 5))
            ssend[block, place] = jnp.sum(
                jnp.where(row == lane, level[d * 48 : d * 48 + 48], 0.0), axis=0, keepdims=True
            )
        srecv[k, me] = ssend[k, me]

    def blend(k):
        count = sources(k)
        part = jnp.dot(
            weights[k, 0 : count * 48], kvv[offsets[k]], preferred_element_type=jnp.float32
        )
        part = (part * inverse[k, 0 : count * 48]).astype(jnp.bfloat16).reshape(count, 48, 128)
        osend[k] = part[0:8]
        if count > 8:
            osend[7, 4 * (k - 5) : 4 * (k - 5) + 4] = part[8:12]
        orecv[k, me] = osend[k, me]

    def send_back(index):
        for i in range(1, 8):
            part_copy(index, i).start()

    hand_on(5, (11,))
    hand_on(6, (12,))
    pass_on(2, 0)
    for i in (4, 7, 8, 11):
        query_sends[i].wait_recv()
    here = ones_where(owners == owner_at(iota((8, 64), 0)) + me)
    match = jnp.concatenate(
        [small_dot(here, named_by(d)) for d in range(8)], axis=0
    )
    earlier = small_dot(match, before)
    numbers = iota((8, 128), 1).astype(jnp.bfloat16)
    for rank in range(2):
        chosen = jnp.where(earlier == rank, match, 0.0).astype(jnp.bfloat16)
        index_rows[rank * 8 : rank * 8 + 8, 0:64] = dot_t(numbers, chosen).astype(jnp.int32)
    index_copy = pltpu.make_async_copy(index_rows, index_ref, index_sem)
    index_copy.start()
    for i in (9, 10, 12):
        query_sends[i].wait_recv()
    index_copy.wait()
    loads[9].wait()
    loads[10].wait()
    pack(7)
    for way in range(2):
        far_query(way).start()
    weigh(0)
    blend(0)
    pass_on(2, 1)
    weigh(1)
    blend(1)
    weigh(2)
    blend(2)
    send_back(0)
    pass_on(3, 0)
    pl.semaphore_wait(above_here.at[0], 1)
    token(True, 1)
    pl.semaphore_wait(below_here.at[0], 1)
    token(False, 1)
    weigh(3)
    weigh(4)
    blend(3)
    blend(4)
    send_back(1)
    for way in range(2):
        far_query(way).wait_recv()
    weigh(5)
    weigh(6)
    for d in range(8):
        far_copy(ssend, srecv, far_s_send_sem, far_s_recv_sem, d).start()
    for i in range(1, 8):
        stat_copy(i).start()
    pl.semaphore_wait(above_here.at[1], 1)
    token(True, 2)
    pl.semaphore_wait(below_here.at[1], 1)
    for k in (5, 6):
        ring(6 - k, 3, 1).wait_recv()
        blend(k)
        for d in range(4 * (k - 5), 4 * (k - 5) + 4):
            far_copy(osend, orecv, far_o_send_sem, far_o_recv_sem, d).start()
    send_back(2)

    def head_copy(i):
        peer = (head + i) % 8
        return pltpu.make_async_remote_copy(
            src_ref=stage.at[peer],
            dst_ref=out_ref.at[head],
            send_sem=y_send_sem,
            recv_sem=y_recv_sem,
            device_id=(pre, peer),
            device_id_type=MESH,
        )

    def settle(target):
        levels = []
        row = iota((24, 128), 0)
        lane = iota((24, 128), 1)
        for j in range(4):
            slot = index_at(2, target * 4 + j, 127)
            stats = srecv[slot // 16, (slot // 2) % 8]
            levels.append(
                jnp.sum(
                    jnp.where(lane == row + 24 * (slot % 2), stats, 0.0), axis=1, keepdims=True
                )
            )
        levels = jnp.concatenate(levels, axis=0)
        rows = pl.ds(target * 96, 96)
        local = lmax[rows, :]
        top = jnp.maximum(levels, local)
        pre_factor = jnp.exp2(levels - top)
        local_factor = jnp.exp2(local - top)
        inverse_sum = 1.0 / (pre_factor + local_factor)
        share[rows, :] = pre_factor * inverse_sum
        lpart[rows, :] = lpart[rows, :] * (local_factor * inverse_sum)

    def combine(target):
        parts = []
        row = iota((24, 128), 0)
        for j in range(4):
            slot = index_at(2, target * 4 + j, 127)
            both = orecv[slot // 16, (slot // 2) % 8].astype(jnp.float32)
            parts.append(jnp.where(row * 0 + slot % 2 == 0, both[:24], both[24:]))
        rows = pl.ds(pl.multiple_of(target * 96, 96), 96)
        mixed = jnp.concatenate(parts, axis=0) * share[rows, :] + lpart[rows, :]
        stage[target] = mixed.astype(jnp.bfloat16)

    wait_for(srecv.at[seven, seven], s_recv_sem)
    wait_for(srecv.at[7], far_s_recv_sem)
    for target in range(8):
        settle(target)
    for index in range(3):
        wait_for(orecv.at[pl.ds(*return_groups[index]), seven], o_recv_sem.at[index])
    wait_for(orecv.at[7], far_o_recv_sem)
    pl.semaphore_wait(above_here.at[2], 1)
    for batch in ((4, 3), (5, 2), (6, 1), (7, 0)):
        for i in batch:
            combine((head + i) % 8)
        for i in batch:
            if i:
                head_copy(i).start()
    own = pltpu.make_async_copy(stage.at[head], out_ref.at[head], own_sem)
    own.start()

    for which in range(2):
        wait_for((kvk, kvv)[which].at[pl.ds(0, 6)], ring_send.at[which])
    for copy in query_sends:
        copy.wait_send()
    for index in range(3):
        wait_for(osend.at[pl.ds(*return_groups[index]), seven], o_send_sem.at[index])
    wait_for(ssend.at[seven, seven], s_send_sem)
    for way in range(2):
        far_query(way).wait_send()
    wait_for(osend.at[7], far_o_send_sem)
    wait_for(ssend.at[7], far_s_send_sem)
    wait_for(stage.at[seven], y_send_sem)
    own.wait()
    wait_for(out_ref.at[seven], y_recv_sem)


def shards(
    queries,
    prefix_keys,
    prefix_values,
    suffix_keys,
    suffix_values,
    new_keys,
    new_values,
    suffix_lengths,
    prefix_of_row,
    owner_of_prefix,
):
    bf16 = jnp.bfloat16
    by_step = jnp.transpose(queries, (0, 2, 1, 3))
    anywhere = pl.BlockSpec(memory_space=pltpu.HBM)
    dma = pltpu.SemaphoreType.DMA
    gathered = pl.pallas_call(
        kernel,
        out_shape=pltpu.VMEM((8, 96, 128), bf16),
        in_specs=[anywhere] * 11,
        out_specs=pl.BlockSpec(memory_space=pltpu.VMEM),
        scratch_shapes=[
            pltpu.VMEM((1, 32), jnp.int32),
            pltpu.VMEM((1, 64), jnp.int32),
            pltpu.SMEM((1, 32), jnp.int32),
            pltpu.VMEM((24, 128), jnp.int32),
            pltpu.SMEM((24, 128), jnp.int32),
            pltpu.VMEM((8, 33, 3, 8, 128), bf16),
            pltpu.VMEM((768, 128), bf16),
            pltpu.VMEM((8, 512, 128), bf16),
            pltpu.VMEM((8, 512, 128), bf16),
            pltpu.VMEM((3072, 128), bf16),
            pltpu.VMEM((3072, 128), bf16),
            pltpu.VMEM((96, 128), bf16),
            pltpu.VMEM((96, 128), bf16),
            pltpu.VMEM((8, 12, 48, 128), bf16),
            pltpu.VMEM((8, 8, 48, 128), bf16),
            pltpu.VMEM((8, 8, 48, 128), bf16),
            pltpu.VMEM((8, 8, 1, 128), jnp.float32),
            pltpu.VMEM((8, 8, 1, 128), jnp.float32),
            pltpu.VMEM((768, 96), jnp.float32),
            pltpu.VMEM((768, 96), bf16),
            pltpu.VMEM((768, 128), jnp.float32),
            pltpu.VMEM((768, 1), jnp.float32),
            pltpu.VMEM((768, 1), jnp.float32),
            pltpu.VMEM((768, 1), jnp.float32),
            pltpu.VMEM((8, 576, 512), bf16),
            pltpu.VMEM((8, 576, 128), jnp.float32),
            pltpu.VMEM((8, 96, 128), bf16),
            dma((11,)),
            dma((2,)),
            dma((2, 4, 2)),
            dma((13,)),
            dma((13,)),
            dma,
            dma((4,)),
            dma((4,)),
            dma,
            dma,
            dma,
            dma,
            dma,
            pltpu.SemaphoreType.REGULAR((3,)),
            pltpu.SemaphoreType.REGULAR((2,)),
            dma((2,)),
            dma((2,)),
            dma,
            dma,
            dma,
            dma,
        ],
        compiler_params=pltpu.CompilerParams(
            collective_id=0, has_side_effects=True, vmem_limit_bytes=60 * 1024 * 1024
        ),
        cost_estimate=pl.CostEstimate(
            flops=1_200_000_000, bytes_accessed=3_000_000, transcendentals=1_800_000
        ),
        name="shared_prefix",
    )(
        prefix_of_row.reshape(1, 32),
        owner_of_prefix.reshape(1, 64),
        suffix_lengths.reshape(1, 32),
        by_step,
        by_step.reshape(768, 128),
        prefix_keys.reshape(512, 128),
        prefix_values.reshape(512, 128),
        suffix_keys.reshape(3072, 128),
        suffix_values.reshape(3072, 128),
        jnp.transpose(new_keys, (1, 2, 0, 3)).reshape(96, 128),
        jnp.transpose(new_values, (1, 2, 0, 3)).reshape(96, 128),
    )
    ordered = jnp.transpose(gathered.reshape(8, 4, 3, 8, 128), (1, 0, 3, 2, 4))
    return ordered.reshape(4, 64, 3, 128)


def solution(mesh):
    in_specs = (
        P("pre", "head", None, None),
        P("pre", None, "head", None),
        P("pre", None, "head", None),
        P("pre", None, "head", None),
        P("pre", None, "head", None),
        P("pre", None, "head", None),
        P("pre", None, "head", None),
        P("pre"),
        P("pre"),
        P(),
    )
    out_specs = P(("pre", "head"), None, None, None)
    return jax.shard_map(shards, mesh=mesh, in_specs=in_specs, out_specs=out_specs, check_vma=False)
```

```python
import math

import jax
import jax.numpy as jnp
from jax import lax
from jax.experimental import pallas as pl
from jax.experimental.pallas import tpu as pltpu
from jax.sharding import PartitionSpec as P

MESH = pl.DeviceIdType.MESH
masked_score = -1e30
offsets = (0, 7, 1, 6, 2, 5, 3, 4)
return_groups = ((0, 3), (3, 2), (5, 2))


def dot_t(a, b):
    return lax.dot_general(a, b, (((1,), (1,)), ((), ())), preferred_element_type=jnp.float32)


def kernel(
    prefix_hbm,
    owner_hbm,
    len_hbm,
    q4_hbm,
    q2_hbm,
    pk_hbm,
    pv_hbm,
    sk_hbm,
    sv_hbm,
    nk_hbm,
    nv_hbm,
    out_ref,
    prefix_here,
    owner_here,
    len_ref,
    index_rows,
    index_ref,
    qall,
    q2,
    kvk,
    kvv,
    sk,
    sv,
    nk,
    nv,
    qpack,
    osend,
    orecv,
    ssend,
    srecv,
    snew,
    pnew,
    lpart,
    lmax,
    share,
    lsum,
    weights,
    inverse,
    stage,
    load_sem,
    ring_send,
    ring_recv,
    q_send_sem,
    q_recv_sem,
    index_sem,
    o_send_sem,
    o_recv_sem,
    s_send_sem,
    s_recv_sem,
    y_send_sem,
    y_recv_sem,
    own_sem,
    above_here,
    below_here,
    far_q_send_sem,
    far_q_recv_sem,
    far_o_send_sem,
    far_o_recv_sem,
    far_s_send_sem,
    far_s_recv_sem,
):
    pre = lax.axis_index("pre")
    head = lax.axis_index("head")
    z = pre // 8
    me = pre % 8
    plane = z * 8
    right = ((z + 1) % 8) * 8 + me
    left = ((z + 7) % 8) * 8 + me
    column, core = me // 2, me % 2
    ahead = ((column + 1) % 4) * 2 + core
    behind = ((column + 3) % 4) * 2 + core
    opposite = ((column + 2) % 4) * 2 + core
    sibling = column * 2 + 1 - core
    to_log2 = 128 ** (-0.5) * math.log2(math.e)

    barrier = pltpu.get_barrier_semaphore()

    def greet(pre_index, head_index):
        pl.semaphore_signal(
            barrier, inc=1, device_id=(pre_index, head_index), device_id_type=MESH
        )

    above, below = (head + 1) % 8, (head + 7) % 8
    for peer in (left, plane + ahead, plane + behind, plane + sibling):
        greet(peer, head)
    greet(pre, above)
    greet(pre, below)

    loads = [
        pltpu.make_async_copy(a, b, load_sem.at[i])
        for i, (a, b) in enumerate(
            (
                (prefix_hbm, prefix_here),
                (owner_hbm, owner_here),
                (len_hbm, len_ref),
                (q4_hbm, qall.at[me, pl.ds(1, 32)]),
                (q2_hbm, q2),
                (nk_hbm, nk),
                (nv_hbm, nv),
                (sk_hbm, sk),
                (sv_hbm, sv),
                (pk_hbm, kvk.at[0]),
                (pv_hbm, kvv.at[0]),
            )
        )
    ]
    for i in (0, 1, 3):
        loads[i].start()

    def ring(way, hop, which):
        held, own = ((kvk, pk_hbm), (kvv, pv_hbm))[which]
        if way == 0:
            source, target, device = (9 - hop) % 8, 8 - hop, right
        else:
            source, target, device = hop - 1, hop, left
        return pltpu.make_async_remote_copy(
            src_ref=own if hop == 1 else held.at[source],
            dst_ref=held.at[target],
            send_sem=ring_send.at[which],
            recv_sem=ring_recv.at[way, hop - 1, which],
            device_id=(device, head),
            device_id_type=MESH,
        )

    def plane_copy(source, target, blocks, send_sem, recv_sem, i):
        peer = (me + i) % 8
        return pltpu.make_async_remote_copy(
            src_ref=source.at[blocks, peer],
            dst_ref=target.at[blocks, me],
            send_sem=send_sem,
            recv_sem=recv_sem,
            device_id=(plane + peer, head),
            device_id_type=MESH,
        )

    def wait_for(block, sem):
        pltpu.make_async_copy(block, block, sem).wait()

    def query_copy(i, source, rows, peer):
        block = qall.at[source, rows]
        return pltpu.make_async_remote_copy(
            src_ref=block,
            dst_ref=block,
            send_sem=q_send_sem.at[i],
            recv_sem=q_recv_sem.at[i],
            device_id=(plane + peer, head),
            device_id_type=MESH,
        )

    every, first_half, second_half = pl.ds(0, 33), pl.ds(0, 17), pl.ds(17, 16)

    seven = pl.ds(0, 7)

    def part_copy(index, i):
        blocks = pl.ds(*return_groups[index])
        return plane_copy(osend, orecv, blocks, o_send_sem.at[index], o_recv_sem.at[index], i)

    def stat_copy(i):
        return plane_copy(ssend, srecv, seven, s_send_sem, s_recv_sem, i)

    def far_query(way):
        return pltpu.make_async_remote_copy(
            src_ref=qpack.at[7, pl.ds(4 * way, 4)],
            dst_ref=qpack.at[6 - way, pl.ds(8, 4)],
            send_sem=far_q_send_sem.at[way],
            recv_sem=far_q_recv_sem.at[way],
            device_id=((right, left)[way], head),
            device_id_type=MESH,
        )

    def far_copy(source, target, send_sem, recv_sem, d):
        return pltpu.make_async_remote_copy(
            src_ref=source.at[7, d],
            dst_ref=target.at[7, me],
            send_sem=send_sem,
            recv_sem=recv_sem,
            device_id=((left if d < 4 else right) - me + d, head),
            device_id_type=MESH,
        )

    pl.semaphore_wait(barrier, 6)
    ring(0, 1, 0).start()
    for i in (4, 5, 2, 7, 8, 6, 9, 10):
        loads[i].start()

    def token(from_above, step):
        tokens, peer = (above_here, below) if from_above else (below_here, above)
        pl.semaphore_signal(
            tokens.at[step], inc=1, device_id=(pre, peer), device_id_type=MESH
        )

    token(True, 0)
    token(False, 0)

    query_sends = [
        query_copy(0, me, first_half, ahead),
        query_copy(1, me, first_half, behind),
        query_copy(2, me, second_half, ahead),
        query_copy(3, me, second_half, behind),
        query_copy(4, me, every, sibling),
        query_copy(5, behind, first_half, ahead),
        query_copy(6, ahead, second_half, behind),
        query_copy(7, behind, first_half, sibling),
        query_copy(8, ahead, first_half, sibling),
        query_copy(9, behind, second_half, sibling),
        query_copy(10, ahead, second_half, sibling),
        query_copy(11, opposite, first_half, sibling),
        query_copy(12, opposite, second_half, sibling),
    ]

    def hand_on(arrived, onward):
        query_sends[arrived].wait_recv()
        for i in onward:
            query_sends[i].start()

    loads[0].wait()
    qall[me, 0] = jnp.full((3, 8, 128), -1.0, jnp.bfloat16)
    qall[me, 0, 0, :, 0:32] = jnp.broadcast_to(prefix_here[...], (8, 32)).astype(jnp.bfloat16)
    loads[3].wait()
    for copy in query_sends[:5]:
        copy.start()

    loads[1].wait()

    def small_dot(a, b):
        return jnp.dot(
            a.astype(jnp.bfloat16), b.astype(jnp.bfloat16), preferred_element_type=jnp.float32
        )

    def iota(shape, dim):
        return lax.broadcasted_iota(jnp.int32, shape, dim)

    def ones_where(condition):
        return jnp.where(condition, 1.0, 0.0)

    def owner_at(k):
        offset = jnp.where((k & 1) == 1, 8 - ((k + 1) >> 1), k >> 1)
        return ((z + offset) & 7) * 8

    def named_by(d):
        names = qall[d, 0, 0].astype(jnp.float32)[0:1]
        return ones_where(names == iota((64, 128), 0).astype(jnp.float32))

    before = ones_where(iota((128, 128), 0) < iota((128, 128), 1))
    place = iota((64, 64), 0)
    owners = owner_here[...]
    held = ones_where(owners == owner_at(place >> 3) + (place & 7))
    mine = small_dot(held, named_by(me))
    earlier = small_dot(mine, before)
    slots = small_dot(2 * iota((8, 64), 1).astype(jnp.float32), mine) + small_dot(
        jnp.ones((8, 64), jnp.float32), mine * earlier
    )
    index_rows[16:24, :] = slots.astype(jnp.int32)

    ring(0, 1, 1).start()

    loads[4].wait()
    loads[5].wait()
    snew[...] = dot_t(q2[...], nk[...])
    loads[2].wait()
    loads[7].wait()
    loads[8].wait()

    def pair(i):
        rows = pl.ds(i * 48, 48)
        keys = pl.ds(i * 192, 192)
        scores = dot_t(q2[rows, :], sk[keys, :])
        row = lax.broadcasted_iota(jnp.int32, (48, 192), 0)
        lane = lax.broadcasted_iota(jnp.int32, (48, 192), 1)
        low = jnp.where(row < 24, 0, 96)
        high = jnp.where(row < 24, len_ref[0, 2 * i], 96 + len_ref[0, 2 * i + 1])
        scores = jnp.where((lane >= low) & (lane < high), scores, masked_score)
        row = lax.broadcasted_iota(jnp.int32, (48, 96), 0)
        lane = lax.broadcasted_iota(jnp.int32, (48, 96), 1)
        second = row >= 24
        place = lane - jnp.where(second, 2 * i + 1, 2 * i)
        within = jnp.where(second, row - 24, row)
        fresh_ok = (
            (place == 0)
            | ((place == 32) & (within >= 8))
            | ((place == 64) & (within >= 16))
        )
        fresh = jnp.where(fresh_ok, snew[rows, :], masked_score)
        top = jnp.maximum(
            jnp.max(scores, axis=1, keepdims=True), jnp.max(fresh, axis=1, keepdims=True)
        )
        scores = jnp.exp2((scores - top) * to_log2)
        fresh = jnp.exp2((fresh - top) * to_log2)
        lmax[rows, :] = top * to_log2
        lsum[rows, :] = jnp.sum(scores, axis=1, keepdims=True) + jnp.sum(
            fresh, axis=1, keepdims=True
        )
        pnew[rows, :] = fresh.astype(jnp.bfloat16)
        lpart[rows, :] = jnp.dot(
            scores.astype(jnp.bfloat16), sv[keys, :], preferred_element_type=jnp.float32
        )

    def pairs(first):
        for j in range(4):
            pair(first + j)

    def pass_on(way, hop, which):
        ring(way, hop, which).wait_recv()
        if hop < 3:
            ring(way, hop + 1, which).start()

    pairs(0)
    pairs(4)
    pass_on(0, 1, 0)
    ring(1, 1, 0).start()
    hand_on(0, (5, 7))
    hand_on(1, (8,))
    pairs(8)
    hand_on(2, (9,))
    hand_on(3, (6, 10))
    ring(1, 1, 1).start()
    pass_on(0, 1, 1)
    pairs(12)
    loads[6].wait()
    part = lpart[...] + jnp.dot(pnew[...], nv[...], preferred_element_type=jnp.float32)
    lpart[...] = part / lsum[...]
    lmax[...] = lmax[...] + jnp.log2(lsum[...])

    def index_at(table, place, last):
        return jnp.minimum(jnp.maximum(index_ref[table * 8, place], 0), last)

    def pack(k):
        for d in range(8):
            rows = [qall[d, 1 + index_at(rank, d * 8 + k, 31)] for rank in range(2)]
            both = [row.astype(jnp.float32).reshape(24, 128) for row in rows]
            qpack[k, d] = jnp.concatenate(both, axis=0).astype(jnp.bfloat16)

    def sources(k):
        return 12 if k in (5, 6) else 8

    def weigh(k):
        pack(k)
        count = sources(k)
        scores = dot_t(qpack[k, 0:count].reshape(count * 48, 128), kvk[offsets[k]])
        top = jnp.max(scores, axis=1, keepdims=True)
        scores = jnp.exp2((scores - top) * to_log2)
        weights[k, 0 : count * 48] = scores.astype(jnp.bfloat16)
        total = jnp.dot(
            weights[k, 0 : count * 48],
            jnp.ones((512, 128), jnp.bfloat16),
            preferred_element_type=jnp.float32,
        )
        inverse[k, 0 : count * 48] = 1.0 / total
        level = top * to_log2 + jnp.log2(total)
        row = iota((48, 128), 0)
        lane = iota((48, 128), 1)
        for d in range(count):
            block, place = (k, d) if d < 8 else (7, d - 8 + 4 * (6 - k))
            ssend[block, place] = jnp.sum(
                jnp.where(row == lane, level[d * 48 : d * 48 + 48], 0.0), axis=0, keepdims=True
            )
        srecv[k, me] = ssend[k, me]

    def blend(k):
        count = sources(k)
        part = jnp.dot(
            weights[k, 0 : count * 48], kvv[offsets[k]], preferred_element_type=jnp.float32
        )
        part = (part * inverse[k, 0 : count * 48]).astype(jnp.bfloat16).reshape(count, 48, 128)
        osend[k] = part[0:8]
        if count > 8:
            osend[7, 4 * (6 - k) : 4 * (6 - k) + 4] = part[8:12]
        orecv[k, me] = osend[k, me]

    def send_back(index):
        for i in range(1, 8):
            part_copy(index, i).start()

    hand_on(5, (11,))
    hand_on(6, (12,))
    pass_on(1, 1, 0)
    pass_on(0, 2, 0)
    for i in (4, 7, 8, 11):
        query_sends[i].wait_recv()
    here = ones_where(owners == owner_at(iota((8, 64), 0)) + me)
    match = jnp.concatenate(
        [small_dot(here, named_by(d)) for d in range(8)], axis=0
    )
    earlier = small_dot(match, before)
    numbers = iota((8, 128), 1).astype(jnp.bfloat16)
    for rank in range(2):
        chosen = jnp.where(earlier == rank, match, 0.0).astype(jnp.bfloat16)
        index_rows[rank * 8 : rank * 8 + 8, 0:64] = dot_t(numbers, chosen).astype(jnp.int32)
    index_copy = pltpu.make_async_copy(index_rows, index_ref, index_sem)
    index_copy.start()
    for i in (9, 10, 12):
        query_sends[i].wait_recv()
    index_copy.wait()
    loads[9].wait()
    loads[10].wait()
    pack(7)
    for way in range(2):
        far_query(way).start()
    weigh(0)
    blend(0)
    pass_on(1, 1, 1)
    pass_on(0, 2, 1)
    weigh(1)
    blend(1)
    weigh(2)
    blend(2)
    send_back(0)
    pass_on(1, 2, 0)
    pass_on(0, 3, 0)
    pl.semaphore_wait(above_here.at[0], 1)
    token(True, 1)
    pl.semaphore_wait(below_here.at[0], 1)
    token(False, 1)
    weigh(3)
    blend(3)
    weigh(4)
    pass_on(1, 2, 1)
    pass_on(0, 3, 1)
    blend(4)
    send_back(1)

    def far_back(k):
        for d in range(4 * (6 - k), 4 * (6 - k) + 4):
            far_copy(osend, orecv, far_o_send_sem, far_o_recv_sem, d).start()

    for way in range(2):
        far_query(way).wait_recv()
    weigh(5)
    blend(5)
    far_back(5)
    pass_on(1, 3, 0)
    weigh(6)
    for d in range(8):
        far_copy(ssend, srecv, far_s_send_sem, far_s_recv_sem, d).start()
    for i in range(1, 8):
        stat_copy(i).start()
    pl.semaphore_wait(above_here.at[1], 1)
    token(True, 2)
    pl.semaphore_wait(below_here.at[1], 1)
    pass_on(1, 3, 1)
    blend(6)
    far_back(6)
    send_back(2)

    def head_copy(i):
        peer = (head + i) % 8
        return pltpu.make_async_remote_copy(
            src_ref=stage.at[peer],
            dst_ref=out_ref.at[head],
            send_sem=y_send_sem,
            recv_sem=y_recv_sem,
            device_id=(pre, peer),
            device_id_type=MESH,
        )

    def settle(target):
        levels = []
        row = iota((24, 128), 0)
        lane = iota((24, 128), 1)
        for j in range(4):
            slot = index_at(2, target * 4 + j, 127)
            stats = srecv[slot // 16, (slot // 2) % 8]
            levels.append(
                jnp.sum(
                    jnp.where(lane == row + 24 * (slot % 2), stats, 0.0), axis=1, keepdims=True
                )
            )
        levels = jnp.concatenate(levels, axis=0)
        rows = pl.ds(target * 96, 96)
        local = lmax[rows, :]
        top = jnp.maximum(levels, local)
        pre_factor = jnp.exp2(levels - top)
        local_factor = jnp.exp2(local - top)
        inverse_sum = 1.0 / (pre_factor + local_factor)
        share[rows, :] = pre_factor * inverse_sum
        lpart[rows, :] = lpart[rows, :] * (local_factor * inverse_sum)

    def combine(target):
        parts = []
        row = iota((24, 128), 0)
        for j in range(4):
            slot = index_at(2, target * 4 + j, 127)
            both = orecv[slot // 16, (slot // 2) % 8].astype(jnp.float32)
            parts.append(jnp.where(row * 0 + slot % 2 == 0, both[:24], both[24:]))
        rows = pl.ds(pl.multiple_of(target * 96, 96), 96)
        mixed = jnp.concatenate(parts, axis=0) * share[rows, :] + lpart[rows, :]
        stage[target] = mixed.astype(jnp.bfloat16)

    wait_for(srecv.at[seven, seven], s_recv_sem)
    wait_for(srecv.at[7], far_s_recv_sem)
    for target in range(8):
        settle(target)
    for index in range(3):
        wait_for(orecv.at[pl.ds(*return_groups[index]), seven], o_recv_sem.at[index])
    wait_for(orecv.at[7], far_o_recv_sem)
    pl.semaphore_wait(above_here.at[2], 1)
    for batch in ((4, 3), (5, 2), (6, 1), (7, 0)):
        for i in batch:
            combine((head + i) % 8)
        for i in batch:
            if i:
                head_copy(i).start()
    own = pltpu.make_async_copy(stage.at[head], out_ref.at[head], own_sem)
    own.start()

    for which in range(2):
        wait_for((kvk, kvv)[which].at[pl.ds(0, 6)], ring_send.at[which])
    for copy in query_sends:
        copy.wait_send()
    for index in range(3):
        wait_for(osend.at[pl.ds(*return_groups[index]), seven], o_send_sem.at[index])
    wait_for(ssend.at[seven, seven], s_send_sem)
    for way in range(2):
        far_query(way).wait_send()
    wait_for(osend.at[7], far_o_send_sem)
    wait_for(ssend.at[7], far_s_send_sem)
    wait_for(stage.at[seven], y_send_sem)
    own.wait()
    wait_for(out_ref.at[seven], y_recv_sem)


def shards(
    queries,
    prefix_keys,
    prefix_values,
    suffix_keys,
    suffix_values,
    new_keys,
    new_values,
    suffix_lengths,
    prefix_of_row,
    owner_of_prefix,
):
    bf16 = jnp.bfloat16
    by_step = jnp.transpose(queries, (0, 2, 1, 3))
    anywhere = pl.BlockSpec(memory_space=pltpu.HBM)
    dma = pltpu.SemaphoreType.DMA
    gathered = pl.pallas_call(
        kernel,
        out_shape=pltpu.VMEM((8, 96, 128), bf16),
        in_specs=[anywhere] * 11,
        out_specs=pl.BlockSpec(memory_space=pltpu.VMEM),
        scratch_shapes=[
            pltpu.VMEM((1, 32), jnp.int32),
            pltpu.VMEM((1, 64), jnp.int32),
            pltpu.SMEM((1, 32), jnp.int32),
            pltpu.VMEM((24, 128), jnp.int32),
            pltpu.SMEM((24, 128), jnp.int32),
            pltpu.VMEM((8, 33, 3, 8, 128), bf16),
            pltpu.VMEM((768, 128), bf16),
            pltpu.VMEM((8, 512, 128), bf16),
            pltpu.VMEM((8, 512, 128), bf16),
            pltpu.VMEM((3072, 128), bf16),
            pltpu.VMEM((3072, 128), bf16),
            pltpu.VMEM((96, 128), bf16),
            pltpu.VMEM((96, 128), bf16),
            pltpu.VMEM((8, 12, 48, 128), bf16),
            pltpu.VMEM((8, 8, 48, 128), bf16),
            pltpu.VMEM((8, 8, 48, 128), bf16),
            pltpu.VMEM((8, 8, 1, 128), jnp.float32),
            pltpu.VMEM((8, 8, 1, 128), jnp.float32),
            pltpu.VMEM((768, 96), jnp.float32),
            pltpu.VMEM((768, 96), bf16),
            pltpu.VMEM((768, 128), jnp.float32),
            pltpu.VMEM((768, 1), jnp.float32),
            pltpu.VMEM((768, 1), jnp.float32),
            pltpu.VMEM((768, 1), jnp.float32),
            pltpu.VMEM((8, 576, 512), bf16),
            pltpu.VMEM((8, 576, 128), jnp.float32),
            pltpu.VMEM((8, 96, 128), bf16),
            dma((11,)),
            dma((2,)),
            dma((2, 4, 2)),
            dma((13,)),
            dma((13,)),
            dma,
            dma((4,)),
            dma((4,)),
            dma,
            dma,
            dma,
            dma,
            dma,
            pltpu.SemaphoreType.REGULAR((3,)),
            pltpu.SemaphoreType.REGULAR((2,)),
            dma((2,)),
            dma((2,)),
            dma,
            dma,
            dma,
            dma,
        ],
        compiler_params=pltpu.CompilerParams(
            collective_id=0, has_side_effects=True, vmem_limit_bytes=60 * 1024 * 1024
        ),
        cost_estimate=pl.CostEstimate(
            flops=1_200_000_000, bytes_accessed=3_000_000, transcendentals=1_800_000
        ),
        name="shared_prefix",
    )(
        prefix_of_row.reshape(1, 32),
        owner_of_prefix.reshape(1, 64),
        suffix_lengths.reshape(1, 32),
        by_step,
        by_step.reshape(768, 128),
        prefix_keys.reshape(512, 128),
        prefix_values.reshape(512, 128),
        suffix_keys.reshape(3072, 128),
        suffix_values.reshape(3072, 128),
        jnp.transpose(new_keys, (1, 2, 0, 3)).reshape(96, 128),
        jnp.transpose(new_values, (1, 2, 0, 3)).reshape(96, 128),
    )
    ordered = jnp.transpose(gathered.reshape(8, 4, 3, 8, 128), (1, 0, 3, 2, 4))
    return ordered.reshape(4, 64, 3, 128)


def solution(mesh):
    in_specs = (
        P("pre", "head", None, None),
        P("pre", None, "head", None),
        P("pre", None, "head", None),
        P("pre", None, "head", None),
        P("pre", None, "head", None),
        P("pre", None, "head", None),
        P("pre", None, "head", None),
        P("pre"),
        P("pre"),
        P(),
    )
    out_specs = P(("pre", "head"), None, None, None)
    return jax.shard_map(shards, mesh=mesh, in_specs=in_specs, out_specs=out_specs, check_vma=False)
```

```python
import math

import jax
import jax.numpy as jnp
from jax import lax
from jax.experimental import pallas as pl
from jax.experimental.pallas import tpu as pltpu
from jax.sharding import PartitionSpec as P

MESH = pl.DeviceIdType.MESH
masked_score = -1e30
offsets = (0, 1, 7, 2, 6, 3, 5, 4)
return_groups = ((0, 3), (3, 2), (5, 1), (6, 1))


def dot_t(a, b):
    return lax.dot_general(a, b, (((1,), (1,)), ((), ())), preferred_element_type=jnp.float32)


def kernel(
    prefix_hbm,
    owner_hbm,
    len_hbm,
    q4_hbm,
    q2_hbm,
    pk_hbm,
    pv_hbm,
    sk_hbm,
    sv_hbm,
    nk_hbm,
    nv_hbm,
    out_ref,
    prefix_here,
    owner_here,
    len_ref,
    index_rows,
    index_ref,
    qall,
    q2,
    kvk,
    kvv,
    sk,
    sv,
    nk,
    nv,
    qpack,
    osend,
    orecv,
    ssend,
    srecv,
    snew,
    pnew,
    lpart,
    lmax,
    share,
    lsum,
    weights,
    inverse,
    stage,
    load_sem,
    ring_send,
    ring_recv,
    q_send_sem,
    q_recv_sem,
    index_sem,
    o_send_sem,
    o_recv_sem,
    s_send_sem,
    s_recv_sem,
    y_send_sem,
    y_recv_sem,
    own_sem,
    above_here,
    below_here,
    far_q_send_sem,
    far_q_recv_sem,
    far_o_send_sem,
    far_o_recv_sem,
    far_s_send_sem,
    far_s_recv_sem,
):
    pre = lax.axis_index("pre")
    head = lax.axis_index("head")
    z = pre // 8
    me = pre % 8
    plane = z * 8
    right = ((z + 1) % 8) * 8 + me
    left = ((z + 7) % 8) * 8 + me
    column, core = me // 2, me % 2
    ahead = ((column + 1) % 4) * 2 + core
    behind = ((column + 3) % 4) * 2 + core
    opposite = ((column + 2) % 4) * 2 + core
    sibling = column * 2 + 1 - core
    to_log2 = 128 ** (-0.5) * math.log2(math.e)

    barrier = pltpu.get_barrier_semaphore()

    def greet(pre_index, head_index):
        pl.semaphore_signal(
            barrier, inc=1, device_id=(pre_index, head_index), device_id_type=MESH
        )

    above, below = (head + 1) % 8, (head + 7) % 8
    for peer in (right, left, plane + ahead, plane + behind, plane + sibling):
        greet(peer, head)
    greet(pre, above)
    greet(pre, below)

    loads = [
        pltpu.make_async_copy(a, b, load_sem.at[i])
        for i, (a, b) in enumerate(
            (
                (prefix_hbm, prefix_here),
                (owner_hbm, owner_here),
                (len_hbm, len_ref),
                (q4_hbm, qall.at[me, pl.ds(1, 32)]),
                (q2_hbm, q2),
                (nk_hbm, nk),
                (nv_hbm, nv),
                (sk_hbm, sk),
                (sv_hbm, sv),
                (pk_hbm, kvk.at[0]),
                (pv_hbm, kvv.at[0]),
            )
        )
    ]
    for i in (0, 1, 3):
        loads[i].start()

    def ring(way, hop, which):
        held, own = ((kvk, pk_hbm), (kvv, pv_hbm))[which]
        if way == 0:
            source, target, device = (9 - hop) % 8, 8 - hop, right
        else:
            source, target, device = hop - 1, hop, left
        return pltpu.make_async_remote_copy(
            src_ref=own if hop == 1 else held.at[source],
            dst_ref=held.at[target],
            send_sem=ring_send.at[which],
            recv_sem=ring_recv.at[way, hop - 1, which],
            device_id=(device, head),
            device_id_type=MESH,
        )

    def plane_copy(source, target, blocks, send_sem, recv_sem, i):
        peer = (me + i) % 8
        return pltpu.make_async_remote_copy(
            src_ref=source.at[blocks, peer],
            dst_ref=target.at[blocks, me],
            send_sem=send_sem,
            recv_sem=recv_sem,
            device_id=(plane + peer, head),
            device_id_type=MESH,
        )

    def wait_for(block, sem):
        pltpu.make_async_copy(block, block, sem).wait()

    def query_copy(i, source, rows, peer):
        block = qall.at[source, rows]
        return pltpu.make_async_remote_copy(
            src_ref=block,
            dst_ref=block,
            send_sem=q_send_sem.at[i],
            recv_sem=q_recv_sem.at[i],
            device_id=(plane + peer, head),
            device_id_type=MESH,
        )

    every, first_half, second_half = pl.ds(0, 33), pl.ds(0, 17), pl.ds(17, 16)

    seven = pl.ds(0, 7)

    def part_copy(index, i):
        blocks = pl.ds(*return_groups[index])
        return plane_copy(osend, orecv, blocks, o_send_sem.at[index], o_recv_sem.at[index], i)

    def stat_copy(i):
        return plane_copy(ssend, srecv, seven, s_send_sem, s_recv_sem, i)

    def far_query(way):
        return pltpu.make_async_remote_copy(
            src_ref=qpack.at[7, pl.ds(4 * way, 4)],
            dst_ref=qpack.at[5 + way, pl.ds(8, 4)],
            send_sem=far_q_send_sem.at[way],
            recv_sem=far_q_recv_sem.at[way],
            device_id=((right, left)[way], head),
            device_id_type=MESH,
        )

    def far_copy(source, target, send_sem, recv_sem, d):
        return pltpu.make_async_remote_copy(
            src_ref=source.at[7, d],
            dst_ref=target.at[7, me],
            send_sem=send_sem,
            recv_sem=recv_sem,
            device_id=((left if d < 4 else right) - me + d, head),
            device_id_type=MESH,
        )

    pl.semaphore_wait(barrier, 7)
    for way in range(2):
        ring(way, 1, 0).start()
    for i in (4, 5, 2, 7, 8, 6, 9, 10):
        loads[i].start()

    def token(from_above, step):
        tokens, peer = (above_here, below) if from_above else (below_here, above)
        pl.semaphore_signal(
            tokens.at[step], inc=1, device_id=(pre, peer), device_id_type=MESH
        )

    token(True, 0)
    token(False, 0)

    query_sends = [
        query_copy(0, me, first_half, ahead),
        query_copy(1, me, first_half, behind),
        query_copy(2, me, second_half, ahead),
        query_copy(3, me, second_half, behind),
        query_copy(4, me, every, sibling),
        query_copy(5, behind, first_half, ahead),
        query_copy(6, ahead, second_half, behind),
        query_copy(7, behind, first_half, sibling),
        query_copy(8, ahead, first_half, sibling),
        query_copy(9, behind, second_half, sibling),
        query_copy(10, ahead, second_half, sibling),
        query_copy(11, opposite, first_half, sibling),
        query_copy(12, opposite, second_half, sibling),
    ]

    def hand_on(arrived, onward):
        query_sends[arrived].wait_recv()
        for i in onward:
            query_sends[i].start()

    loads[0].wait()
    qall[me, 0] = jnp.full((3, 8, 128), -1.0, jnp.bfloat16)
    qall[me, 0, 0, :, 0:32] = jnp.broadcast_to(prefix_here[...], (8, 32)).astype(jnp.bfloat16)
    loads[3].wait()
    for copy in query_sends[:5]:
        copy.start()

    loads[1].wait()

    def small_dot(a, b):
        return jnp.dot(
            a.astype(jnp.bfloat16), b.astype(jnp.bfloat16), preferred_element_type=jnp.float32
        )

    def iota(shape, dim):
        return lax.broadcasted_iota(jnp.int32, shape, dim)

    def ones_where(condition):
        return jnp.where(condition, 1.0, 0.0)

    def owner_at(k):
        offset = jnp.zeros_like(k)
        for place, value in enumerate(offsets):
            offset = jnp.where(k == place, value, offset)
        return ((z + offset) & 7) * 8

    def named_by(d):
        names = qall[d, 0, 0].astype(jnp.float32)[0:1]
        return ones_where(names == iota((64, 128), 0).astype(jnp.float32))

    before = ones_where(iota((128, 128), 0) < iota((128, 128), 1))
    place = iota((64, 64), 0)
    owners = owner_here[...]
    held = ones_where(owners == owner_at(place >> 3) + (place & 7))
    mine = small_dot(held, named_by(me))
    earlier = small_dot(mine, before)
    slots = small_dot(2 * iota((8, 64), 1).astype(jnp.float32), mine) + small_dot(
        jnp.ones((8, 64), jnp.float32), mine * earlier
    )
    index_rows[16:24, :] = slots.astype(jnp.int32)

    for way in range(2):
        ring(way, 1, 1).start()

    loads[4].wait()
    loads[5].wait()
    snew[...] = dot_t(q2[...], nk[...])
    loads[2].wait()
    loads[7].wait()
    loads[8].wait()

    def pair(i):
        rows = pl.ds(i * 48, 48)
        keys = pl.ds(i * 192, 192)
        scores = dot_t(q2[rows, :], sk[keys, :])
        row = lax.broadcasted_iota(jnp.int32, (48, 192), 0)
        lane = lax.broadcasted_iota(jnp.int32, (48, 192), 1)
        low = jnp.where(row < 24, 0, 96)
        high = jnp.where(row < 24, len_ref[0, 2 * i], 96 + len_ref[0, 2 * i + 1])
        scores = jnp.where((lane >= low) & (lane < high), scores, masked_score)
        row = lax.broadcasted_iota(jnp.int32, (48, 96), 0)
        lane = lax.broadcasted_iota(jnp.int32, (48, 96), 1)
        second = row >= 24
        place = lane - jnp.where(second, 2 * i + 1, 2 * i)
        within = jnp.where(second, row - 24, row)
        fresh_ok = (
            (place == 0)
            | ((place == 32) & (within >= 8))
            | ((place == 64) & (within >= 16))
        )
        fresh = jnp.where(fresh_ok, snew[rows, :], masked_score)
        top = jnp.maximum(
            jnp.max(scores, axis=1, keepdims=True), jnp.max(fresh, axis=1, keepdims=True)
        )
        scores = jnp.exp2((scores - top) * to_log2)
        fresh = jnp.exp2((fresh - top) * to_log2)
        lmax[rows, :] = top * to_log2
        lsum[rows, :] = jnp.sum(scores, axis=1, keepdims=True) + jnp.sum(
            fresh, axis=1, keepdims=True
        )
        pnew[rows, :] = fresh.astype(jnp.bfloat16)
        lpart[rows, :] = jnp.dot(
            scores.astype(jnp.bfloat16), sv[keys, :], preferred_element_type=jnp.float32
        )

    def pairs(first):
        for j in range(4):
            pair(first + j)

    def pass_on(hop, which):
        for way in (1, 0):
            ring(way, hop, which).wait_recv()
            if hop < 3:
                ring(way, hop + 1, which).start()

    pairs(0)
    pairs(4)
    pass_on(1, 0)
    hand_on(0, (5, 7))
    hand_on(1, (8,))
    pairs(8)
    hand_on(2, (9,))
    hand_on(3, (6, 10))
    pass_on(1, 1)
    pairs(12)
    loads[6].wait()
    part = lpart[...] + jnp.dot(pnew[...], nv[...], preferred_element_type=jnp.float32)
    lpart[...] = part / lsum[...]
    lmax[...] = lmax[...] + jnp.log2(lsum[...])

    def index_at(table, place, last):
        return jnp.minimum(jnp.maximum(index_ref[table * 8, place], 0), last)

    def pack(k):
        for d in range(8):
            rows = [qall[d, 1 + index_at(rank, d * 8 + k, 31)] for rank in range(2)]
            both = [row.astype(jnp.float32).reshape(24, 128) for row in rows]
            qpack[k, d] = jnp.concatenate(both, axis=0).astype(jnp.bfloat16)

    def sources(k):
        return 12 if k in (5, 6) else 8

    def weigh(k):
        pack(k)
        count = sources(k)
        scores = dot_t(qpack[k, 0:count].reshape(count * 48, 128), kvk[offsets[k]])
        top = jnp.max(scores, axis=1, keepdims=True)
        scores = jnp.exp2((scores - top) * to_log2)
        weights[k, 0 : count * 48] = scores.astype(jnp.bfloat16)
        total = jnp.dot(
            weights[k, 0 : count * 48],
            jnp.ones((512, 128), jnp.bfloat16),
            preferred_element_type=jnp.float32,
        )
        inverse[k, 0 : count * 48] = 1.0 / total
        level = top * to_log2 + jnp.log2(total)
        row = iota((48, 128), 0)
        lane = iota((48, 128), 1)
        for d in range(count):
            block, place = (k, d) if d < 8 else (7, d - 8 + 4 * (k - 5))
            ssend[block, place] = jnp.sum(
                jnp.where(row == lane, level[d * 48 : d * 48 + 48], 0.0), axis=0, keepdims=True
            )
        srecv[k, me] = ssend[k, me]

    def blend(k):
        count = sources(k)
        part = jnp.dot(
            weights[k, 0 : count * 48], kvv[offsets[k]], preferred_element_type=jnp.float32
        )
        part = (part * inverse[k, 0 : count * 48]).astype(jnp.bfloat16).reshape(count, 48, 128)
        osend[k] = part[0:8]
        if count > 8:
            osend[7, 4 * (k - 5) : 4 * (k - 5) + 4] = part[8:12]
        orecv[k, me] = osend[k, me]

    def send_back(index):
        for i in range(1, 8):
            part_copy(index, i).start()

    hand_on(5, (11,))
    hand_on(6, (12,))
    pass_on(2, 0)
    for i in (4, 7, 8, 11):
        query_sends[i].wait_recv()
    here = ones_where(owners == owner_at(iota((8, 64), 0)) + me)
    match = jnp.concatenate(
        [small_dot(here, named_by(d)) for d in range(8)], axis=0
    )
    earlier = small_dot(match, before)
    numbers = iota((8, 128), 1).astype(jnp.bfloat16)
    for rank in range(2):
        chosen = jnp.where(earlier == rank, match, 0.0).astype(jnp.bfloat16)
        index_rows[rank * 8 : rank * 8 + 8, 0:64] = dot_t(numbers, chosen).astype(jnp.int32)
    index_copy = pltpu.make_async_copy(index_rows, index_ref, index_sem)
    index_copy.start()
    for i in (9, 10, 12):
        query_sends[i].wait_recv()
    index_copy.wait()
    loads[9].wait()
    loads[10].wait()
    pack(7)
    for way in range(2):
        far_query(way).start()
    weigh(0)
    blend(0)
    pass_on(2, 1)
    weigh(1)
    blend(1)
    weigh(2)
    blend(2)
    send_back(0)
    pass_on(3, 0)
    pl.semaphore_wait(above_here.at[0], 1)
    token(True, 1)
    pl.semaphore_wait(below_here.at[0], 1)
    token(False, 1)
    weigh(3)
    weigh(4)
    blend(3)
    blend(4)
    send_back(1)
    for way in range(2):
        far_query(way).wait_recv()
    weigh(5)
    weigh(6)
    for d in range(8):
        far_copy(ssend, srecv, far_s_send_sem, far_s_recv_sem, d).start()
    for i in range(1, 8):
        stat_copy(i).start()
    pl.semaphore_wait(above_here.at[1], 1)
    token(True, 2)
    pl.semaphore_wait(below_here.at[1], 1)
    for k in (5, 6):
        ring(6 - k, 3, 1).wait_recv()
        blend(k)
        for d in range(4 * (k - 5), 4 * (k - 5) + 4):
            far_copy(osend, orecv, far_o_send_sem, far_o_recv_sem, d).start()
        send_back(k - 3)

    def head_copy(i):
        peer = (head + i) % 8
        return pltpu.make_async_remote_copy(
            src_ref=stage.at[peer],
            dst_ref=out_ref.at[head],
            send_sem=y_send_sem,
            recv_sem=y_recv_sem,
            device_id=(pre, peer),
            device_id_type=MESH,
        )

    def settle(target):
        levels = []
        row = iota((24, 128), 0)
        lane = iota((24, 128), 1)
        for j in range(4):
            slot = index_at(2, target * 4 + j, 127)
            stats = srecv[slot // 16, (slot // 2) % 8]
            levels.append(
                jnp.sum(
                    jnp.where(lane == row + 24 * (slot % 2), stats, 0.0), axis=1, keepdims=True
                )
            )
        levels = jnp.concatenate(levels, axis=0)
        rows = pl.ds(target * 96, 96)
        local = lmax[rows, :]
        top = jnp.maximum(levels, local)
        pre_factor = jnp.exp2(levels - top)
        local_factor = jnp.exp2(local - top)
        inverse_sum = 1.0 / (pre_factor + local_factor)
        share[rows, :] = pre_factor * inverse_sum
        lpart[rows, :] = lpart[rows, :] * (local_factor * inverse_sum)

    def combine(target):
        parts = []
        row = iota((24, 128), 0)
        for j in range(4):
            slot = index_at(2, target * 4 + j, 127)
            both = orecv[slot // 16, (slot // 2) % 8].astype(jnp.float32)
            parts.append(jnp.where(row * 0 + slot % 2 == 0, both[:24], both[24:]))
        rows = pl.ds(pl.multiple_of(target * 96, 96), 96)
        mixed = jnp.concatenate(parts, axis=0) * share[rows, :] + lpart[rows, :]
        stage[target] = mixed.astype(jnp.bfloat16)

    wait_for(srecv.at[seven, seven], s_recv_sem)
    wait_for(srecv.at[7], far_s_recv_sem)
    for target in range(8):
        settle(target)
    for index in range(4):
        wait_for(orecv.at[pl.ds(*return_groups[index]), seven], o_recv_sem.at[index])
    wait_for(orecv.at[7], far_o_recv_sem)
    pl.semaphore_wait(above_here.at[2], 1)
    for batch in ((4, 3), (5, 2), (6, 1), (7, 0)):
        for i in batch:
            combine((head + i) % 8)
        for i in batch:
            if i:
                head_copy(i).start()
    own = pltpu.make_async_copy(stage.at[head], out_ref.at[head], own_sem)
    own.start()

    for which in range(2):
        wait_for((kvk, kvv)[which].at[pl.ds(0, 6)], ring_send.at[which])
    for copy in query_sends:
        copy.wait_send()
    for index in range(4):
        wait_for(osend.at[pl.ds(*return_groups[index]), seven], o_send_sem.at[index])
    wait_for(ssend.at[seven, seven], s_send_sem)
    for way in range(2):
        far_query(way).wait_send()
    wait_for(osend.at[7], far_o_send_sem)
    wait_for(ssend.at[7], far_s_send_sem)
    wait_for(stage.at[seven], y_send_sem)
    own.wait()
    wait_for(out_ref.at[seven], y_recv_sem)


def shards(
    queries,
    prefix_keys,
    prefix_values,
    suffix_keys,
    suffix_values,
    new_keys,
    new_values,
    suffix_lengths,
    prefix_of_row,
    owner_of_prefix,
):
    bf16 = jnp.bfloat16
    by_step = jnp.transpose(queries, (0, 2, 1, 3))
    anywhere = pl.BlockSpec(memory_space=pltpu.HBM)
    dma = pltpu.SemaphoreType.DMA
    gathered = pl.pallas_call(
        kernel,
        out_shape=pltpu.VMEM((8, 96, 128), bf16),
        in_specs=[anywhere] * 11,
        out_specs=pl.BlockSpec(memory_space=pltpu.VMEM),
        scratch_shapes=[
            pltpu.VMEM((1, 32), jnp.int32),
            pltpu.VMEM((1, 64), jnp.int32),
            pltpu.SMEM((1, 32), jnp.int32),
            pltpu.VMEM((24, 128), jnp.int32),
            pltpu.SMEM((24, 128), jnp.int32),
            pltpu.VMEM((8, 33, 3, 8, 128), bf16),
            pltpu.VMEM((768, 128), bf16),
            pltpu.VMEM((8, 512, 128), bf16),
            pltpu.VMEM((8, 512, 128), bf16),
            pltpu.VMEM((3072, 128), bf16),
            pltpu.VMEM((3072, 128), bf16),
            pltpu.VMEM((96, 128), bf16),
            pltpu.VMEM((96, 128), bf16),
            pltpu.VMEM((8, 12, 48, 128), bf16),
            pltpu.VMEM((8, 8, 48, 128), bf16),
            pltpu.VMEM((8, 8, 48, 128), bf16),
            pltpu.VMEM((8, 8, 1, 128), jnp.float32),
            pltpu.VMEM((8, 8, 1, 128), jnp.float32),
            pltpu.VMEM((768, 96), jnp.float32),
            pltpu.VMEM((768, 96), bf16),
            pltpu.VMEM((768, 128), jnp.float32),
            pltpu.VMEM((768, 1), jnp.float32),
            pltpu.VMEM((768, 1), jnp.float32),
            pltpu.VMEM((768, 1), jnp.float32),
            pltpu.VMEM((8, 576, 512), bf16),
            pltpu.VMEM((8, 576, 128), jnp.float32),
            pltpu.VMEM((8, 96, 128), bf16),
            dma((11,)),
            dma((2,)),
            dma((2, 4, 2)),
            dma((13,)),
            dma((13,)),
            dma,
            dma((4,)),
            dma((4,)),
            dma,
            dma,
            dma,
            dma,
            dma,
            pltpu.SemaphoreType.REGULAR((3,)),
            pltpu.SemaphoreType.REGULAR((2,)),
            dma((2,)),
            dma((2,)),
            dma,
            dma,
            dma,
            dma,
        ],
        compiler_params=pltpu.CompilerParams(
            collective_id=0, has_side_effects=True, vmem_limit_bytes=60 * 1024 * 1024
        ),
        cost_estimate=pl.CostEstimate(
            flops=1_200_000_000, bytes_accessed=3_000_000, transcendentals=1_800_000
        ),
        name="shared_prefix",
    )(
        prefix_of_row.reshape(1, 32),
        owner_of_prefix.reshape(1, 64),
        suffix_lengths.reshape(1, 32),
        by_step,
        by_step.reshape(768, 128),
        prefix_keys.reshape(512, 128),
        prefix_values.reshape(512, 128),
        suffix_keys.reshape(3072, 128),
        suffix_values.reshape(3072, 128),
        jnp.transpose(new_keys, (1, 2, 0, 3)).reshape(96, 128),
        jnp.transpose(new_values, (1, 2, 0, 3)).reshape(96, 128),
    )
    ordered = jnp.transpose(gathered.reshape(8, 4, 3, 8, 128), (1, 0, 3, 2, 4))
    return ordered.reshape(4, 64, 3, 128)


def solution(mesh):
    in_specs = (
        P("pre", "head", None, None),
        P("pre", None, "head", None),
        P("pre", None, "head", None),
        P("pre", None, "head", None),
        P("pre", None, "head", None),
        P("pre", None, "head", None),
        P("pre", None, "head", None),
        P("pre"),
        P("pre"),
        P(),
    )
    out_specs = P(("pre", "head"), None, None, None)
    return jax.shard_map(shards, mesh=mesh, in_specs=in_specs, out_specs=out_specs, check_vma=False)
```

```python
import math

import jax
import jax.numpy as jnp
from jax import lax
from jax.experimental import pallas as pl
from jax.experimental.pallas import tpu as pltpu
from jax.sharding import PartitionSpec as P

MESH = pl.DeviceIdType.MESH
masked_score = -1e30
offsets = (0, 1, 7, 2, 6, 3, 5, 4)
return_groups = ((0, 3), (3, 2), (5, 2))


def dot_t(a, b):
    return lax.dot_general(a, b, (((1,), (1,)), ((), ())), preferred_element_type=jnp.float32)


def kernel(
    prefix_hbm,
    owner_hbm,
    len_hbm,
    q4_hbm,
    q2_hbm,
    pk_hbm,
    pv_hbm,
    sk_hbm,
    sv_hbm,
    nk_hbm,
    nv_hbm,
    out_ref,
    prefix_here,
    owner_here,
    len_ref,
    index_rows,
    index_ref,
    qall,
    q2,
    kvk,
    kvv,
    sk,
    sv,
    nk,
    nv,
    qpack,
    osend,
    orecv,
    ssend,
    srecv,
    snew,
    pnew,
    lpart,
    lmax,
    share,
    lsum,
    weights,
    inverse,
    stage,
    load_sem,
    ring_send,
    ring_recv,
    q_send_sem,
    q_recv_sem,
    index_sem,
    o_send_sem,
    o_recv_sem,
    s_send_sem,
    s_recv_sem,
    y_send_sem,
    y_recv_sem,
    own_sem,
    above_here,
    below_here,
    lower_here,
    far_q_send_sem,
    far_q_recv_sem,
    far_o_send_sem,
    far_o_recv_sem,
    far_s_send_sem,
    far_s_recv_sem,
):
    pre = lax.axis_index("pre")
    head = lax.axis_index("head")
    z = pre // 8
    me = pre % 8
    plane = z * 8
    right = ((z + 1) % 8) * 8 + me
    left = ((z + 7) % 8) * 8 + me
    column, core = me // 2, me % 2
    ahead = ((column + 1) % 4) * 2 + core
    behind = ((column + 3) % 4) * 2 + core
    opposite = ((column + 2) % 4) * 2 + core
    sibling = column * 2 + 1 - core
    to_log2 = 128 ** (-0.5) * math.log2(math.e)

    barrier = pltpu.get_barrier_semaphore()

    def greet(pre_index, head_index):
        pl.semaphore_signal(
            barrier, inc=1, device_id=(pre_index, head_index), device_id_type=MESH
        )

    above, below = (head + 1) % 8, (head + 7) % 8
    for peer in (left, plane + ahead, plane + behind, plane + sibling):
        greet(peer, head)
    greet(pre, above)
    greet(pre, below)

    loads = [
        pltpu.make_async_copy(a, b, load_sem.at[i])
        for i, (a, b) in enumerate(
            (
                (prefix_hbm, prefix_here),
                (owner_hbm, owner_here),
                (len_hbm, len_ref),
                (q4_hbm, qall.at[me, pl.ds(1, 32)]),
                (q2_hbm, q2),
                (nk_hbm, nk),
                (nv_hbm, nv),
                (sk_hbm, sk),
                (sv_hbm, sv),
                (pk_hbm, kvk.at[0]),
                (pv_hbm, kvv.at[0]),
            )
        )
    ]
    for i in (0, 1, 3):
        loads[i].start()

    def ring(way, hop, which):
        held, own = ((kvk, pk_hbm), (kvv, pv_hbm))[which]
        if way == 0:
            source, target, device = (9 - hop) % 8, 8 - hop, right
        else:
            source, target, device = hop - 1, hop, left
        return pltpu.make_async_remote_copy(
            src_ref=own if hop == 1 else held.at[source],
            dst_ref=held.at[target],
            send_sem=ring_send.at[which],
            recv_sem=ring_recv.at[way, hop - 1, which],
            device_id=(device, head),
            device_id_type=MESH,
        )

    def plane_copy(source, target, blocks, send_sem, recv_sem, i):
        peer = (me + i) % 8
        return pltpu.make_async_remote_copy(
            src_ref=source.at[blocks, peer],
            dst_ref=target.at[blocks, me],
            send_sem=send_sem,
            recv_sem=recv_sem,
            device_id=(plane + peer, head),
            device_id_type=MESH,
        )

    def wait_for(block, sem):
        pltpu.make_async_copy(block, block, sem).wait()

    def query_copy(i, source, rows, peer):
        block = qall.at[source, rows]
        return pltpu.make_async_remote_copy(
            src_ref=block,
            dst_ref=block,
            send_sem=q_send_sem.at[i],
            recv_sem=q_recv_sem.at[i],
            device_id=(plane + peer, head),
            device_id_type=MESH,
        )

    every, first_half, second_half = pl.ds(0, 33), pl.ds(0, 17), pl.ds(17, 16)

    seven = pl.ds(0, 7)

    def part_copy(index, i):
        blocks = pl.ds(*return_groups[index])
        return plane_copy(osend, orecv, blocks, o_send_sem.at[index], o_recv_sem.at[index], i)

    def stat_copy(i):
        return plane_copy(ssend, srecv, seven, s_send_sem, s_recv_sem, i)

    def far_query(way):
        return pltpu.make_async_remote_copy(
            src_ref=qpack.at[7, pl.ds(4 * way, 4)],
            dst_ref=qpack.at[5 + way, pl.ds(8, 4)],
            send_sem=far_q_send_sem.at[way],
            recv_sem=far_q_recv_sem.at[way],
            device_id=((right, left)[way], head),
            device_id_type=MESH,
        )

    def far_copy(source, target, send_sem, recv_sem, d):
        return pltpu.make_async_remote_copy(
            src_ref=source.at[7, d],
            dst_ref=target.at[7, me],
            send_sem=send_sem,
            recv_sem=recv_sem,
            device_id=((left if d < 4 else right) - me + d, head),
            device_id_type=MESH,
        )

    pl.semaphore_wait(barrier, 6)
    ring(0, 1, 0).start()
    pl.semaphore_signal(lower_here, inc=1, device_id=(right, head), device_id_type=MESH)
    for i in (4, 5, 2, 7, 8, 6, 9, 10):
        loads[i].start()

    def token(from_above, step):
        tokens, peer = (above_here, below) if from_above else (below_here, above)
        pl.semaphore_signal(
            tokens.at[step], inc=1, device_id=(pre, peer), device_id_type=MESH
        )

    token(True, 0)
    token(False, 0)

    query_sends = [
        query_copy(0, me, first_half, ahead),
        query_copy(1, me, first_half, behind),
        query_copy(2, me, second_half, ahead),
        query_copy(3, me, second_half, behind),
        query_copy(4, me, every, sibling),
        query_copy(5, behind, first_half, ahead),
        query_copy(6, ahead, second_half, behind),
        query_copy(7, behind, first_half, sibling),
        query_copy(8, ahead, first_half, sibling),
        query_copy(9, behind, second_half, sibling),
        query_copy(10, ahead, second_half, sibling),
        query_copy(11, opposite, first_half, sibling),
        query_copy(12, opposite, second_half, sibling),
    ]

    def hand_on(arrived, onward):
        query_sends[arrived].wait_recv()
        for i in onward:
            query_sends[i].start()

    loads[0].wait()
    qall[me, 0] = jnp.full((3, 8, 128), -1.0, jnp.bfloat16)
    qall[me, 0, 0, :, 0:32] = jnp.broadcast_to(prefix_here[...], (8, 32)).astype(jnp.bfloat16)
    loads[3].wait()
    for copy in query_sends[:5]:
        copy.start()

    loads[1].wait()

    def small_dot(a, b):
        return jnp.dot(
            a.astype(jnp.bfloat16), b.astype(jnp.bfloat16), preferred_element_type=jnp.float32
        )

    def iota(shape, dim):
        return lax.broadcasted_iota(jnp.int32, shape, dim)

    def ones_where(condition):
        return jnp.where(condition, 1.0, 0.0)

    def owner_at(k):
        offset = jnp.zeros_like(k)
        for place, value in enumerate(offsets):
            offset = jnp.where(k == place, value, offset)
        return ((z + offset) & 7) * 8

    def named_by(d):
        names = qall[d, 0, 0].astype(jnp.float32)[0:1]
        return ones_where(names == iota((64, 128), 0).astype(jnp.float32))

    before = ones_where(iota((128, 128), 0) < iota((128, 128), 1))
    place = iota((64, 64), 0)
    owners = owner_here[...]
    held = ones_where(owners == owner_at(place >> 3) + (place & 7))
    mine = small_dot(held, named_by(me))
    earlier = small_dot(mine, before)
    slots = small_dot(2 * iota((8, 64), 1).astype(jnp.float32), mine) + small_dot(
        jnp.ones((8, 64), jnp.float32), mine * earlier
    )
    index_rows[16:24, :] = slots.astype(jnp.int32)

    ring(0, 1, 1).start()
    pl.semaphore_wait(lower_here, 1)
    ring(1, 1, 0).start()

    loads[4].wait()
    loads[5].wait()
    snew[...] = dot_t(q2[...], nk[...])
    loads[2].wait()
    loads[7].wait()
    loads[8].wait()

    def pair(i):
        rows = pl.ds(i * 48, 48)
        keys = pl.ds(i * 192, 192)
        scores = dot_t(q2[rows, :], sk[keys, :])
        row = lax.broadcasted_iota(jnp.int32, (48, 192), 0)
        lane = lax.broadcasted_iota(jnp.int32, (48, 192), 1)
        low = jnp.where(row < 24, 0, 96)
        high = jnp.where(row < 24, len_ref[0, 2 * i], 96 + len_ref[0, 2 * i + 1])
        scores = jnp.where((lane >= low) & (lane < high), scores, masked_score)
        row = lax.broadcasted_iota(jnp.int32, (48, 96), 0)
        lane = lax.broadcasted_iota(jnp.int32, (48, 96), 1)
        second = row >= 24
        place = lane - jnp.where(second, 2 * i + 1, 2 * i)
        within = jnp.where(second, row - 24, row)
        fresh_ok = (
            (place == 0)
            | ((place == 32) & (within >= 8))
            | ((place == 64) & (within >= 16))
        )
        fresh = jnp.where(fresh_ok, snew[rows, :], masked_score)
        top = jnp.maximum(
            jnp.max(scores, axis=1, keepdims=True), jnp.max(fresh, axis=1, keepdims=True)
        )
        scores = jnp.exp2((scores - top) * to_log2)
        fresh = jnp.exp2((fresh - top) * to_log2)
        lmax[rows, :] = top * to_log2
        lsum[rows, :] = jnp.sum(scores, axis=1, keepdims=True) + jnp.sum(
            fresh, axis=1, keepdims=True
        )
        pnew[rows, :] = fresh.astype(jnp.bfloat16)
        lpart[rows, :] = jnp.dot(
            scores.astype(jnp.bfloat16), sv[keys, :], preferred_element_type=jnp.float32
        )

    def pairs(first):
        for j in range(4):
            pair(first + j)

    def pass_on(hop, which):
        for way in (1, 0):
            ring(way, hop, which).wait_recv()
            if hop < 3:
                ring(way, hop + 1, which).start()

    pairs(0)
    ring(1, 1, 1).start()
    pairs(4)
    pass_on(1, 0)
    hand_on(0, (5, 7))
    hand_on(1, (8,))
    pairs(8)
    hand_on(2, (9,))
    hand_on(3, (6, 10))
    pass_on(1, 1)
    pairs(12)
    loads[6].wait()
    part = lpart[...] + jnp.dot(pnew[...], nv[...], preferred_element_type=jnp.float32)
    lpart[...] = part / lsum[...]
    lmax[...] = lmax[...] + jnp.log2(lsum[...])

    def index_at(table, place, last):
        return jnp.minimum(jnp.maximum(index_ref[table * 8, place], 0), last)

    def pack(k):
        for d in range(8):
            rows = [qall[d, 1 + index_at(rank, d * 8 + k, 31)] for rank in range(2)]
            both = [row.astype(jnp.float32).reshape(24, 128) for row in rows]
            qpack[k, d] = jnp.concatenate(both, axis=0).astype(jnp.bfloat16)

    def sources(k):
        return 12 if k in (5, 6) else 8

    def weigh(k):
        pack(k)
        count = sources(k)
        scores = dot_t(qpack[k, 0:count].reshape(count * 48, 128), kvk[offsets[k]])
        top = jnp.max(scores, axis=1, keepdims=True)
        scores = jnp.exp2((scores - top) * to_log2)
        weights[k, 0 : count * 48] = scores.astype(jnp.bfloat16)
        total = jnp.dot(
            weights[k, 0 : count * 48],
            jnp.ones((512, 128), jnp.bfloat16),
            preferred_element_type=jnp.float32,
        )
        inverse[k, 0 : count * 48] = 1.0 / total
        level = top * to_log2 + jnp.log2(total)
        row = iota((48, 128), 0)
        lane = iota((48, 128), 1)
        for d in range(count):
            block, place = (k, d) if d < 8 else (7, d - 8 + 4 * (k - 5))
            ssend[block, place] = jnp.sum(
                jnp.where(row == lane, level[d * 48 : d * 48 + 48], 0.0), axis=0, keepdims=True
            )
        srecv[k, me] = ssend[k, me]

    def blend(k):
        count = sources(k)
        part = jnp.dot(
            weights[k, 0 : count * 48], kvv[offsets[k]], preferred_element_type=jnp.float32
        )
        part = (part * inverse[k, 0 : count * 48]).astype(jnp.bfloat16).reshape(count, 48, 128)
        osend[k] = part[0:8]
        if count > 8:
            osend[7, 4 * (k - 5) : 4 * (k - 5) + 4] = part[8:12]
        orecv[k, me] = osend[k, me]

    def send_back(index):
        for i in range(1, 8):
            part_copy(index, i).start()

    hand_on(5, (11,))
    hand_on(6, (12,))
    pass_on(2, 0)
    for i in (4, 7, 8, 11):
        query_sends[i].wait_recv()
    here = ones_where(owners == owner_at(iota((8, 64), 0)) + me)
    match = jnp.concatenate(
        [small_dot(here, named_by(d)) for d in range(8)], axis=0
    )
    earlier = small_dot(match, before)
    numbers = iota((8, 128), 1).astype(jnp.bfloat16)
    for rank in range(2):
        chosen = jnp.where(earlier == rank, match, 0.0).astype(jnp.bfloat16)
        index_rows[rank * 8 : rank * 8 + 8, 0:64] = dot_t(numbers, chosen).astype(jnp.int32)
    index_copy = pltpu.make_async_copy(index_rows, index_ref, index_sem)
    index_copy.start()
    for i in (9, 10, 12):
        query_sends[i].wait_recv()
    index_copy.wait()
    loads[9].wait()
    loads[10].wait()
    pack(7)
    for way in range(2):
        far_query(way).start()
    weigh(0)
    blend(0)
    pass_on(2, 1)
    weigh(1)
    blend(1)
    weigh(2)
    blend(2)
    send_back(0)
    pass_on(3, 0)
    pl.semaphore_wait(above_here.at[0], 1)
    token(True, 1)
    pl.semaphore_wait(below_here.at[0], 1)
    token(False, 1)
    weigh(3)
    weigh(4)
    blend(3)
    blend(4)
    send_back(1)
    for way in range(2):
        far_query(way).wait_recv()
    weigh(5)
    weigh(6)
    for d in range(8):
        far_copy(ssend, srecv, far_s_send_sem, far_s_recv_sem, d).start()
    for i in range(1, 8):
        stat_copy(i).start()
    pl.semaphore_wait(above_here.at[1], 1)
    token(True, 2)
    pl.semaphore_wait(below_here.at[1], 1)
    for k in (5, 6):
        ring(6 - k, 3, 1).wait_recv()
        blend(k)
        for d in range(4 * (k - 5), 4 * (k - 5) + 4):
            far_copy(osend, orecv, far_o_send_sem, far_o_recv_sem, d).start()
    send_back(2)

    def head_copy(i):
        peer = (head + i) % 8
        return pltpu.make_async_remote_copy(
            src_ref=stage.at[peer],
            dst_ref=out_ref.at[head],
            send_sem=y_send_sem,
            recv_sem=y_recv_sem,
            device_id=(pre, peer),
            device_id_type=MESH,
        )

    def settle(target):
        levels = []
        row = iota((24, 128), 0)
        lane = iota((24, 128), 1)
        for j in range(4):
            slot = index_at(2, target * 4 + j, 127)
            stats = srecv[slot // 16, (slot // 2) % 8]
            levels.append(
                jnp.sum(
                    jnp.where(lane == row + 24 * (slot % 2), stats, 0.0), axis=1, keepdims=True
                )
            )
        levels = jnp.concatenate(levels, axis=0)
        rows = pl.ds(target * 96, 96)
        local = lmax[rows, :]
        top = jnp.maximum(levels, local)
        pre_factor = jnp.exp2(levels - top)
        local_factor = jnp.exp2(local - top)
        inverse_sum = 1.0 / (pre_factor + local_factor)
        share[rows, :] = pre_factor * inverse_sum
        lpart[rows, :] = lpart[rows, :] * (local_factor * inverse_sum)

    def combine(target):
        parts = []
        row = iota((24, 128), 0)
        for j in range(4):
            slot = index_at(2, target * 4 + j, 127)
            both = orecv[slot // 16, (slot // 2) % 8].astype(jnp.float32)
            parts.append(jnp.where(row * 0 + slot % 2 == 0, both[:24], both[24:]))
        rows = pl.ds(pl.multiple_of(target * 96, 96), 96)
        mixed = jnp.concatenate(parts, axis=0) * share[rows, :] + lpart[rows, :]
        stage[target] = mixed.astype(jnp.bfloat16)

    wait_for(srecv.at[seven, seven], s_recv_sem)
    wait_for(srecv.at[7], far_s_recv_sem)
    for target in range(8):
        settle(target)
    for index in range(3):
        wait_for(orecv.at[pl.ds(*return_groups[index]), seven], o_recv_sem.at[index])
    wait_for(orecv.at[7], far_o_recv_sem)
    pl.semaphore_wait(above_here.at[2], 1)
    for batch in ((4, 3), (5, 2), (6, 1), (7, 0)):
        for i in batch:
            combine((head + i) % 8)
        for i in batch:
            if i:
                head_copy(i).start()
    own = pltpu.make_async_copy(stage.at[head], out_ref.at[head], own_sem)
    own.start()

    for which in range(2):
        wait_for((kvk, kvv)[which].at[pl.ds(0, 6)], ring_send.at[which])
    for copy in query_sends:
        copy.wait_send()
    for index in range(3):
        wait_for(osend.at[pl.ds(*return_groups[index]), seven], o_send_sem.at[index])
    wait_for(ssend.at[seven, seven], s_send_sem)
    for way in range(2):
        far_query(way).wait_send()
    wait_for(osend.at[7], far_o_send_sem)
    wait_for(ssend.at[7], far_s_send_sem)
    wait_for(stage.at[seven], y_send_sem)
    own.wait()
    wait_for(out_ref.at[seven], y_recv_sem)


def shards(
    queries,
    prefix_keys,
    prefix_values,
    suffix_keys,
    suffix_values,
    new_keys,
    new_values,
    suffix_lengths,
    prefix_of_row,
    owner_of_prefix,
):
    bf16 = jnp.bfloat16
    by_step = jnp.transpose(queries, (0, 2, 1, 3))
    anywhere = pl.BlockSpec(memory_space=pltpu.HBM)
    dma = pltpu.SemaphoreType.DMA
    gathered = pl.pallas_call(
        kernel,
        out_shape=pltpu.VMEM((8, 96, 128), bf16),
        in_specs=[anywhere] * 11,
        out_specs=pl.BlockSpec(memory_space=pltpu.VMEM),
        scratch_shapes=[
            pltpu.VMEM((1, 32), jnp.int32),
            pltpu.VMEM((1, 64), jnp.int32),
            pltpu.SMEM((1, 32), jnp.int32),
            pltpu.VMEM((24, 128), jnp.int32),
            pltpu.SMEM((24, 128), jnp.int32),
            pltpu.VMEM((8, 33, 3, 8, 128), bf16),
            pltpu.VMEM((768, 128), bf16),
            pltpu.VMEM((8, 512, 128), bf16),
            pltpu.VMEM((8, 512, 128), bf16),
            pltpu.VMEM((3072, 128), bf16),
            pltpu.VMEM((3072, 128), bf16),
            pltpu.VMEM((96, 128), bf16),
            pltpu.VMEM((96, 128), bf16),
            pltpu.VMEM((8, 12, 48, 128), bf16),
            pltpu.VMEM((8, 8, 48, 128), bf16),
            pltpu.VMEM((8, 8, 48, 128), bf16),
            pltpu.VMEM((8, 8, 1, 128), jnp.float32),
            pltpu.VMEM((8, 8, 1, 128), jnp.float32),
            pltpu.VMEM((768, 96), jnp.float32),
            pltpu.VMEM((768, 96), bf16),
            pltpu.VMEM((768, 128), jnp.float32),
            pltpu.VMEM((768, 1), jnp.float32),
            pltpu.VMEM((768, 1), jnp.float32),
            pltpu.VMEM((768, 1), jnp.float32),
            pltpu.VMEM((8, 576, 512), bf16),
            pltpu.VMEM((8, 576, 128), jnp.float32),
            pltpu.VMEM((8, 96, 128), bf16),
            dma((11,)),
            dma((2,)),
            dma((2, 4, 2)),
            dma((13,)),
            dma((13,)),
            dma,
            dma((4,)),
            dma((4,)),
            dma,
            dma,
            dma,
            dma,
            dma,
            pltpu.SemaphoreType.REGULAR((3,)),
            pltpu.SemaphoreType.REGULAR((2,)),
            pltpu.SemaphoreType.REGULAR,
            dma((2,)),
            dma((2,)),
            dma,
            dma,
            dma,
            dma,
        ],
        compiler_params=pltpu.CompilerParams(
            collective_id=0, has_side_effects=True, vmem_limit_bytes=60 * 1024 * 1024
        ),
        cost_estimate=pl.CostEstimate(
            flops=1_200_000_000, bytes_accessed=3_000_000, transcendentals=1_800_000
        ),
        name="shared_prefix",
    )(
        prefix_of_row.reshape(1, 32),
        owner_of_prefix.reshape(1, 64),
        suffix_lengths.reshape(1, 32),
        by_step,
        by_step.reshape(768, 128),
        prefix_keys.reshape(512, 128),
        prefix_values.reshape(512, 128),
        suffix_keys.reshape(3072, 128),
        suffix_values.reshape(3072, 128),
        jnp.transpose(new_keys, (1, 2, 0, 3)).reshape(96, 128),
        jnp.transpose(new_values, (1, 2, 0, 3)).reshape(96, 128),
    )
    ordered = jnp.transpose(gathered.reshape(8, 4, 3, 8, 128), (1, 0, 3, 2, 4))
    return ordered.reshape(4, 64, 3, 128)


def solution(mesh):
    in_specs = (
        P("pre", "head", None, None),
        P("pre", None, "head", None),
        P("pre", None, "head", None),
        P("pre", None, "head", None),
        P("pre", None, "head", None),
        P("pre", None, "head", None),
        P("pre", None, "head", None),
        P("pre"),
        P("pre"),
        P(),
    )
    out_specs = P(("pre", "head"), None, None, None)
    return jax.shard_map(shards, mesh=mesh, in_specs=in_specs, out_specs=out_specs, check_vma=False)
```

```python
import math

import jax
import jax.numpy as jnp
from jax import lax
from jax.experimental import pallas as pl
from jax.experimental.pallas import tpu as pltpu
from jax.sharding import PartitionSpec as P

MESH = pl.DeviceIdType.MESH
masked_score = -1e30
offsets = (0, 1, 7, 2, 6, 3, 5, 4)
return_groups = ((0, 3), (3, 2), (5, 2))


def dot_t(a, b):
    return lax.dot_general(a, b, (((1,), (1,)), ((), ())), preferred_element_type=jnp.float32)


def kernel(
    prefix_hbm,
    owner_hbm,
    len_hbm,
    q4_hbm,
    q2_hbm,
    pk_hbm,
    pv_hbm,
    sk_hbm,
    sv_hbm,
    nk_hbm,
    nv_hbm,
    out_ref,
    prefix_here,
    owner_here,
    len_ref,
    index_rows,
    index_ref,
    qall,
    q2,
    kvk,
    kvv,
    sk,
    sv,
    nk,
    nv,
    qpack,
    osend,
    orecv,
    ssend,
    srecv,
    snew,
    pnew,
    lpart,
    lmax,
    share,
    lsum,
    weights,
    inverse,
    stage,
    load_sem,
    ring_send,
    ring_recv,
    q_send_sem,
    q_recv_sem,
    index_sem,
    o_send_sem,
    o_recv_sem,
    s_send_sem,
    s_recv_sem,
    y_send_sem,
    y_recv_sem,
    own_sem,
    above_here,
    below_here,
    far_q_send_sem,
    far_q_recv_sem,
    far_o_send_sem,
    far_o_recv_sem,
    far_s_send_sem,
    far_s_recv_sem,
):
    pre = lax.axis_index("pre")
    head = lax.axis_index("head")
    z = pre // 8
    me = pre % 8
    plane = z * 8
    right = ((z + 1) % 8) * 8 + me
    left = ((z + 7) % 8) * 8 + me
    column, core = me // 2, me % 2
    ahead = ((column + 1) % 4) * 2 + core
    behind = ((column + 3) % 4) * 2 + core
    opposite = ((column + 2) % 4) * 2 + core
    sibling = column * 2 + 1 - core
    to_log2 = 128 ** (-0.5) * math.log2(math.e)

    barrier = pltpu.get_barrier_semaphore()

    def greet(pre_index, head_index):
        pl.semaphore_signal(
            barrier, inc=1, device_id=(pre_index, head_index), device_id_type=MESH
        )

    above, below = (head + 1) % 8, (head + 7) % 8
    for peer in (right, left, plane + ahead, plane + behind, plane + sibling):
        greet(peer, head)
    greet(pre, above)
    greet(pre, below)

    loads = [
        pltpu.make_async_copy(a, b, load_sem.at[i])
        for i, (a, b) in enumerate(
            (
                (prefix_hbm, prefix_here),
                (owner_hbm, owner_here),
                (len_hbm, len_ref),
                (q4_hbm, qall.at[me, pl.ds(1, 32)]),
                (q2_hbm, q2),
                (nk_hbm, nk),
                (nv_hbm, nv),
                (sk_hbm, sk),
                (sv_hbm, sv),
                (pk_hbm, kvk.at[0]),
                (pv_hbm, kvv.at[0]),
            )
        )
    ]
    for i in (0, 1, 3):
        loads[i].start()

    def ring(way, hop, which):
        held, own = ((kvk, pk_hbm), (kvv, pv_hbm))[which]
        if way == 0:
            source, target, device = (9 - hop) % 8, 8 - hop, right
        else:
            source, target, device = hop - 1, hop, left
        return pltpu.make_async_remote_copy(
            src_ref=own if hop == 1 else held.at[source],
            dst_ref=held.at[target],
            send_sem=ring_send.at[which],
            recv_sem=ring_recv.at[way, hop - 1, which],
            device_id=(device, head),
            device_id_type=MESH,
        )

    def plane_copy(source, target, blocks, send_sem, recv_sem, i):
        peer = (me + i) % 8
        return pltpu.make_async_remote_copy(
            src_ref=source.at[blocks, peer],
            dst_ref=target.at[blocks, me],
            send_sem=send_sem,
            recv_sem=recv_sem,
            device_id=(plane + peer, head),
            device_id_type=MESH,
        )

    def wait_for(block, sem):
        pltpu.make_async_copy(block, block, sem).wait()

    def query_copy(i, source, rows, peer):
        block = qall.at[source, rows]
        return pltpu.make_async_remote_copy(
            src_ref=block,
            dst_ref=block,
            send_sem=q_send_sem.at[i],
            recv_sem=q_recv_sem.at[i],
            device_id=(plane + peer, head),
            device_id_type=MESH,
        )

    every, first_half, second_half = pl.ds(0, 33), pl.ds(0, 17), pl.ds(17, 16)

    seven = pl.ds(0, 7)

    def part_copy(index, i):
        blocks = pl.ds(*return_groups[index])
        return plane_copy(osend, orecv, blocks, o_send_sem.at[index], o_recv_sem.at[index], i)

    def stat_copy(i):
        return plane_copy(ssend, srecv, seven, s_send_sem, s_recv_sem, i)

    def far_query(way):
        return pltpu.make_async_remote_copy(
            src_ref=qpack.at[7, pl.ds(4 * way, 4)],
            dst_ref=qpack.at[5 + way, pl.ds(8, 4)],
            send_sem=far_q_send_sem.at[way],
            recv_sem=far_q_recv_sem.at[way],
            device_id=((right, left)[way], head),
            device_id_type=MESH,
        )

    def far_copy(source, target, send_sem, recv_sem, d):
        return pltpu.make_async_remote_copy(
            src_ref=source.at[7, d],
            dst_ref=target.at[7, me],
            send_sem=send_sem,
            recv_sem=recv_sem,
            device_id=((left if d < 4 else right) - me + d, head),
            device_id_type=MESH,
        )

    pl.semaphore_wait(barrier, 7)
    for way in range(2):
        ring(way, 1, 0).start()
    for i in (4, 5, 2, 7, 8, 6, 9, 10):
        loads[i].start()

    def token(from_above, step):
        tokens, peer = (above_here, below) if from_above else (below_here, above)
        pl.semaphore_signal(
            tokens.at[step], inc=1, device_id=(pre, peer), device_id_type=MESH
        )

    token(True, 0)
    token(False, 0)

    query_sends = [
        query_copy(0, me, first_half, ahead),
        query_copy(1, me, first_half, behind),
        query_copy(2, me, second_half, ahead),
        query_copy(3, me, second_half, behind),
        query_copy(4, me, every, sibling),
        query_copy(5, behind, first_half, ahead),
        query_copy(6, ahead, second_half, behind),
        query_copy(7, behind, first_half, sibling),
        query_copy(8, ahead, first_half, sibling),
        query_copy(9, behind, second_half, sibling),
        query_copy(10, ahead, second_half, sibling),
        query_copy(11, opposite, first_half, sibling),
        query_copy(12, opposite, second_half, sibling),
    ]

    def hand_on(arrived, onward):
        query_sends[arrived].wait_recv()
        for i in onward:
            query_sends[i].start()

    loads[0].wait()
    qall[me, 0] = jnp.full((3, 8, 128), -1.0, jnp.bfloat16)
    qall[me, 0, 0, :, 0:32] = jnp.broadcast_to(prefix_here[...], (8, 32)).astype(jnp.bfloat16)
    loads[3].wait()
    for copy in query_sends[:5]:
        copy.start()

    loads[1].wait()

    def small_dot(a, b):
        return jnp.dot(
            a.astype(jnp.bfloat16), b.astype(jnp.bfloat16), preferred_element_type=jnp.float32
        )

    def iota(shape, dim):
        return lax.broadcasted_iota(jnp.int32, shape, dim)

    def ones_where(condition):
        return jnp.where(condition, 1.0, 0.0)

    def owner_at(k):
        offset = jnp.zeros_like(k)
        for place, value in enumerate(offsets):
            offset = jnp.where(k == place, value, offset)
        return ((z + offset) & 7) * 8

    def named_by(d):
        names = qall[d, 0, 0].astype(jnp.float32)[0:1]
        return ones_where(names == iota((64, 128), 0).astype(jnp.float32))

    before = ones_where(iota((128, 128), 0) < iota((128, 128), 1))
    place = iota((64, 64), 0)
    owners = owner_here[...]
    held = ones_where(owners == owner_at(place >> 3) + (place & 7))
    mine = small_dot(held, named_by(me))
    earlier = small_dot(mine, before)
    slots = small_dot(2 * iota((8, 64), 1).astype(jnp.float32), mine) + small_dot(
        jnp.ones((8, 64), jnp.float32), mine * earlier
    )
    index_rows[16:24, :] = slots.astype(jnp.int32)

    for way in range(2):
        ring(way, 1, 1).start()

    loads[4].wait()
    loads[5].wait()
    snew[...] = dot_t(q2[...], nk[...])
    loads[2].wait()
    loads[7].wait()
    loads[8].wait()

    def pair(i):
        rows = pl.ds(i * 48, 48)
        keys = pl.ds(i * 192, 192)
        scores = dot_t(q2[rows, :], sk[keys, :])
        row = lax.broadcasted_iota(jnp.int32, (48, 192), 0)
        lane = lax.broadcasted_iota(jnp.int32, (48, 192), 1)
        low = jnp.where(row < 24, 0, 96)
        high = jnp.where(row < 24, len_ref[0, 2 * i], 96 + len_ref[0, 2 * i + 1])
        scores = jnp.where((lane >= low) & (lane < high), scores, masked_score)
        row = lax.broadcasted_iota(jnp.int32, (48, 96), 0)
        lane = lax.broadcasted_iota(jnp.int32, (48, 96), 1)
        second = row >= 24
        place = lane - jnp.where(second, 2 * i + 1, 2 * i)
        within = jnp.where(second, row - 24, row)
        fresh_ok = (
            (place == 0)
            | ((place == 32) & (within >= 8))
            | ((place == 64) & (within >= 16))
        )
        fresh = jnp.where(fresh_ok, snew[rows, :], masked_score)
        top = jnp.maximum(
            jnp.max(scores, axis=1, keepdims=True), jnp.max(fresh, axis=1, keepdims=True)
        )
        scores = jnp.exp2((scores - top) * to_log2)
        fresh = jnp.exp2((fresh - top) * to_log2)
        lmax[rows, :] = top * to_log2
        lsum[rows, :] = jnp.sum(scores, axis=1, keepdims=True) + jnp.sum(
            fresh, axis=1, keepdims=True
        )
        pnew[rows, :] = fresh.astype(jnp.bfloat16)
        lpart[rows, :] = jnp.dot(
            scores.astype(jnp.bfloat16), sv[keys, :], preferred_element_type=jnp.float32
        )

    def pairs(first):
        for j in range(4):
            pair(first + j)

    def pass_on(hop, which):
        for way in (1, 0):
            ring(way, hop, which).wait_recv()
            if hop < 3:
                ring(way, hop + 1, which).start()

    pairs(0)
    pass_on(1, 0)
    pairs(4)
    hand_on(0, (5, 7))
    hand_on(1, (8,))
    pairs(8)
    hand_on(2, (9,))
    hand_on(3, (6, 10))
    pass_on(1, 1)
    pairs(12)
    loads[6].wait()
    part = lpart[...] + jnp.dot(pnew[...], nv[...], preferred_element_type=jnp.float32)
    lpart[...] = part / lsum[...]
    lmax[...] = lmax[...] + jnp.log2(lsum[...])

    def index_at(table, place, last):
        return jnp.minimum(jnp.maximum(index_ref[table * 8, place], 0), last)

    def pack(k):
        for d in range(8):
            rows = [qall[d, 1 + index_at(rank, d * 8 + k, 31)] for rank in range(2)]
            both = [row.astype(jnp.float32).reshape(24, 128) for row in rows]
            qpack[k, d] = jnp.concatenate(both, axis=0).astype(jnp.bfloat16)

    def sources(k):
        return 12 if k in (5, 6) else 8

    def weigh(k):
        pack(k)
        count = sources(k)
        scores = dot_t(qpack[k, 0:count].reshape(count * 48, 128), kvk[offsets[k]])
        top = jnp.max(scores, axis=1, keepdims=True)
        scores = jnp.exp2((scores - top) * to_log2)
        weights[k, 0 : count * 48] = scores.astype(jnp.bfloat16)
        total = jnp.dot(
            weights[k, 0 : count * 48],
            jnp.ones((512, 128), jnp.bfloat16),
            preferred_element_type=jnp.float32,
        )
        inverse[k, 0 : count * 48] = 1.0 / total
        level = top * to_log2 + jnp.log2(total)
        row = iota((48, 128), 0)
        lane = iota((48, 128), 1)
        for d in range(count):
            block, place = (k, d) if d < 8 else (7, d - 8 + 4 * (k - 5))
            ssend[block, place] = jnp.sum(
                jnp.where(row == lane, level[d * 48 : d * 48 + 48], 0.0), axis=0, keepdims=True
            )
        srecv[k, me] = ssend[k, me]

    def blend(k):
        count = sources(k)
        part = jnp.dot(
            weights[k, 0 : count * 48], kvv[offsets[k]], preferred_element_type=jnp.float32
        )
        part = (part * inverse[k, 0 : count * 48]).astype(jnp.bfloat16).reshape(count, 48, 128)
        osend[k] = part[0:8]
        if count > 8:
            osend[7, 4 * (k - 5) : 4 * (k - 5) + 4] = part[8:12]
        orecv[k, me] = osend[k, me]

    def send_back(index):
        for i in range(1, 8):
            part_copy(index, i).start()

    hand_on(5, (11,))
    hand_on(6, (12,))
    pass_on(2, 0)
    for i in (4, 7, 8, 11):
        query_sends[i].wait_recv()
    here = ones_where(owners == owner_at(iota((8, 64), 0)) + me)
    match = jnp.concatenate(
        [small_dot(here, named_by(d)) for d in range(8)], axis=0
    )
    earlier = small_dot(match, before)
    numbers = iota((8, 128), 1).astype(jnp.bfloat16)
    for rank in range(2):
        chosen = jnp.where(earlier == rank, match, 0.0).astype(jnp.bfloat16)
        index_rows[rank * 8 : rank * 8 + 8, 0:64] = dot_t(numbers, chosen).astype(jnp.int32)
    index_copy = pltpu.make_async_copy(index_rows, index_ref, index_sem)
    index_copy.start()
    for i in (9, 10, 12):
        query_sends[i].wait_recv()
    index_copy.wait()
    loads[9].wait()
    loads[10].wait()
    pack(7)
    for way in range(2):
        far_query(way).start()
    weigh(0)
    blend(0)
    pass_on(2, 1)
    weigh(1)
    blend(1)
    weigh(2)
    blend(2)
    send_back(0)
    pass_on(3, 0)
    pl.semaphore_wait(above_here.at[0], 1)
    token(True, 1)
    pl.semaphore_wait(below_here.at[0], 1)
    token(False, 1)
    weigh(3)
    weigh(4)
    blend(3)
    blend(4)
    send_back(1)
    for way in range(2):
        far_query(way).wait_recv()
    weigh(5)
    weigh(6)
    for d in range(8):
        far_copy(ssend, srecv, far_s_send_sem, far_s_recv_sem, d).start()
    for i in range(1, 8):
        stat_copy(i).start()
    pl.semaphore_wait(above_here.at[1], 1)
    token(True, 2)
    pl.semaphore_wait(below_here.at[1], 1)
    for k in (5, 6):
        ring(6 - k, 3, 1).wait_recv()
        blend(k)
        for d in range(4 * (k - 5), 4 * (k - 5) + 4):
            far_copy(osend, orecv, far_o_send_sem, far_o_recv_sem, d).start()
    send_back(2)

    def head_copy(i):
        peer = (head + i) % 8
        return pltpu.make_async_remote_copy(
            src_ref=stage.at[peer],
            dst_ref=out_ref.at[head],
            send_sem=y_send_sem,
            recv_sem=y_recv_sem,
            device_id=(pre, peer),
            device_id_type=MESH,
        )

    def settle(target):
        levels = []
        row = iota((24, 128), 0)
        lane = iota((24, 128), 1)
        for j in range(4):
            slot = index_at(2, target * 4 + j, 127)
            stats = srecv[slot // 16, (slot // 2) % 8]
            levels.append(
                jnp.sum(
                    jnp.where(lane == row + 24 * (slot % 2), stats, 0.0), axis=1, keepdims=True
                )
            )
        levels = jnp.concatenate(levels, axis=0)
        rows = pl.ds(target * 96, 96)
        local = lmax[rows, :]
        top = jnp.maximum(levels, local)
        pre_factor = jnp.exp2(levels - top)
        local_factor = jnp.exp2(local - top)
        inverse_sum = 1.0 / (pre_factor + local_factor)
        share[rows, :] = pre_factor * inverse_sum
        lpart[rows, :] = lpart[rows, :] * (local_factor * inverse_sum)

    def combine(target):
        parts = []
        row = iota((24, 128), 0)
        for j in range(4):
            slot = index_at(2, target * 4 + j, 127)
            both = orecv[slot // 16, (slot // 2) % 8].astype(jnp.float32)
            parts.append(jnp.where(row * 0 + slot % 2 == 0, both[:24], both[24:]))
        rows = pl.ds(pl.multiple_of(target * 96, 96), 96)
        mixed = jnp.concatenate(parts, axis=0) * share[rows, :] + lpart[rows, :]
        stage[target] = mixed.astype(jnp.bfloat16)

    wait_for(srecv.at[seven, seven], s_recv_sem)
    wait_for(srecv.at[7], far_s_recv_sem)
    for target in range(8):
        settle(target)
    for index in range(3):
        wait_for(orecv.at[pl.ds(*return_groups[index]), seven], o_recv_sem.at[index])
    wait_for(orecv.at[7], far_o_recv_sem)
    pl.semaphore_wait(above_here.at[2], 1)
    for batch in ((4, 3), (5, 2), (6, 1), (7, 0)):
        for i in batch:
            combine((head + i) % 8)
        for i in batch:
            if i:
                head_copy(i).start()
    own = pltpu.make_async_copy(stage.at[head], out_ref.at[head], own_sem)
    own.start()

    for which in range(2):
        wait_for((kvk, kvv)[which].at[pl.ds(0, 6)], ring_send.at[which])
    for copy in query_sends:
        copy.wait_send()
    for index in range(3):
        wait_for(osend.at[pl.ds(*return_groups[index]), seven], o_send_sem.at[index])
    wait_for(ssend.at[seven, seven], s_send_sem)
    for way in range(2):
        far_query(way).wait_send()
    wait_for(osend.at[7], far_o_send_sem)
    wait_for(ssend.at[7], far_s_send_sem)
    wait_for(stage.at[seven], y_send_sem)
    own.wait()
    wait_for(out_ref.at[seven], y_recv_sem)


def shards(
    queries,
    prefix_keys,
    prefix_values,
    suffix_keys,
    suffix_values,
    new_keys,
    new_values,
    suffix_lengths,
    prefix_of_row,
    owner_of_prefix,
):
    bf16 = jnp.bfloat16
    by_step = jnp.transpose(queries, (0, 2, 1, 3))
    anywhere = pl.BlockSpec(memory_space=pltpu.HBM)
    dma = pltpu.SemaphoreType.DMA
    gathered = pl.pallas_call(
        kernel,
        out_shape=pltpu.VMEM((8, 96, 128), bf16),
        in_specs=[anywhere] * 11,
        out_specs=pl.BlockSpec(memory_space=pltpu.VMEM),
        scratch_shapes=[
            pltpu.VMEM((1, 32), jnp.int32),
            pltpu.VMEM((1, 64), jnp.int32),
            pltpu.SMEM((1, 32), jnp.int32),
            pltpu.VMEM((24, 128), jnp.int32),
            pltpu.SMEM((24, 128), jnp.int32),
            pltpu.VMEM((8, 33, 3, 8, 128), bf16),
            pltpu.VMEM((768, 128), bf16),
            pltpu.VMEM((8, 512, 128), bf16),
            pltpu.VMEM((8, 512, 128), bf16),
            pltpu.VMEM((3072, 128), bf16),
            pltpu.VMEM((3072, 128), bf16),
            pltpu.VMEM((96, 128), bf16),
            pltpu.VMEM((96, 128), bf16),
            pltpu.VMEM((8, 12, 48, 128), bf16),
            pltpu.VMEM((8, 8, 48, 128), bf16),
            pltpu.VMEM((8, 8, 48, 128), bf16),
            pltpu.VMEM((8, 8, 1, 128), jnp.float32),
            pltpu.VMEM((8, 8, 1, 128), jnp.float32),
            pltpu.VMEM((768, 96), jnp.float32),
            pltpu.VMEM((768, 96), bf16),
            pltpu.VMEM((768, 128), jnp.float32),
            pltpu.VMEM((768, 1), jnp.float32),
            pltpu.VMEM((768, 1), jnp.float32),
            pltpu.VMEM((768, 1), jnp.float32),
            pltpu.VMEM((8, 576, 512), bf16),
            pltpu.VMEM((8, 576, 128), jnp.float32),
            pltpu.VMEM((8, 96, 128), bf16),
            dma((11,)),
            dma((2,)),
            dma((2, 4, 2)),
            dma((13,)),
            dma((13,)),
            dma,
            dma((4,)),
            dma((4,)),
            dma,
            dma,
            dma,
            dma,
            dma,
            pltpu.SemaphoreType.REGULAR((3,)),
            pltpu.SemaphoreType.REGULAR((2,)),
            dma((2,)),
            dma((2,)),
            dma,
            dma,
            dma,
            dma,
        ],
        compiler_params=pltpu.CompilerParams(
            collective_id=0, has_side_effects=True, vmem_limit_bytes=60 * 1024 * 1024
        ),
        cost_estimate=pl.CostEstimate(
            flops=1_200_000_000, bytes_accessed=3_000_000, transcendentals=1_800_000
        ),
        name="shared_prefix",
    )(
        prefix_of_row.reshape(1, 32),
        owner_of_prefix.reshape(1, 64),
        suffix_lengths.reshape(1, 32),
        by_step,
        by_step.reshape(768, 128),
        prefix_keys.reshape(512, 128),
        prefix_values.reshape(512, 128),
        suffix_keys.reshape(3072, 128),
        suffix_values.reshape(3072, 128),
        jnp.transpose(new_keys, (1, 2, 0, 3)).reshape(96, 128),
        jnp.transpose(new_values, (1, 2, 0, 3)).reshape(96, 128),
    )
    ordered = jnp.transpose(gathered.reshape(8, 4, 3, 8, 128), (1, 0, 3, 2, 4))
    return ordered.reshape(4, 64, 3, 128)


def solution(mesh):
    in_specs = (
        P("pre", "head", None, None),
        P("pre", None, "head", None),
        P("pre", None, "head", None),
        P("pre", None, "head", None),
        P("pre", None, "head", None),
        P("pre", None, "head", None),
        P("pre", None, "head", None),
        P("pre"),
        P("pre"),
        P(),
    )
    out_specs = P(("pre", "head"), None, None, None)
    return jax.shard_map(shards, mesh=mesh, in_specs=in_specs, out_specs=out_specs, check_vma=False)
```
